128 devices in a mesh: kv: 8 (over y, core), seq: 16 (over x, z).
Axes of the slice: x: 4, y: 4, z: 4, core: 2. Of those that a mesh axis runs over, the one named last changes fastest.
Arguments:
- inputs: bfloat16 [4096, 2048], P('seq'), may hold values from -6 to 6
- cotangent: bfloat16 [4096, 2048], P('seq'), may hold values from -6 to 6
- segment_ids: int32 [4096], replicated, may hold values from 0 to 3, as said below
- attn_gain: bfloat16 [2048], P('seq'), may hold values from 0.5 to 1.5
- query_weight: bfloat16 [2048, 2048], P('seq', 'kv'), may hold values from -0.125 to 0.125
- gate_weight: bfloat16 [2048, 2048], P('seq', 'kv'), may hold values from -0.125 to 0.125
- key_weight: bfloat16 [2048, 1024], P('seq', 'kv'), may hold values from -0.125 to 0.125
- value_weight: bfloat16 [2048, 1024], P('seq', 'kv'), may hold values from -0.125 to 0.125
- output_weight: bfloat16 [2048, 2048], P('kv', 'seq'), may hold values from -0.75 to 0.75
- mlp_gain: bfloat16 [2048], P('seq'), may hold values from 0.5 to 1.5
- mlp_gate: bfloat16 [2048, 6144], P('seq', 'kv'), may hold values from -0.125 to 0.125
- mlp_up: bfloat16 [2048, 6144], P('seq', 'kv'), may hold values from -0.125 to 0.125
- mlp_down: bfloat16 [6144, 2048], P('kv', 'seq'), may hold values from -0.078125 to 0.078125
Outputs:
- block_out: bfloat16 [4096, 2048], P('seq')
- input_grad: float32 [4096, 2048], P('seq')
- attn_gain_grad: float32 [2048], P('seq')
- query_grad: float32 [2048, 2048], P('seq', 'kv')
- gate_grad: float32 [2048, 2048], P('seq', 'kv')
- key_grad: float32 [2048, 1024], P('seq', 'kv')
- value_grad: float32 [2048, 1024], P('seq', 'kv')
- output_grad: float32 [2048, 2048], P('kv', 'seq')
- mlp_gain_grad: float32 [2048], P('seq')
- mlp_gate_grad: float32 [2048, 6144], P('seq', 'kv')
- mlp_up_grad: float32 [2048, 6144], P('seq', 'kv')
- mlp_down_grad: float32 [6144, 2048], P('kv', 'seq')
The draws below stay inside these ranges and needn't reach their ends.
Inputs may be any that keep to these rules, and one draw needn't show every extreme that they name: `segment_ids`: ids never fall. The packed row holds documents 0, 1 and 2: document 0 ends within the first 256 tokens, document 1 ends within the last 128 tokens, and then document 2 is followed by padding, id 3, of 1 to 64 tokens at the row's end. Every id occurs.
All inputs are finite; a program needn't handle non-finite values.
Results may differ from the reference program's by a relative error of at most 0.024.
Values may be sent and summed in bfloat16 or wider, within the bound.
A program may use at most 128 MiB of HBM per device.

```python
import jax
import jax.numpy as jnp
from jax import lax

D = 2048
HEADS = 16
KV_HEADS = 8
HEAD_DIM = 128
FF = 6144
TOK_DEV = 256
ROW_LEN = 4096
TOKENS = 4096


def draw_segment_ids(key, part):
    key = jax.random.fold_in(key, 7)
    streams = jax.random.split(key, 3)
    first_end = jax.random.randint(streams[0], (), 1, TOK_DEV // 2)
    second_end = jax.random.randint(streams[1], (), TOKENS - TOK_DEV // 2, TOKENS - TOK_DEV // 4 - 1)
    padding = jax.random.randint(streams[2], (), 1, TOK_DEV // 4 + 1)
    places = lax.iota(jnp.int32, TOKENS)
    ids = (places >= first_end).astype(jnp.int32) + (places >= second_end).astype(jnp.int32)
    ids = jnp.where(places >= TOKENS - padding, 3, ids)
    return ids.astype(jnp.int32)


def levels(stream_key, shape, cuts, least, largest):
    loudness, own = 1.0, jax.random.fold_in(stream_key, 6)
    for dim, blocks in cuts:
        steps = jnp.exp(jax.random.uniform(jax.random.fold_in(own, dim), (blocks,), jnp.float32, least / len(cuts), largest / len(cuts)))
        loudness = loudness * jnp.repeat(steps, shape[dim] // blocks).reshape([-1 if axis == dim else 1 for axis in range(len(shape))])
    return loudness


def bell_draw(own_key, extent, scale, reach, cuts=(), kind=jnp.bfloat16):
    drawn = jax.random.normal(own_key, extent, jnp.float32) * scale
    if len(cuts) > 0:
        drawn = levels(own_key, extent, cuts, -0.22, 0.18) * drawn
    return jnp.clip(drawn, min=-reach, max=reach).astype(kind)


def setup_inputs(seed: int = 0) -> dict:
    streams_of = jax.random.split(jax.random.key(seed), 14)
    return {
        "inputs": bell_draw(streams_of[0], (TOKENS, D), 1.0, 6.0, ((0, 16),)),
        "cotangent": bell_draw(streams_of[1], (TOKENS, D), 1.0, 6.0, ((0, 16),)),
        "segment_ids": draw_segment_ids(jax.random.fold_in(streams_of[13], 71), 0),
        "attn_gain": jnp.clip(1.0 + 0.1 * jax.random.normal(streams_of[3], (D,), jnp.float32), 0.5, 1.5).astype(jnp.bfloat16),
        "query_weight": bell_draw(streams_of[4], (D, HEADS * HEAD_DIM), D ** -0.5, 0.125, ((0, 16), (1, 8))),
        "gate_weight": bell_draw(streams_of[5], (D, HEADS * HEAD_DIM), D ** -0.5, 0.125, ((0, 16), (1, 8))),
        "key_weight": bell_draw(streams_of[6], (D, KV_HEADS * HEAD_DIM), D ** -0.5, 0.125, ((0, 16), (1, 8))),
        "value_weight": bell_draw(streams_of[7], (D, KV_HEADS * HEAD_DIM), D ** -0.5, 0.125, ((0, 16), (1, 8))),
        "output_weight": bell_draw(streams_of[8], (HEADS * HEAD_DIM, D), 64 ** -0.5, 0.75, ((0, 8), (1, 16))),
        "mlp_gain": jnp.clip(1.0 + 0.1 * jax.random.normal(streams_of[9], (D,), jnp.float32), 0.5, 1.5).astype(jnp.bfloat16),
        "mlp_gate": bell_draw(streams_of[10], (D, FF), D ** -0.5, 0.125, ((0, 16), (1, 8))),
        "mlp_up": bell_draw(streams_of[11], (D, FF), D ** -0.5, 0.125, ((0, 16), (1, 8))),
        "mlp_down": bell_draw(streams_of[12], (FF, D), FF ** -0.5, 0.078125, ((0, 8), (1, 16))),
    }


epsilon = 1e-06
masked_value = -1e+30

@jax.custom_vjp
def low(v):
    return lax.optimization_barrier(v.astype(jnp.bfloat16)).astype(jnp.float32)

@jax.custom_vjp
def low_back(v):
    return v

def low_keep(v):
    return (low(v), None)

def low_pass(kept, grad):
    return (grad,)

def back_keep(v):
    return (v, None)

def back_low(kept, grad):
    return (low(grad),)
low.defvjp(low_keep, low_pass)
low_back.defvjp(back_keep, back_low)

def exact_dot(left, right):
    return jnp.dot(left, right, precision=lax.Precision.HIGHEST, preferred_element_type=jnp.float32)

def rms_norm(rows_in, gain):
    scale_rows = lax.rsqrt(lax.optimization_barrier(jnp.mean(rows_in * rows_in, axis=-1, keepdims=True)) + epsilon)
    return rows_in * scale_rows * gain

def row_attention(packed):
    queries, key_rows, value_rows, row_segments = packed
    row_tokens = queries.shape[0]
    query_span = min(512, row_tokens)
    keys_all = key_rows.reshape(row_tokens, KV_HEADS, HEAD_DIM)
    values_all = value_rows.reshape(row_tokens, KV_HEADS, HEAD_DIM)
    places = lax.iota(jnp.int32, row_tokens)

    def one_block(block_index):
        row_start = (block_index * query_span).astype(jnp.int32)
        query_part = lax.dynamic_slice_in_dim(queries, row_start, query_span, 0)
        query_part = query_part.reshape(query_span, KV_HEADS, HEADS // KV_HEADS, HEAD_DIM)
        query_segment = lax.dynamic_slice_in_dim(row_segments, row_start, query_span, 0)
        query_place = row_start + lax.iota(jnp.int32, query_span)
        products = low_back(jnp.einsum('qgrd,kgd->grqk', query_part, keys_all, precision=lax.Precision.HIGHEST))
        scores = products * HEAD_DIM ** (-0.5)
        allowed = (query_segment[:, None] == row_segments[None, :]) & (query_place[:, None] >= places[None, :])
        masked = jnp.where(allowed, scores, masked_value)
        log_total = jax.nn.logsumexp(masked, axis=-1, keepdims=True)
        probs = low(jnp.exp(masked - log_total))
        outcome = low_back(jnp.einsum('grqk,kgd->qgrd', probs, values_all, precision=lax.Precision.HIGHEST))
        return outcome.reshape(query_span, HEADS * HEAD_DIM)
    blocks = lax.map(jax.checkpoint(one_block), jnp.arange(row_tokens // query_span, dtype=jnp.int32))
    return blocks.reshape(row_tokens, HEADS * HEAD_DIM)

def attention(queries, key_rows, value_rows, segment_ids):
    total_rows = queries.shape[0]
    row_count = total_rows // ROW_LEN
    packed = (queries.reshape(row_count, ROW_LEN, HEADS * HEAD_DIM), key_rows.reshape(row_count, ROW_LEN, KV_HEADS * HEAD_DIM), value_rows.reshape(row_count, ROW_LEN, KV_HEADS * HEAD_DIM), segment_ids.reshape(row_count, ROW_LEN))
    rows_out = lax.map(row_attention, packed)
    return rows_out.reshape(total_rows, HEADS * HEAD_DIM)

def forward(x_float, gain_one, w_query, w_gate, w_key, w_value, w_out, gain_two, w_mlp_gate, w_mlp_up, w_down, segment_ids):
    x_norm = low(rms_norm(x_float, gain_one))
    queries = low_back(low(exact_dot(x_norm, w_query)))
    key_rows = low_back(low(exact_dot(x_norm, w_key)))
    value_rows = low_back(low(exact_dot(x_norm, w_value)))
    gate_pre = low_back(exact_dot(x_norm, w_gate))
    attended = attention(queries, key_rows, value_rows, segment_ids)
    gated = low(attended * jax.nn.sigmoid(gate_pre))
    mid_rows = x_float + low_back(exact_dot(gated, w_out))
    h_norm = low(rms_norm(mid_rows, gain_two))
    gate_mlp = low_back(exact_dot(h_norm, w_mlp_gate))
    up_mlp = low_back(exact_dot(h_norm, w_mlp_up))
    mixed = low(jax.nn.silu(gate_mlp) * up_mlp)
    return mid_rows + low_back(exact_dot(mixed, w_down))

def reference(inputs, cotangent, segment_ids, attn_gain, query_weight, gate_weight, key_weight, value_weight, output_weight, mlp_gain, mlp_gate, mlp_up, mlp_down):
    params = tuple((w.astype(jnp.float32) for w in (attn_gain, query_weight, gate_weight, key_weight, value_weight, output_weight, mlp_gain, mlp_gate, mlp_up, mlp_down)))
    x_float = inputs.astype(jnp.float32)

    def layer(x_in, gain_one, w_query, w_gate, w_key, w_value, w_out, gain_two, w_mlp_gate, w_mlp_up, w_down):
        return forward(x_in, gain_one, w_query, w_gate, w_key, w_value, w_out, gain_two, w_mlp_gate, w_mlp_up, w_down, segment_ids)
    result, pullback = jax.vjp(layer, x_float, *params)
    keep_rows = (segment_ids != jnp.max(segment_ids)).astype(jnp.float32)
    grads = pullback(cotangent.astype(jnp.float32) * keep_rows[:, None])
    return (result.astype(jnp.bfloat16), grads[0], grads[1], grads[2], grads[3], grads[4], grads[5], grads[6], grads[7], grads[8], grads[9], grads[10])
```

```python
import functools

import jax
import jax.numpy as jnp
from jax import lax
from jax.experimental import pallas as pl
from jax.experimental.pallas import tpu as pltpu
from jax.sharding import PartitionSpec as P

F32 = jnp.float32
BF16 = jnp.bfloat16
MESH = pl.DeviceIdType.MESH
EPS = 1e-06
HEAD = 128
SCALE = HEAD**-0.5
LOG2E = 1.4426950408889634
MASKED = -1e30
FLOOR = -1e29
ROWS = 32


def nn(left, right):
    return jnp.dot(left, right, preferred_element_type=F32)


def nt(left, right):
    return lax.dot_general(left, right, (((1,), (1,)), ((), ())), preferred_element_type=F32)


class Net:
    def __init__(self, send, recv):
        s, k = lax.axis_index("seq"), lax.axis_index("kv")
        self.s, self.k = s, k
        self.x, self.z, self.y, self.c = s // 4, s % 4, k // 2, k % 2
        self.send, self.recv, self.used = send, recv, 0

    def at(self, dx=0, dz=0, dy=0, dc=0):
        return {
            "kv": ((self.y + dy) % 4) * 2 + (self.c + dc) % 2,
            "seq": ((self.x + dx) % 4) * 4 + (self.z + dz) % 4,
        }

    def along(self, axis, d):
        return self.at(dx=d) if axis == 0 else self.at(dz=d)

    def copy(self, src, dst, to):
        i = self.used
        self.used += 1
        return pltpu.make_async_remote_copy(
            src_ref=src,
            dst_ref=dst,
            send_sem=self.send.at[i],
            recv_sem=self.recv.at[i],
            device_id=to,
            device_id_type=MESH,
        )

    def barrier(self):
        sem = pltpu.get_barrier_semaphore()
        near = [self.at(dx=d) for d in (1, 2, 3)] + [self.at(dz=d) for d in (1, 2, 3)]
        near += [self.at(dy=d) for d in (1, 2, 3)] + [self.at(dc=1)]
        for to in near:
            pl.semaphore_signal(sem, inc=1, device_id=to, device_id_type=MESH)
        pl.semaphore_wait(sem, len(near))


class Gather:
    def __init__(self, net, w, cuts):
        q, h, q2, r = cuts
        x, z = net.x, net.z
        place = (x, z)
        self.steps = [[], [], [], []]
        for o, (r0, r1, r2) in enumerate(((0, q, h), (h, q2, r))):
            full, one, two = pl.ds(r0, r2 - r0), pl.ds(r0, r1 - r0), pl.ds(r1, r2 - r1)
            me, other = place[o], place[1 - o]
            low, high = (me + 3) % 4, (me + 1) % 4
            up, down = net.along(o, 1), net.along(o, -1)

            def single(a, rows, o=o, other=other):
                return w.at[a, other, rows] if o == 0 else w.at[other, a, rows]

            def bundle(b, rows, o=o):
                return w.at[:, b, rows] if o == 0 else w.at[b, :, rows]

            def mk(ref, to):
                return net.copy(ref, ref, to)

            self.steps[0] += [mk(single(me, full), up), mk(single(me, full), down)]
            self.steps[1] += [mk(single(low, one), up), mk(single(high, two), down)]
            low, high = (other + 3) % 4, (other + 1) % 4
            up, down = net.along(1 - o, 1), net.along(1 - o, -1)
            self.steps[2] += [mk(bundle(other, full), up), mk(bundle(other, full), down)]
            self.steps[3] += [mk(bundle(low, one), up), mk(bundle(high, two), down)]

    def start(self):
        for d in self.steps[0]:
            d.start()

    def step(self, n):
        if n == 1 or n == 3:
            for a, b in zip(self.steps[n - 1], self.steps[n]):
                a.wait_recv()
                b.start()
        else:
            for o in (0, 1):
                for b in self.steps[1][2 * o : 2 * o + 2]:
                    b.wait_recv()
                for b in self.steps[2][2 * o : 2 * o + 2]:
                    b.start()

    def finish(self):
        for d in self.steps[3]:
            d.wait_recv()

    def drain(self):
        for step in self.steps:
            for d in step:
                d.wait_send()


class Scatter:
    def __init__(self, net, p, rows, bufs):
        self.net, self.p, self.bufs = net, p, bufs
        self.h, self.q = rows // 2, rows // 4
        self.sent = []
        self.d = [{}, {}]

    def rows(self, o, part):
        base = o * self.h
        if part == 1:
            return pl.ds(base, self.q)
        if part == 2:
            return pl.ds(base + self.q, self.q)
        return pl.ds(base, self.h)

    def place(self, o):
        return (self.net.x, self.net.z) if o == 0 else (self.net.z, self.net.x)

    def bundle(self, o, a, part):
        r = self.rows(o, part)
        return self.p.at[a, :, r] if o == 0 else self.p.at[:, a, r]

    def block(self, o, a, i, part):
        r = self.rows(o, part)
        return self.p.at[a, i, r] if o == 0 else self.p.at[i, a, r]

    def go(self, o, name, src, dst, axis, d):
        c = self.net.copy(src, dst, self.net.along(axis, d))
        c.start()
        self.d[o][name] = c
        self.sent.append(c)

    def start(self):
        r1, r2 = self.bufs[0], self.bufs[1]
        q = self.q
        for o in (0, 1):
            me, _ = self.place(o)
            self.go(o, "c1", self.bundle(o, (me + 2) % 4, 1), r1.at[o, 0], o, 1)
            self.go(o, "c2", self.bundle(o, (me + 2) % 4, 2), r1.at[o, 1], o, -1)
        for o in (0, 1):
            me, _ = self.place(o)
            self.go(o, "c3", self.bundle(o, (me + 1) % 4, 2), r2.at[o, 0, :, pl.ds(q, q)], o, 1)
            self.go(o, "c4", self.bundle(o, (me + 3) % 4, 1), r2.at[o, 1, :, pl.ds(0, q)], o, -1)

    def step2(self):
        r1, r2 = self.bufs[0], self.bufs[1]
        q = self.q
        for o in (0, 1):
            me, _ = self.place(o)
            for name, a, part, side, d in (("c1", (me + 1) % 4, 1, 0, 1), ("c2", (me + 3) % 4, 2, 1, -1)):
                self.d[o][name].wait_recv()

                def add(i, _, o=o, a=a, part=part, side=side):
                    b = self.block(o, a, i, part)
                    b[...] = (b[...].astype(F32) + r1[o, side, i].astype(F32)).astype(BF16)
                    return 0

                lax.fori_loop(0, 4, add, 0)
                self.go(o, "c5" if side == 0 else "c6", self.bundle(o, a, part), r2.at[o, side, :, pl.ds(side * q, q)], o, d)

    def step3(self):
        r2, r3, r4 = self.bufs[1], self.bufs[2], self.bufs[3]
        q = self.q
        for o in (0, 1):
            me, other = self.place(o)
            for name in ("c3", "c4", "c5", "c6"):
                self.d[o][name].wait_recv()

            def add(i, o=o, me=me):
                b = self.block(o, me, i, 0)
                total = b[...].astype(F32) + r2[o, 0, i].astype(F32) + r2[o, 1, i].astype(F32)
                b[...] = total.astype(BF16)

            def far(n, _, add=add, other=other):
                add((other + 2 + n) % 4)
                return 0

            add((other + 2) % 4)
            self.go(o, "d1", self.block(o, me, (other + 2) % 4, 1), r3.at[o, 0], 1 - o, 1)
            self.go(o, "d2", self.block(o, me, (other + 2) % 4, 2), r3.at[o, 1], 1 - o, -1)
            lax.fori_loop(1, 4, far, 0)
            self.go(o, "d3", self.block(o, me, (other + 1) % 4, 2), r4.at[o, 0, pl.ds(q, q)], 1 - o, 1)
            self.go(o, "d4", self.block(o, me, (other + 3) % 4, 1), r4.at[o, 1, pl.ds(0, q)], 1 - o, -1)

    def step4(self):
        r3, r4 = self.bufs[2], self.bufs[3]
        q = self.q
        for o in (0, 1):
            me, other = self.place(o)
            for name, a, part, side, d in (("d1", (other + 1) % 4, 1, 0, 1), ("d2", (other + 3) % 4, 2, 1, -1)):
                self.d[o][name].wait_recv()
                b = self.block(o, me, a, part)
                b[...] = (b[...].astype(F32) + r3[o, side].astype(F32)).astype(BF16)
                self.go(o, "d5" if side == 0 else "d6", b, r4.at[o, side, pl.ds(side * q, q)], 1 - o, d)

    def finish(self, store):
        r4 = self.bufs[3]
        for o in (0, 1):
            me, other = self.place(o)
            for name in ("d3", "d4", "d5", "d6"):
                self.d[o][name].wait_recv()
            total = self.block(o, me, other, 0)[...].astype(F32) + r4[o, 0].astype(F32) + r4[o, 1].astype(F32)
            store(self.rows(o, 0), total)

    def drain(self):
        for c in self.sent:
            c.wait_send()


def scatter_bufs(rows, cols):
    h, q = rows // 2, rows // 4
    return [
        pltpu.VMEM((2, 2, 4, q, cols), BF16),
        pltpu.VMEM((2, 2, 4, h, cols), BF16),
        pltpu.VMEM((2, 2, q, cols), BF16),
        pltpu.VMEM((2, 2, h, cols), BF16),
    ]


class ReduceY:
    def __init__(self, net, part, cr, yr):
        self.net, self.part, self.cr, self.yr = net, part, cr, yr

    def start(self):
        n = self.net
        self.core = n.copy(self.part.at[:, 1 - n.c], self.cr, n.at(dc=1))
        self.core.start()

    def step(self):
        n = self.net
        self.core.wait_recv()
        self.far = []
        for d in (2, 1, 3):
            to = (n.y + d) % 4
            own = self.part.at[to, n.c]
            own[...] = (own[...].astype(F32) + self.cr[to].astype(F32)).astype(BF16)
            c = n.copy(own, self.yr.at[d - 1], n.at(dy=d))
            c.start()
            self.far.append(c)

    def finish(self):
        n = self.net
        total = self.part[n.y, n.c].astype(F32) + self.cr[n.y].astype(F32)
        for c in self.far:
            c.wait_recv()
        return total + self.yr[0].astype(F32) + self.yr[1].astype(F32) + self.yr[2].astype(F32)

    def drain(self):
        for c in [self.core] + self.far:
            c.wait_send()


class GatherY:
    def __init__(self, net, g):
        self.net, self.g = net, g

    def start(self):
        n, g = self.net, self.g
        own = g.at[n.y, n.c]
        self.far = [n.copy(own, own, n.at(dy=d)) for d in (1, 2, 3)]
        self.near = [n.copy(own, own, n.at(dc=1))]
        for c in self.far + self.near:
            c.start()

    def step(self):
        n, g = self.net, self.g
        for d, c in zip((1, 2, 3), self.far):
            c.wait_recv()
            came = g.at[(n.y + 4 - d) % 4, n.c]
            on = n.copy(came, came, n.at(dc=1))
            on.start()
            self.near.append(on)

    def finish(self):
        for c in self.near:
            c.wait_recv()

    def drain(self):
        for c in self.far + self.near:
            c.wait_send()


def kernel(*refs):
    it = iter(refs)
    (x_in, cot_in, seg_a, seg_b, gains, wq_in, wg_in, wk_in, wv_in, wo_in, mg_in, mu_in, md_in) = (next(it) for _ in range(13))
    (bo, ig_out, gain1_out, qg_out, gg_out, kg_out, vg_out, og_out, gain2_out, mg_out, mu_out, md_out) = (next(it) for _ in range(12))
    (wqg, wkv, wo, wm, wd, kv, kvg) = (next(it) for _ in range(7))
    (xb, xn, xnt, g, hnb, hnt, dcb, igb) = (next(it) for _ in range(8))
    (part_a, part_b) = (next(it) for _ in range(2))
    yb = [tuple(next(it) for _ in range(2)) for _ in range(4)]
    (r1c, gp, ob, ot, qt, dot_, dqt, dmb, dadu, mt) = (next(it) for _ in range(10))
    (h32, z32, r32, dh32) = (next(it) for _ in range(4))
    (gx0, gxr, gx1, gzr, gy, gc) = (next(it) for _ in range(6))
    sb = [[next(it) for _ in range(4)] for _ in range(6)]
    send, recv, local = (next(it) for _ in range(3))

    net = Net(send, recv)
    s, x, z, y, c = net.s, net.x, net.z, net.y, net.c
    loads = []

    def load(src, dst):
        d = pltpu.make_async_copy(src, dst, local.at[len(loads)])
        d.start()
        loads.append(d)

    load(wo_in, wo.at[x, z, pl.ds(0, 256)])
    load(wq_in, wqg.at[x, z, :, pl.ds(0, 256)])
    load(wg_in, wqg.at[x, z, :, pl.ds(256, 256)])
    load(wk_in, wkv.at[x, z, :, pl.ds(0, 128)])
    load(wv_in, wkv.at[x, z, :, pl.ds(128, 128)])
    load(x_in, xb)
    load(md_in, wd.at[x, z])
    load(mg_in, wm.at[x, z, :, pl.ds(0, 768)])
    load(mu_in, wm.at[x, z, :, pl.ds(768, 768)])
    load(cot_in, g)
    line = lax.broadcasted_iota(jnp.int32, (16, 128), 0)
    tile = jnp.where(line == 0, gains[0:1, :].astype(F32), jnp.where(line == 1, gains[1:2, :].astype(F32), 0.0))
    wo[x, z, 256:272, :] = tile.astype(BF16)
    net.barrier()

    ag_o = Gather(net, wo, (64, 128, 208, 272))
    ag_qg = Gather(net, wqg, (32, 64, 96, 128))
    ag_kvw = Gather(net, wkv, (32, 64, 96, 128))
    ag_kv = Gather(net, kv, (64, 128, 192, 256))
    ag_d = Gather(net, wd, (192, 384, 576, 768))
    ag_m = Gather(net, wm, (32, 64, 96, 128))
    first = (ag_o, ag_qg, ag_kvw)
    for d in loads[:5]:
        d.wait()
    for a in first:
        a.start()

    loads[5].wait()

    def scales(i, _):
        rows = pl.ds(pl.multiple_of(i * 32, 32), 32)
        v = xb[rows, :].astype(F32)
        scale = lax.rsqrt(jnp.mean(v * v, axis=-1, keepdims=True) + EPS)
        r1c[rows, :] = jnp.broadcast_to(scale, (32, 128))
        return 0

    lax.fori_loop(0, 8, scales, 0)
    ids = seg_a[...].astype(F32)

    def below(v):
        return jnp.sum(jnp.where(ids < v, 1.0, 0.0), axis=(0, 1), keepdims=True)

    own_ids = seg_b[pl.ds(s, 1), :].astype(F32)
    first_key = jnp.where(own_ids > 2.5, below(2.5), jnp.where(own_ids > 1.5, below(1.5), jnp.where(own_ids > 0.5, below(0.5), 0.0)))
    first_key = jnp.concatenate([first_key, first_key], axis=1).astype(jnp.int32)
    query_place = s * 256 + lax.broadcasted_iota(jnp.int32, (1, 256), 1)
    query_place = jnp.concatenate([query_place, query_place], axis=1)
    top = jnp.max(ids, axis=(0, 1), keepdims=True)
    kept = below(top)

    for a in first:
        a.step(1)
    for d in loads[6:]:
        d.wait()

    def mask_cot(i, _):
        rows = pl.ds(pl.multiple_of(i * 32, 32), 32)
        place = (s * 256 + i * 32 + lax.broadcasted_iota(jnp.int32, (32, 1), 0)).astype(F32)
        g[rows, :] = jnp.where(place < kept, g[rows, :].astype(F32), 0.0).astype(BF16)
        return 0

    lax.fori_loop(0, 8, mask_cot, 0)

    def clear(j, _):
        kvg[j // 4, j % 4] = jnp.zeros((256, 256), BF16)
        return 0

    lax.fori_loop(s + 1, 16, clear, 0)
    for a in first:
        a.step(2)
    for a in first:
        a.step(3)
    ag_d.start()
    ag_o.finish()

    def gain_row(n):
        return jnp.concatenate([wo[j // 4, j % 4, 256:272, :].astype(F32)[n : n + 1, :] for j in range(16)], axis=1)

    gain1 = gain_row(0)

    def norm_in(i, _):
        rows = pl.ds(pl.multiple_of(i * 32, 32), 32)
        v = xb[rows, :].astype(F32) * r1c[rows, 0:1]
        xn[rows, :] = (v * gain1).astype(BF16)
        return 0

    lax.fori_loop(0, 8, norm_in, 0)
    ag_d.step(1)
    ag_kvw.finish()
    kv[x, z] = nn(xn[...], wkv[...].reshape(2048, 256)).astype(BF16)
    ag_kv.start()
    ag_qg.finish()
    qg = nn(xn[...], wqg[...].reshape(2048, 512))
    q = qg[:, :256].astype(BF16)
    gp[...] = qg[:, 256:]
    qt[...] = jnp.concatenate([q[:, :128].T, q[:, 128:].T], axis=1)
    ag_kv.step(1)
    ag_m.start()
    ag_kv.step(2)
    ag_kv.step(3)
    ag_d.step(2)
    ag_m.step(1)
    ag_kv.finish()

    ot[...] = jnp.zeros_like(ot)
    key_line = lax.broadcasted_iota(jnp.int32, (256, 512), 0)

    def scores(j):
        keys = kv[j // 4, j % 4, :, 0:128]
        values = kv[j // 4, j % 4, :, 128:256]
        place = j * 256 + key_line
        allowed = (place >= first_key) & (place <= query_place)
        return keys, values, jnp.where(allowed, nn(keys, qt[...]) * (SCALE * LOG2E), MASKED)

    def attend(j, state):
        top, total = state
        _, values, st = scores(j)
        new_top = jnp.maximum(top, jnp.max(st, axis=0, keepdims=True))
        probs = jnp.exp2(st - new_top)
        shrink = jnp.exp2(top - new_top)
        ot[...] = ot[...] * shrink + nn(values.T, probs.astype(BF16))
        return new_top, total * shrink + jnp.sum(probs, axis=0, keepdims=True)

    state = (jnp.full((1, 512), FLOOR, F32), jnp.zeros((1, 512), F32))
    top, total = lax.fori_loop(0, s + 1, attend, state)
    lse = top + jnp.log(total) * LOG2E
    ot[...] = ot[...] / total
    o = jnp.concatenate([ot[:, 0:256].T, ot[:, 256:512].T], axis=1)
    ob[...] = o
    yv = (o * jax.nn.sigmoid(gp[...])).astype(BF16)
    ag_m.step(2)
    ag_d.step(3)
    for j in range(8):
        w2 = jnp.concatenate([wo[j // 2, 2 * (j % 2) + i, 0:256, :] for i in (0, 1)], axis=1)
        part_a[:, :, :, 256 * j : 256 * j + 256] = nn(yv, w2).astype(BF16).reshape(4, 2, 32, 256)
    red = ReduceY(net, part_a, *yb[0])
    red.start()
    yt = yv.T
    gain2 = gain_row(1)
    red.step()
    own_rows = pl.ds(pl.multiple_of(net.k * ROWS, ROWS), ROWS)
    h = xb[own_rows, :].astype(F32) + red.finish()
    h32[...] = h
    scale2 = lax.rsqrt(jnp.mean(h * h, axis=-1, keepdims=True) + EPS)
    z2 = h * scale2
    z32[...] = z2
    r32[...] = jnp.broadcast_to(scale2, (ROWS, 128))
    hnb[y, c] = (z2 * gain2).astype(BF16)
    gat = GatherY(net, hnb)
    gat.start()
    ag_m.step(3)
    gat.step()
    ag_d.finish()

    for n in range(3):
        w2 = jnp.concatenate([wd[j // 4, j % 4, 256 * n : 256 * n + 256, :] for j in range(16)], axis=1)
        dmb[:, 256 * n : 256 * n + 256] = nt(g[...], w2)
    gat.finish()
    hn = hnb[...].reshape(256, 2048)
    for j in range(8):
        hnt[256 * j : 256 * j + 256, :] = hnb[:, :, :, 256 * j : 256 * j + 256].reshape(256, 256).T
    ag_m.finish()
    for n in range(3):
        cols = slice(256 * n, 256 * n + 256)
        up_cols = slice(768 + 256 * n, 1024 + 256 * n)
        a = nn(hn, wm[:, :, :, cols].reshape(2048, 256))
        u = nn(hn, wm[:, :, :, up_cols].reshape(2048, 256))
        sig = jax.nn.sigmoid(a)
        silu = a * sig
        mt[cols, :] = (silu * u).astype(BF16).T
        dm = dmb[:, cols]
        dadu[:, cols] = (dm * u * sig * (1.0 + a * (1.0 - sig))).astype(BF16)
        dadu[:, up_cols] = (dm * silu).astype(BF16)
    for a in first + (ag_d, ag_m):
        a.drain()
    red.drain()
    for j in range(8):
        w2 = wm[j // 2, 2 * (j % 2) : 2 * (j % 2) + 2].reshape(256, 1536)
        part_a[:, :, :, 256 * j : 256 * j + 256] = nt(dadu[...], w2).astype(BF16).reshape(4, 2, 32, 256)
    red3 = ReduceY(net, part_a, *yb[1])
    red3.start()
    for j in range(8):
        pm = nn(hnt[256 * j : 256 * j + 256, :], dadu[...])
        wm[j // 2, 2 * (j % 2) : 2 * (j % 2) + 2] = pm.astype(BF16).reshape(2, 128, 1536)
    red3.step()
    rs_m = Scatter(net, wm, 128, sb[0])
    rs_m.start()
    mm = mt[...].T
    for j in range(8):
        w2 = jnp.concatenate([wd[j // 2, 2 * (j % 2) + i] for i in (0, 1)], axis=1)
        part_b[:, :, :, 256 * j : 256 * j + 256] = nn(mm, w2).astype(BF16).reshape(4, 2, 32, 256)
    dhn = red3.finish()
    z2 = z32[...]
    e2 = dhn * gain2
    grads_gain2 = jnp.sum(dhn * z2, axis=0, keepdims=True)
    dh = g[own_rows, :].astype(F32) + r32[:, 0:1] * (e2 - z2 * jnp.mean(e2 * z2, axis=-1, keepdims=True))
    dh32[...] = dh
    dcb[y, c] = dh.astype(BF16)
    gat3 = GatherY(net, dcb)
    gat3.start()
    red2 = ReduceY(net, part_b, *yb[2])
    red2.start()
    for j in range(8):
        pd = nn(mt[...], g[:, 256 * j : 256 * j + 256])
        for i in (0, 1):
            wd[j // 2, 2 * (j % 2) + i] = pd[:, 128 * i : 128 * i + 128].astype(BF16)
    rs_d = Scatter(net, wd, 768, sb[1])
    rs_d.start()
    gat3.step()
    rs_m.step2()
    gat3.finish()
    dc = dcb[...].reshape(256, 2048)
    w2 = jnp.concatenate([wo[j // 4, j % 4, 0:256, :] for j in range(16)], axis=1)
    dy = nt(dc, w2)
    sig = jax.nn.sigmoid(gp[...])
    do = (dy * sig).astype(BF16)
    dg = (dy * ob[...] * sig * (1.0 - sig)).astype(BF16)
    for j in range(8):
        po = nn(yt, dcb[:, :, :, 256 * j : 256 * j + 256].reshape(256, 256))
        for i in (0, 1):
            wo[j // 2, 2 * (j % 2) + i, 0:256, :] = po[:, 128 * i : 128 * i + 128].astype(BF16)
    dot_[...] = jnp.concatenate([do[:, :128].T, do[:, 128:].T], axis=1)
    q_rows = jnp.concatenate([qt[:, 0:256].T, qt[:, 256:512].T], axis=0)
    do_rows = jnp.concatenate([do[:, :128], do[:, 128:]], axis=0)
    w = jnp.sum(dot_[...].astype(F32) * ot[...], axis=0, keepdims=True)
    red2.step()
    rs_d.step2()
    rs_m.step3()
    dqt[...] = jnp.zeros_like(dqt)

    def attend_back(j, _):
        keys, values, st = scores(j)
        probs = jnp.exp2(st - lse)
        dp = nn(values, dot_[...])
        ds = (probs * (dp - w) * SCALE).astype(BF16)
        kvg[j // 4, j % 4, :, 0:128] = nn(ds, q_rows).astype(BF16)
        kvg[j // 4, j % 4, :, 128:256] = nn(probs.astype(BF16), do_rows).astype(BF16)
        dqt[...] += nn(keys.T, ds)
        return 0

    lax.fori_loop(0, s + 1, attend_back, 0)
    rs_kv = Scatter(net, kvg, 256, sb[2])
    rs_kv.start()
    rs_d.step3()
    rs_m.step4()
    dq = jnp.concatenate([dqt[:, 0:256].T, dqt[:, 256:512].T], axis=1).astype(BF16)
    dqdg = jnp.concatenate([dq, dg], axis=1)
    rs_kv.step2()
    rs_d.step4()
    for j in range(8):
        xnt[256 * j : 256 * j + 256, :] = xn[:, 256 * j : 256 * j + 256].T
    red3.drain()
    rs_kv.step3()
    for j in range(8):
        w2 = wqg[j // 2, 2 * (j % 2) : 2 * (j % 2) + 2].reshape(256, 512)
        xn[:, 256 * j : 256 * j + 256] = nt(dqdg, w2).astype(BF16)
        pq = nn(xnt[256 * j : 256 * j + 256, :], dqdg)
        wqg[j // 2, 2 * (j % 2) : 2 * (j % 2) + 2] = pq.astype(BF16).reshape(2, 128, 512)
    rs_kv.step4()
    rs_qg = Scatter(net, wqg, 128, sb[3])
    rs_qg.start()
    rs_o = Scatter(net, wo, 256, sb[4])
    rs_o.start()

    def store_kv(rows, v):
        kv[0, 0, rows, :] = v.astype(BF16)

    ag_kv.drain()
    rs_kv.finish(store_kv)
    dkdv = kv[0, 0]
    for j in range(8):
        w2 = wkv[j // 2, 2 * (j % 2) : 2 * (j % 2) + 2].reshape(256, 256)
        px = nt(dkdv, w2) + xn[:, 256 * j : 256 * j + 256].astype(F32)
        part_a[:, :, :, 256 * j : 256 * j + 256] = px.astype(BF16).reshape(4, 2, 32, 256)
    red4 = ReduceY(net, part_a, *yb[3])
    red4.start()
    for j in range(8):
        pk = nn(xnt[256 * j : 256 * j + 256, :], dkdv)
        wkv[j // 2, 2 * (j % 2) : 2 * (j % 2) + 2] = pk.astype(BF16).reshape(2, 128, 256)
    rs_kvw = Scatter(net, wkv, 128, sb[5])
    rs_kvw.start()
    red4.step()
    rs_qg.step2()
    rs_o.step2()
    rs_kvw.step2()
    bo[y, c] = (h32[...] + red2.finish()).astype(BF16)
    gat2 = GatherY(net, bo)
    gat2.start()
    dxn = red4.finish()
    scale1 = r1c[own_rows, 0:1]
    z1 = xb[own_rows, :].astype(F32) * scale1
    e1 = dxn * gain1
    grads_gain1 = jnp.sum(dxn * z1, axis=0, keepdims=True)
    input_grad = dh32[...] + scale1 * (e1 - z1 * jnp.mean(e1 * z1, axis=-1, keepdims=True))
    igb[y, c] = input_grad.astype(BF16)
    gat4 = GatherY(net, igb)
    gat4.start()
    line8 = lax.broadcasted_iota(jnp.int32, (8, 128), 0)
    for j in range(16):
        cols = slice(128 * j, 128 * j + 128)
        gx0[j // 4, j % 4] = jnp.where(line8 == 0, grads_gain1[:, cols], jnp.where(line8 == 1, grads_gain2[:, cols], 0.0))
    cx = [net.copy(gx0.at[(x + d) % 4], gxr.at[d - 1], net.at(dx=d)) for d in (1, 2, 3)]
    for d in cx:
        d.start()
    rs_qg.step3()
    rs_o.step3()
    rs_kvw.step3()
    for d in cx:
        d.wait_recv()
    gx1[...] = gx0[x] + gxr[0] + gxr[1] + gxr[2]
    cz = [net.copy(gx1.at[(z + d) % 4], gzr.at[d - 1], net.at(dz=d)) for d in (1, 2, 3)]
    for d in cz:
        d.start()
    gat2.step()
    gat4.step()
    rs_qg.step4()
    rs_o.step4()
    rs_kvw.step4()
    for d in cz:
        d.wait_recv()
    gy[y] = gx1[z] + gzr[0] + gzr[1] + gzr[2]
    cy = [net.copy(gy.at[y], gy.at[y], net.at(dy=d)) for d in (1, 2, 3)]
    for d in cy:
        d.start()

    def store_m(rows, v):
        mg_out[rows, :] = v[:, :768]
        mu_out[rows, :] = v[:, 768:]

    def store_d(rows, v):
        md_out[rows, :] = v

    rs_m.finish(store_m)
    rs_d.finish(store_d)
    for d in cy:
        d.wait_recv()
    gc[c] = gy[0] + gy[1] + gy[2] + gy[3]
    cc = net.copy(gc.at[c], gc.at[c], net.at(dc=1))
    cc.start()

    def store_qg(rows, v):
        qg_out[rows, :] = v[:, :256]
        gg_out[rows, :] = v[:, 256:]

    def store_kvw(rows, v):
        kg_out[rows, :] = v[:, :128]
        vg_out[rows, :] = v[:, 128:]

    def store_o(rows, v):
        og_out[rows, :] = v

    rs_qg.finish(store_qg)
    rs_o.finish(store_o)
    rs_kvw.finish(store_kvw)
    gat2.finish()
    gat4.finish()

    def widen(i, _):
        ig_out[i // 2, i % 2] = igb[i // 2, i % 2].astype(F32)
        return 0

    lax.fori_loop(0, 8, widen, 0)
    cc.wait_recv()
    sums = gc[0] + gc[1]
    gain1_out[...] = sums[0:1, :]
    gain2_out[...] = sums[1:2, :]
    for a in (rs_m, rs_d, rs_kv, rs_qg, rs_o, rs_kvw, red2, red4, gat, gat2, gat3, gat4):
        a.drain()
    for d in cx + cz + cy + [cc]:
        d.wait_send()


def per_device(inputs, cotangent, segment_ids, attn_gain, query_weight, gate_weight, key_weight, value_weight, output_weight, mlp_gain, mlp_gate, mlp_up, mlp_down):
    v = pltpu.VMEM
    y_rows = (4, 2, ROWS, 2048)
    scratch = [
        v((4, 4, 128, 512), BF16),
        v((4, 4, 128, 256), BF16),
        v((4, 4, 272, 128), BF16),
        v((4, 4, 128, 1536), BF16),
        v((4, 4, 768, 128), BF16),
        v((4, 4, 256, 256), BF16),
        v((4, 4, 256, 256), BF16),
        v((256, 2048), BF16),
        v((256, 2048), BF16),
        v((2048, 256), BF16),
        v((256, 2048), BF16),
        v(y_rows, BF16),
        v((2048, 256), BF16),
        v(y_rows, BF16),
        v(y_rows, BF16),
        v(y_rows, BF16),
        v(y_rows, BF16),
    ]
    for _ in range(4):
        scratch += [v((4, ROWS, 2048), BF16), v((3, ROWS, 2048), BF16)]
    scratch += [
        v((256, 128), F32),
        v((256, 256), F32),
        v((256, 256), F32),
        v((128, 512), F32),
        v((128, 512), BF16),
        v((128, 512), BF16),
        v((128, 512), F32),
        v((256, 768), F32),
        v((256, 1536), BF16),
        v((768, 256), BF16),
        v((ROWS, 2048), F32),
        v((ROWS, 2048), F32),
        v((ROWS, 128), F32),
        v((ROWS, 2048), F32),
        v((4, 4, 8, 128), F32),
        v((3, 4, 8, 128), F32),
        v((4, 8, 128), F32),
        v((3, 8, 128), F32),
        v((4, 8, 128), F32),
        v((2, 8, 128), F32),
    ]
    for rows, cols in ((128, 1536), (768, 128), (256, 256), (128, 512), (256, 128), (128, 256)):
        scratch += scatter_bufs(rows, cols)
    n_sems = 320
    scratch += [pltpu.SemaphoreType.DMA((n_sems,)), pltpu.SemaphoreType.DMA((n_sems,)), pltpu.SemaphoreType.DMA((16,))]
    whole = pl.BlockSpec(memory_space=pltpu.VMEM)
    there = pl.BlockSpec(memory_space=pl.ANY)
    shape = jax.ShapeDtypeStruct
    outs = pl.pallas_call(
        kernel,
        out_shape=(
            shape(y_rows, BF16),
            shape(y_rows, F32),
            shape((1, 128), F32),
            shape((128, 256), F32),
            shape((128, 256), F32),
            shape((128, 128), F32),
            shape((128, 128), F32),
            shape((256, 128), F32),
            shape((1, 128), F32),
            shape((128, 768), F32),
            shape((128, 768), F32),
            shape((768, 128), F32),
        ),
        in_specs=[there, there, whole, whole, whole] + [there] * 8,
        out_specs=[whole] * 12,
        scratch_shapes=scratch,
        compiler_params=pltpu.CompilerParams(collective_id=0, has_side_effects=True, vmem_limit_bytes=63 << 20),
    )(
        inputs,
        cotangent,
        segment_ids.reshape(32, 128),
        segment_ids.reshape(16, 256),
        jnp.stack([attn_gain, mlp_gain]),
        query_weight,
        gate_weight,
        key_weight,
        value_weight,
        output_weight,
        mlp_gate,
        mlp_up,
        mlp_down,
    )
    outs = list(outs)
    outs[0] = outs[0].reshape(256, 2048)
    outs[1] = outs[1].reshape(256, 2048)
    outs[2] = outs[2].reshape(128)
    outs[8] = outs[8].reshape(128)
    return tuple(outs)


def solution(mesh):
    weights = (P("seq"), P("seq", "kv"), P("seq", "kv"), P("seq", "kv"), P("seq", "kv"), P("kv", "seq"))
    weights += (P("seq"), P("seq", "kv"), P("seq", "kv"), P("kv", "seq"))
    return jax.shard_map(
        per_device,
        mesh=mesh,
        in_specs=(P("seq", None), P("seq", None), P()) + weights,
        out_specs=(P("seq", None), P("seq", None)) + weights,
        check_vma=False,
    )
```

```python
import functools

import jax
import jax.numpy as jnp
from jax import lax
from jax.experimental import pallas as pl
from jax.experimental.pallas import tpu as pltpu
from jax.sharding import PartitionSpec as P

F32 = jnp.float32
BF16 = jnp.bfloat16
MESH = pl.DeviceIdType.MESH
EPS = 1e-06
HEAD = 128
SCALE = HEAD**-0.5
LOG2E = 1.4426950408889634
MASKED = -1e30
FLOOR = -1e29
ROWS = 32


def nn(left, right):
    return jnp.dot(left, right, preferred_element_type=F32)


def nt(left, right):
    return lax.dot_general(left, right, (((1,), (1,)), ((), ())), preferred_element_type=F32)


class Net:
    def __init__(self, sems):
        s, k = lax.axis_index("seq"), lax.axis_index("kv")
        self.s, self.k = s, k
        self.x, self.z, self.y, self.c = s // 4, s % 4, k // 2, k % 2
        self.sems, self.used = sems, 0

    def at(self, dx=0, dz=0, dy=0, dc=0):
        return {
            "kv": ((self.y + dy) % 4) * 2 + (self.c + dc) % 2,
            "seq": ((self.x + dx) % 4) * 4 + (self.z + dz) % 4,
        }

    def along(self, axis, d):
        return self.at(dx=d) if axis == 0 else self.at(dz=d)

    def sem(self):
        self.used += 1
        return self.sems.at[self.used - 1]

    def copy(self, src, dst, to, sent, came):
        return pltpu.make_async_remote_copy(
            src_ref=src,
            dst_ref=dst,
            send_sem=sent,
            recv_sem=came,
            device_id=to,
            device_id_type=MESH,
        )

    def send(self, src, dst, to, sent, came):
        self.copy(src, dst, to, sent, came).start()

    def wait_sent(self, ref, sem):
        self.copy(ref, ref, self.at(dc=1), sem, sem).wait_send()

    def wait_came(self, ref, sem):
        self.copy(ref, ref, self.at(dc=1), sem, sem).wait_recv()

    def barrier(self):
        sem = pltpu.get_barrier_semaphore()
        near = [self.at(dx=d) for d in (1, 2, 3)] + [self.at(dz=d) for d in (1, 2, 3)]
        near += [self.at(dy=d) for d in (1, 2, 3)] + [self.at(dc=1)]
        for to in near:
            pl.semaphore_signal(sem, inc=1, device_id=to, device_id_type=MESH)
        pl.semaphore_wait(sem, len(near))


class Gather:
    def __init__(self, net, w, cuts, cols=slice(None)):
        self.net, self.w, self.cols = net, w, cols
        q, h, q2, r = cuts
        self.spans = ((0, q, h), (h, q2, r))
        self.rows = pl.ds(0, r)
        self.sent = [net.sem() for _ in range(4)]
        self.came = [[[net.sem(), net.sem()], [net.sem()], [net.sem(), net.sem()], [net.sem()]] for _ in (0, 1)]

    def part(self, o, n):
        r0, r1, r2 = self.spans[o]
        return (pl.ds(r0, r2 - r0), pl.ds(r0, r1 - r0), pl.ds(r1, r2 - r1))[n]

    def single(self, o, a, n):
        x, z = (a, self.net.z) if o == 0 else (self.net.x, a)
        return self.w.at[x, z, self.part(o, n), self.cols]

    def bundle(self, o, b, n):
        rows = self.part(o, n)
        return self.w.at[:, b, rows, self.cols] if o == 0 else self.w.at[b, :, rows, self.cols]

    def push(self, o, n, ref, axis, d, sem):
        self.net.send(ref, ref, self.net.along(axis, d), self.sent[n], sem)

    def start(self):
        for o in (0, 1):
            own = self.single(o, (self.net.x, self.net.z)[o], 0)
            self.push(o, 0, own, o, 1, self.came[o][0][0])
            self.push(o, 0, own, o, -1, self.came[o][0][1])

    def step(self, n):
        net = self.net
        for o in (0, 1):
            me, other = (net.x, net.z) if o == 0 else (net.z, net.x)
            came = self.came[o]
            if n == 1:
                low, high = (me + 3) % 4, (me + 1) % 4
                net.wait_came(self.single(o, low, 0), came[0][0])
                self.push(o, 1, self.single(o, low, 1), o, 1, came[1][0])
                net.wait_came(self.single(o, high, 0), came[0][1])
                self.push(o, 1, self.single(o, high, 2), o, -1, came[1][0])
            elif n == 2:
                net.wait_came(self.single(o, (me + 2) % 4, 0), came[1][0])
                own = self.bundle(o, other, 0)
                self.push(o, 2, own, 1 - o, 1, came[2][0])
                self.push(o, 2, own, 1 - o, -1, came[2][1])
            else:
                low, high = (other + 3) % 4, (other + 1) % 4
                net.wait_came(self.bundle(o, low, 0), came[2][0])
                self.push(o, 3, self.bundle(o, low, 1), 1 - o, 1, came[3][0])
                net.wait_came(self.bundle(o, high, 0), came[2][1])
                self.push(o, 3, self.bundle(o, high, 2), 1 - o, -1, came[3][0])

    def finish(self):
        for o in (0, 1):
            other = self.net.z if o == 0 else self.net.x
            self.net.wait_came(self.bundle(o, (other + 2) % 4, 0), self.came[o][3][0])

    def drain(self):
        w, rows, cols = self.w, self.rows, self.cols
        for ref, sem in zip((w.at[0, 0:2, rows, cols], w.at[0, 0, rows, cols], w.at[0:2, :, rows, cols], w.at[0, :, rows, cols]), self.sent):
            self.net.wait_sent(ref, sem)


class Scatter:
    def __init__(self, net, p, rows, bufs, cols=slice(None)):
        self.net, self.p, self.bufs, self.cols = net, p, bufs, cols
        self.r, self.h, self.q = rows, rows // 2, rows // 4
        self.sent = [net.sem(), net.sem()]
        self.came = [[[net.sem(), net.sem()] for _ in range(4)] for _ in (0, 1)]

    def rows(self, o, part):
        base = o * self.h
        if part == 1:
            return pl.ds(base, self.q)
        if part == 2:
            return pl.ds(base + self.q, self.q)
        return pl.ds(base, self.h)

    def place(self, o):
        return (self.net.x, self.net.z) if o == 0 else (self.net.z, self.net.x)

    def bundle(self, o, a, part):
        r = self.rows(o, part)
        return self.p.at[a, :, r, self.cols] if o == 0 else self.p.at[:, a, r, self.cols]

    def block(self, o, a, i, part):
        r = self.rows(o, part)
        return self.p.at[a, i, r, self.cols] if o == 0 else self.p.at[i, a, r, self.cols]

    def half(self, side):
        return pl.ds(side * self.q, self.q)

    def start(self):
        r1, r2 = self.bufs[0], self.bufs[1]
        for o in (0, 1):
            me, _ = self.place(o)
            for side, d in ((0, 1), (1, -1)):
                self.net.send(self.bundle(o, (me + 2) % 4, 1 + side), r1.at[o, side], self.net.along(o, d), self.sent[0], self.came[o][0][side])
        for o in (0, 1):
            me, _ = self.place(o)
            for side, d in ((0, 1), (1, -1)):
                self.net.send(self.bundle(o, (me + d) % 4, 2 - side), r2.at[o, side, :, self.half(1 - side)], self.net.along(o, d), self.sent[0], self.came[o][1][side])

    def step2(self):
        r1, r2 = self.bufs[0], self.bufs[1]
        for o in (0, 1):
            me, _ = self.place(o)
            for side, d in ((0, 1), (1, -1)):
                a, part = (me + d) % 4, 1 + side
                self.net.wait_came(r1.at[o, side], self.came[o][0][side])

                def add(i, _, o=o, a=a, part=part, side=side):
                    b = self.block(o, a, i, part)
                    b[...] = (b[...].astype(F32) + r1[o, side, i].astype(F32)).astype(BF16)
                    return 0

                lax.fori_loop(0, 4, add, 0)
                self.net.send(self.bundle(o, a, part), r2.at[o, side, :, self.half(side)], self.net.along(o, d), self.sent[0], self.came[o][1][side])

    def step3(self):
        r2, r3, r4 = self.bufs[1], self.bufs[2], self.bufs[3]
        for o in (0, 1):
            me, other = self.place(o)
            for side in (0, 1):
                self.net.wait_came(r2.at[o, side], self.came[o][1][side])

            def add(i, o=o, me=me):
                b = self.block(o, me, i, 0)
                total = b[...].astype(F32) + r2[o, 0, i].astype(F32) + r2[o, 1, i].astype(F32)
                b[...] = total.astype(BF16)

            def far(n, _, add=add, other=other):
                add((other + 2 + n) % 4)
                return 0

            add((other + 2) % 4)
            for side, d in ((0, 1), (1, -1)):
                self.net.send(self.block(o, me, (other + 2) % 4, 1 + side), r3.at[o, side], self.net.along(1 - o, d), self.sent[1], self.came[o][2][side])
            lax.fori_loop(1, 4, far, 0)
            for side, d in ((0, 1), (1, -1)):
                self.net.send(self.block(o, me, (other + d) % 4, 2 - side), r4.at[o, side, self.half(1 - side)], self.net.along(1 - o, d), self.sent[1], self.came[o][3][side])

    def step4(self):
        r3, r4 = self.bufs[2], self.bufs[3]
        for o in (0, 1):
            me, other = self.place(o)
            for side, d in ((0, 1), (1, -1)):
                self.net.wait_came(r3.at[o, side], self.came[o][2][side])
                b = self.block(o, me, (other + d) % 4, 1 + side)
                b[...] = (b[...].astype(F32) + r3[o, side].astype(F32)).astype(BF16)
                self.net.send(b, r4.at[o, side, self.half(side)], self.net.along(1 - o, d), self.sent[1], self.came[o][3][side])

    def finish(self, store):
        r4 = self.bufs[3]
        for o in (0, 1):
            me, other = self.place(o)
            for side in (0, 1):
                self.net.wait_came(r4.at[o, side], self.came[o][3][side])
            total = self.block(o, me, other, 0)[...].astype(F32) + r4[o, 0].astype(F32) + r4[o, 1].astype(F32)
            store(self.rows(o, 0), total)

    def drain(self):
        rows = pl.ds(0, self.r)
        self.net.wait_sent(self.p.at[0:3, :, rows, self.cols], self.sent[0])
        self.net.wait_sent(self.p.at[0, 0:3, rows, self.cols], self.sent[1])


def scatter_bufs(rows, cols):
    h, q = rows // 2, rows // 4
    return [
        pltpu.VMEM((2, 2, 4, q, cols), BF16),
        pltpu.VMEM((2, 2, 4, h, cols), BF16),
        pltpu.VMEM((2, 2, q, cols), BF16),
        pltpu.VMEM((2, 2, h, cols), BF16),
    ]


class ReduceY:
    def __init__(self, net, part, cr, yr):
        self.net, self.part, self.cr, self.yr = net, part, cr, yr
        self.sent, self.came, self.core = [net.sem(), net.sem()], net.sem(), [net.sem(), net.sem()]

    def cols(self, n):
        return pl.ds(1024 * n, 1024)

    def start(self, n):
        net, cols = self.net, self.cols(n)
        net.send(self.part.at[:, 1 - net.c, :, cols], self.cr.at[:, :, cols], net.at(dc=1), self.sent[0], self.core[n])

    def step(self, n):
        net, cols = self.net, self.cols(n)
        net.wait_came(self.cr.at[:, :, cols], self.core[n])
        for d in (2, 1, 3):
            to = (net.y + d) % 4
            own = self.part.at[to, net.c, :, cols]
            own[...] = (own[...].astype(F32) + self.cr[to, :, cols].astype(F32)).astype(BF16)
            net.send(own, self.yr.at[d - 1, :, cols], net.at(dy=d), self.sent[1], self.came)

    def finish(self):
        net = self.net
        total = self.part[net.y, net.c].astype(F32) + self.cr[net.y].astype(F32)
        net.wait_came(self.yr, self.came)
        return total + self.yr[0].astype(F32) + self.yr[1].astype(F32) + self.yr[2].astype(F32)

    def drain(self):
        self.net.wait_sent(self.cr, self.sent[0])
        self.net.wait_sent(self.yr, self.sent[1])


class GatherY:
    def __init__(self, net, g):
        self.net, self.g = net, g
        self.sent, self.near, self.far = [net.sem(), net.sem()], net.sem(), [net.sem() for _ in range(3)]

    def start(self):
        n = self.net
        own = self.g.at[n.y, n.c]
        for d in (1, 2, 3):
            n.send(own, own, n.at(dy=d), self.sent[0], self.far[d - 1])
        n.send(own, own, n.at(dc=1), self.sent[1], self.near)

    def step(self):
        n = self.net
        for d in (1, 3, 2):
            came = self.g.at[(n.y + 4 - d) % 4, n.c]
            n.wait_came(came, self.far[d - 1])
            n.send(came, came, n.at(dc=1), self.sent[1], self.near)

    def finish(self):
        self.net.wait_came(self.g.at[:, 1 - self.net.c], self.near)

    def drain(self):
        self.net.wait_sent(self.g.at[0:3, 0], self.sent[0])
        self.net.wait_sent(self.g.at[:, 0], self.sent[1])


def kernel(*refs):
    it = iter(refs)

    def take(n):
        return [next(it) for _ in range(n)]

    x_in, cot_in, seg, gain_a, gain_b, wq_in, wg_in, wk_in, wv_in, wo_in, mg_in, mu_in, md_in = take(13)
    bo_out, ig_out, gain1_out, qg_out, gg_out, kg_out, vg_out, og_out, gain2_out, mg_out, mu_out, md_out = take(12)
    wq, wg, wkv, wo, wm, wd, kv, kvg = take(8)
    xb, xn, xnt, g, hnb, hnt, dcb, igb, bo = take(9)
    part_a, part_b = take(2)
    yb = [take(2) for _ in range(4)]
    r1c, gp, ob, ot, qt, dot_, dqt, dmb, ab, dadu, mt = take(11)
    h32, z32, r32, dh32 = take(4)
    gx0, gxr, gx1, gzr, gy, gc = take(6)
    mg_f, mu_f, md_f, og_f, qg_f, gg_f, kg_f, vg_f, gn_f = take(9)
    sb = [take(4) for _ in range(8)]
    sems, local = take(2)

    net = Net(sems)
    s, x, z, y, c = net.s, net.x, net.z, net.y, net.c
    moved = []

    def move(src, dst):
        d = pltpu.make_async_copy(src, dst, local.at[len(moved)])
        d.start()
        moved.append(d)
        return d

    load_kv = [move(wk_in, wkv.at[x, z, pl.ds(0, 128), pl.ds(0, 128)]), move(wv_in, wkv.at[x, z, pl.ds(0, 128), pl.ds(128, 128)])]
    load_q = move(wq_in, wq.at[x, z])
    load_g = move(wg_in, wg.at[x, z])
    load_o = move(wo_in, wo.at[x, z])
    load_x = move(x_in, xb)
    load_d = move(md_in, wd.at[x, z])
    load_m = [move(mg_in, wm.at[x, z, :, pl.ds(0, 768)]), move(mu_in, wm.at[x, z, :, pl.ds(768, 768)])]
    load_c = move(cot_in, g)
    line = lax.broadcasted_iota(jnp.int32, (16, 128), 0)
    tile = jnp.where(line == 0, gain_a[...].astype(F32), jnp.where(line == 1, gain_b[...].astype(F32), 0.0))
    wkv[x, z, 128:144, :] = jnp.concatenate([tile, tile], axis=1).astype(BF16)
    net.barrier()

    ag_kvw = Gather(net, wkv, (32, 64, 112, 144))
    ag_q = Gather(net, wq, (32, 64, 96, 128))
    ag_g = Gather(net, wg, (32, 64, 96, 128))
    ag_o = Gather(net, wo, (64, 128, 192, 256))
    ag_kv = Gather(net, kv, (64, 128, 192, 256))
    ag_d = Gather(net, wd, (192, 384, 576, 768))
    ag_mg = Gather(net, wm, (32, 64, 96, 128), pl.ds(0, 768))
    ag_mu = Gather(net, wm, (32, 64, 96, 128), pl.ds(768, 768))
    for d in load_kv:
        d.wait()
    ag_kvw.start()
    load_q.wait()
    ag_q.start()
    load_g.wait()
    ag_g.start()
    load_o.wait()
    ag_o.start()
    load_d.wait()
    ag_d.start()

    load_x.wait()

    def scales(i, _):
        rows = pl.ds(pl.multiple_of(i * 32, 32), 32)
        v = xb[rows, :].astype(F32)
        scale = lax.rsqrt(jnp.mean(v * v, axis=-1, keepdims=True) + EPS)
        r1c[rows, :] = jnp.broadcast_to(scale, (32, 128))
        return 0

    lax.fori_loop(0, 8, scales, 0)
    ids = seg[...].astype(F32)

    def below(v):
        return jnp.sum(jnp.where(ids < v, 1.0, 0.0), axis=(0, 1), keepdims=True)

    own_ids = jnp.concatenate([seg[pl.ds(2 * s, 1), :], seg[pl.ds(2 * s + 1, 1), :]], axis=1).astype(F32)
    first_key = jnp.where(own_ids > 2.5, below(2.5), jnp.where(own_ids > 1.5, below(1.5), jnp.where(own_ids > 0.5, below(0.5), 0.0)))
    first_key = jnp.concatenate([first_key, first_key], axis=1).astype(jnp.int32)
    query_place = s * 256 + lax.broadcasted_iota(jnp.int32, (1, 256), 1)
    query_place = jnp.concatenate([query_place, query_place], axis=1)
    top = jnp.max(ids, axis=(0, 1), keepdims=True)
    kept = below(top)

    ag_kvw.step(1)
    ag_q.step(1)
    load_c.wait()

    def mask_cot(i, _):
        rows = pl.ds(pl.multiple_of(i * 32, 32), 32)
        place = (s * 256 + i * 32 + lax.broadcasted_iota(jnp.int32, (32, 1), 0)).astype(F32)
        g[rows, :] = jnp.where(place < kept, g[rows, :].astype(F32), 0.0).astype(BF16)
        return 0

    lax.fori_loop(0, 8, mask_cot, 0)
    pairs = (s + 2) // 2

    def clear(j, _):
        kvg[j // 4, j % 4] = jnp.zeros((256, 256), BF16)
        return 0

    lax.fori_loop(2 * pairs, 16, clear, 0)
    ag_kvw.step(2)
    ag_q.step(2)
    ag_g.step(1)
    ag_o.step(1)
    ag_d.step(1)
    ag_kvw.step(3)
    ag_q.step(3)
    ag_g.step(2)
    ag_kvw.finish()

    def gain_row(n):
        return jnp.concatenate([wkv[j // 4, j % 4, 128:144, 0:128].astype(F32)[n : n + 1, :] for j in range(16)], axis=1)

    gain1 = gain_row(0)
    gain2 = gain_row(1)

    def norm_in(i, _):
        rows = pl.ds(pl.multiple_of(i * 32, 32), 32)
        v = xb[rows, :].astype(F32) * r1c[rows, 0:1]
        xn[rows, :] = (v * gain1).astype(BF16)
        return 0

    lax.fori_loop(0, 8, norm_in, 0)
    kv[x, z] = nn(xn[...], wkv[:, :, 0:128, :].reshape(2048, 256)).astype(BF16)
    ag_kv.start()
    for d in load_m:
        d.wait()
    ag_mg.start()
    ag_q.finish()
    q = nn(xn[...], wq[...].reshape(2048, 256)).astype(BF16)
    qt[...] = jnp.concatenate([q[:, :128].T, q[:, 128:].T], axis=1)
    ag_kv.step(1)
    ag_o.step(2)
    ag_kv.step(2)
    ag_mg.step(1)
    ag_mu.start()
    for j in range(8):
        xnt[256 * j : 256 * j + 256, :] = xn[:, 256 * j : 256 * j + 256].T
    ag_kv.step(3)
    ag_g.step(3)
    ag_o.step(3)
    ag_mu.step(1)
    ag_d.step(2)
    ag_mg.step(2)
    ag_kv.finish()

    ot[...] = jnp.zeros_like(ot)
    key_line = lax.broadcasted_iota(jnp.int32, (512, 512), 0)

    def scores(i):
        both = kv[i // 2, pl.ds(2 * (i % 2), 2)].reshape(512, 256)
        keys, values = both[:, 0:128], both[:, 128:256]
        place = i * 512 + key_line
        allowed = (place >= first_key) & (place <= query_place)
        return keys, values, jnp.where(allowed, nn(keys, qt[...]) * (SCALE * LOG2E), MASKED)

    def attend(i, state):
        top, total = state
        _, values, st = scores(i)
        new_top = jnp.maximum(top, jnp.max(st, axis=0, keepdims=True))
        probs = jnp.exp2(st - new_top)
        shrink = jnp.exp2(top - new_top)
        ot[...] = ot[...] * shrink + nn(values.T, probs.astype(BF16))
        return new_top, total * shrink + jnp.sum(probs, axis=0, keepdims=True)

    state = (jnp.full((1, 512), FLOOR, F32), jnp.zeros((1, 512), F32))
    top, total = lax.fori_loop(0, pairs, attend, state)
    lse = top + jnp.log(total) * LOG2E
    ot[...] = ot[...] / total
    o = jnp.concatenate([ot[:, 0:256].T, ot[:, 256:512].T], axis=1)
    ob[...] = o
    ag_g.finish()
    gp[...] = nn(xn[...], wg[...].reshape(2048, 256))
    yv = (o * jax.nn.sigmoid(gp[...])).astype(BF16)
    ag_o.finish()
    red = ReduceY(net, part_a, *yb[0])
    for j in range(8):
        w2 = jnp.concatenate([wo[j // 2, 2 * (j % 2) + i] for i in (0, 1)], axis=1)
        part_a[:, :, :, 256 * j : 256 * j + 256] = nn(yv, w2).astype(BF16).reshape(4, 2, 32, 256)
        if j % 4 == 3:
            red.start(j // 4)
    ag_d.step(3)
    red.step(0)
    red.step(1)
    ag_mg.step(3)
    ag_mu.step(2)
    yt = yv.T
    own_rows = pl.ds(pl.multiple_of(net.k * ROWS, ROWS), ROWS)
    h = xb[own_rows, :].astype(F32) + red.finish()
    h32[...] = h
    scale2 = lax.rsqrt(jnp.mean(h * h, axis=-1, keepdims=True) + EPS)
    z2 = h * scale2
    z32[...] = z2
    r32[...] = jnp.broadcast_to(scale2, (ROWS, 128))
    hnb[y, c] = (z2 * gain2).astype(BF16)
    gat = GatherY(net, hnb)
    gat.start()
    ag_d.finish()

    for n in range(3):
        w2 = jnp.concatenate([wd[j // 4, j % 4, 256 * n : 256 * n + 256, :] for j in range(16)], axis=1)
        dmb[:, 256 * n : 256 * n + 256] = nt(g[...], w2)
    gat.step()
    gat.finish()
    hn = hnb[...].reshape(256, 2048)
    for j in range(8):
        hnt[256 * j : 256 * j + 256, :] = hnb[:, :, :, 256 * j : 256 * j + 256].reshape(256, 256).T
    ag_mu.step(3)
    ag_mg.finish()
    for n in range(3):
        ab[:, 256 * n : 256 * n + 256] = nn(hn, wm[:, :, :, 256 * n : 256 * n + 256].reshape(2048, 256))
    ag_mu.finish()
    for n in range(3):
        cols = slice(256 * n, 256 * n + 256)
        up_cols = slice(768 + 256 * n, 1024 + 256 * n)
        a = ab[:, cols]
        u = nn(hn, wm[:, :, :, up_cols].reshape(2048, 256))
        sig = jax.nn.sigmoid(a)
        silu = a * sig
        mt[cols, :] = (silu * u).astype(BF16).T
        dm = dmb[:, cols]
        dadu[:, cols] = (dm * u * sig * (1.0 + a * (1.0 - sig))).astype(BF16)
        dadu[:, up_cols] = (dm * silu).astype(BF16)
    for a in (ag_kvw, ag_q, ag_g, ag_o, ag_d, ag_mg, ag_mu, red):
        a.drain()
    mm = mt[...].T
    for j in range(8):
        w2 = jnp.concatenate([wd[j // 2, 2 * (j % 2) + i] for i in (0, 1)], axis=1)
        part_b[:, :, :, 256 * j : 256 * j + 256] = nn(mm, w2).astype(BF16).reshape(4, 2, 32, 256)
    for j in range(8):
        pd = nn(mt[...], g[:, 256 * j : 256 * j + 256])
        for i in (0, 1):
            wd[j // 2, 2 * (j % 2) + i] = pd[:, 128 * i : 128 * i + 128].astype(BF16)
    rs_d = Scatter(net, wd, 768, sb[0])
    rs_d.start()
    red3 = ReduceY(net, part_a, *yb[1])
    for j in range(8):
        w2 = wm[j // 2, 2 * (j % 2) : 2 * (j % 2) + 2].reshape(256, 1536)
        part_a[:, :, :, 256 * j : 256 * j + 256] = nt(dadu[...], w2).astype(BF16).reshape(4, 2, 32, 256)
        if j % 4 == 3:
            red3.start(j // 4)
    rs_mg = Scatter(net, wm, 128, sb[1], pl.ds(0, 768))
    rs_mu = Scatter(net, wm, 128, sb[2], pl.ds(768, 768))
    red3.step(0)
    for n, rs in ((0, rs_mg), (1, rs_mu)):
        for j in range(8):
            pm = nn(hnt[256 * j : 256 * j + 256, :], dadu[:, 768 * n : 768 * n + 768])
            wm[j // 2, 2 * (j % 2) : 2 * (j % 2) + 2, :, 768 * n : 768 * n + 768] = pm.astype(BF16).reshape(2, 128, 768)
            if n == 0 and j == 3:
                red3.step(1)
        rs.start()
    dhn = red3.finish()
    z2 = z32[...]
    e2 = dhn * gain2
    grads_gain2 = jnp.sum(dhn * z2, axis=0, keepdims=True)
    dh = g[own_rows, :].astype(F32) + r32[:, 0:1] * (e2 - z2 * jnp.mean(e2 * z2, axis=-1, keepdims=True))
    dh32[...] = dh
    dcb[y, c] = dh.astype(BF16)
    gat3 = GatherY(net, dcb)
    gat3.start()
    red2 = ReduceY(net, part_b, *yb[2])
    red2.start(0)
    red2.start(1)
    rs_d.step2()
    gat3.step()
    red2.step(0)
    red2.step(1)
    gat3.finish()
    dc = dcb[...].reshape(256, 2048)
    w2 = jnp.concatenate([wo[j // 4, j % 4] for j in range(16)], axis=1)
    dy = nt(dc, w2)
    sig = jax.nn.sigmoid(gp[...])
    do = (dy * sig).astype(BF16)
    dg = (dy * ob[...] * sig * (1.0 - sig)).astype(BF16)
    dot_[...] = jnp.concatenate([do[:, :128].T, do[:, 128:].T], axis=1)
    q_rows = jnp.concatenate([qt[:, 0:256].T, qt[:, 256:512].T], axis=0)
    do_rows = jnp.concatenate([do[:, :128], do[:, 128:]], axis=0)
    w = jnp.sum(dot_[...].astype(F32) * ot[...], axis=0, keepdims=True)
    dqt[...] = jnp.zeros_like(dqt)
    rs_mg.step2()

    def attend_back(i, _):
        keys, values, st = scores(i)
        probs = jnp.exp2(st - lse)
        dp = nn(values, dot_[...])
        ds = (probs * (dp - w) * SCALE).astype(BF16)
        dk = nn(ds, q_rows).astype(BF16)
        dv = nn(probs.astype(BF16), do_rows).astype(BF16)
        kvg[i // 2, pl.ds(2 * (i % 2), 2)] = jnp.concatenate([dk, dv], axis=1).reshape(2, 256, 256)
        dqt[...] += nn(keys.T, ds)
        return 0

    lax.fori_loop(0, pairs, attend_back, 0)
    rs_kv = Scatter(net, kvg, 256, sb[3])
    rs_kv.start()
    rs_mu.step2()
    for j in range(8):
        po = nn(yt, dcb[:, :, :, 256 * j : 256 * j + 256].reshape(256, 256))
        for i in (0, 1):
            wo[j // 2, 2 * (j % 2) + i] = po[:, 128 * i : 128 * i + 128].astype(BF16)
    rs_o = Scatter(net, wo, 256, sb[4])
    rs_o.start()
    rs_kv.step2()
    dq = jnp.concatenate([dqt[:, 0:256].T, dqt[:, 256:512].T], axis=1).astype(BF16)
    for j in range(8):
        pair = (j // 2, slice(2 * (j % 2), 2 * (j % 2) + 2))
        xnt_j = xnt[256 * j : 256 * j + 256, :]
        xn[:, 256 * j : 256 * j + 256] = (nt(dq, wq[pair].reshape(256, 256)) + nt(dg, wg[pair].reshape(256, 256))).astype(BF16)
        wq[pair] = nn(xnt_j, dq).astype(BF16).reshape(2, 128, 256)
        wg[pair] = nn(xnt_j, dg).astype(BF16).reshape(2, 128, 256)
    rs_g = Scatter(net, wg, 128, sb[5])
    rs_g.start()
    bo[y, c] = (h32[...] + red2.finish()).astype(BF16)
    gat2 = GatherY(net, bo)
    gat2.start()
    rs_kv.step3()
    rs_q = Scatter(net, wq, 128, sb[6])
    rs_q.start()
    rs_d.step3()
    rs_mg.step3()
    rs_kv.step4()
    rs_o.step2()
    rs_g.step2()
    for a in (ag_kv, red3):
        a.drain()

    def store_kv(rows, v):
        kv[0, 0, rows, :] = v.astype(BF16)

    rs_kv.finish(store_kv)
    dkdv = kv[0, 0]
    red4 = ReduceY(net, part_a, *yb[3])
    for j in range(8):
        w2 = wkv[j // 2, 2 * (j % 2) : 2 * (j % 2) + 2, 0:128, :].reshape(256, 256)
        px = nt(dkdv, w2) + xn[:, 256 * j : 256 * j + 256].astype(F32)
        part_a[:, :, :, 256 * j : 256 * j + 256] = px.astype(BF16).reshape(4, 2, 32, 256)
        if j % 4 == 3:
            red4.start(j // 4)
    for j in range(8):
        pk = nn(xnt[256 * j : 256 * j + 256, :], dkdv)
        wkv[j // 2, 2 * (j % 2) : 2 * (j % 2) + 2, 0:128, :] = pk.astype(BF16).reshape(2, 128, 256)
    rs_kvw = Scatter(net, wkv, 128, sb[7])
    rs_kvw.start()
    red4.step(0)
    red4.step(1)
    rs_mu.step3()
    rs_q.step2()
    rs_kvw.step2()
    rs_d.step4()
    rs_mg.step4()
    rs_o.step3()
    rs_g.step3()
    dxn = red4.finish()
    scale1 = r1c[own_rows, 0:1]
    z1 = xb[own_rows, :].astype(F32) * scale1
    e1 = dxn * gain1
    grads_gain1 = jnp.sum(dxn * z1, axis=0, keepdims=True)
    input_grad = dh32[...] + scale1 * (e1 - z1 * jnp.mean(e1 * z1, axis=-1, keepdims=True))
    igb[y, c] = input_grad.astype(BF16)
    gat4 = GatherY(net, igb)
    gat4.start()
    line8 = lax.broadcasted_iota(jnp.int32, (8, 128), 0)
    for j in range(16):
        cols = slice(128 * j, 128 * j + 128)
        gx0[j // 4, j % 4] = jnp.where(line8 == 0, grads_gain1[:, cols], jnp.where(line8 == 1, grads_gain2[:, cols], 0.0))
    sx, sz, sy, sc = ([net.sem(), net.sem()] for _ in range(4))
    for d in (1, 2, 3):
        net.send(gx0.at[(x + d) % 4], gxr.at[d - 1], net.at(dx=d), *sx)
    rs_kvw.step3()
    rs_q.step3()
    rs_mu.step4()
    rs_o.step4()
    rs_g.step4()

    def keep(ref):
        def store(rows, v):
            ref[rows, :] = v

        return store

    net.wait_came(gxr, sx[1])
    gx1[...] = gx0[x] + gxr[0] + gxr[1] + gxr[2]
    for d in (1, 2, 3):
        net.send(gx1.at[(z + d) % 4], gzr.at[d - 1], net.at(dz=d), *sz)
    rs_d.finish(keep(md_f))
    move(md_f, md_out)
    rs_mg.finish(keep(mg_f))
    move(mg_f, mg_out)
    gat2.step()
    rs_kvw.step4()
    rs_q.step4()
    net.wait_came(gzr, sz[1])
    gy[y] = gx1[z] + gzr[0] + gzr[1] + gzr[2]
    for d in (1, 2, 3):
        net.send(gy.at[y], gy.at[y], net.at(dy=d), *sy)
    rs_mu.finish(keep(mu_f))
    move(mu_f, mu_out)
    rs_o.finish(keep(og_f))
    move(og_f, og_out)
    rs_g.finish(keep(gg_f))
    move(gg_f, gg_out)
    gat4.step()

    def store_kvw(rows, v):
        kg_f[rows, :] = v[:, :128]
        vg_f[rows, :] = v[:, 128:]

    gat2.finish()
    move(bo, bo_out)
    net.wait_came(gy.at[0:3], sy[1])
    gc[c] = gy[0] + gy[1] + gy[2] + gy[3]
    net.send(gc.at[c], gc.at[c], net.at(dc=1), *sc)
    rs_q.finish(keep(qg_f))
    move(qg_f, qg_out)
    rs_kvw.finish(store_kvw)
    move(kg_f, kg_out)
    move(vg_f, vg_out)
    gat4.finish()
    move(igb, ig_out)
    net.wait_came(gc.at[0], sc[1])
    gn_f[...] = gc[0] + gc[1]
    move(gn_f.at[pl.ds(0, 1)], gain1_out)
    move(gn_f.at[pl.ds(1, 1)], gain2_out)
    for a in (rs_mg, rs_mu, rs_d, rs_kv, rs_g, rs_q, rs_o, rs_kvw, red2, red4, gat, gat2, gat3, gat4):
        a.drain()
    net.wait_sent(gxr, sx[0])
    net.wait_sent(gzr, sz[0])
    net.wait_sent(gy.at[0:3], sy[0])
    net.wait_sent(gc.at[0], sc[0])
    for d in moved[10:]:
        d.wait()


def place_outputs(*refs):
    ins, outs, bufs, (wide, sems) = refs[:12], refs[12:24], refs[24:36], refs[36:]
    spans = [pl.ds(64 * i, 64) for i in range(4)]
    loads = [pltpu.make_async_copy(ins[1].at[r], bufs[1].at[r], sems.at[i]) for i, r in enumerate(spans)]
    order = [0, 9, 10, 11, 3, 4, 5, 6, 7, 2, 8]
    rest = [pltpu.make_async_copy(ins[i], bufs[i], sems.at[4 + i]) for i in order]
    for d in loads + rest:
        d.start()
    copies = []

    def out(src, dst, n):
        d = pltpu.make_async_copy(src, dst, sems.at[n])
        d.start()
        copies.append(d)

    for i, r in enumerate(spans):
        loads[i].wait()
        wide[r, :] = bufs[1][r, :].astype(F32)
        out(wide.at[r], outs[1].at[r], 16 + i)
    for i, d in zip(order, rest):
        d.wait()
        out(bufs[i], outs[i], 20 + i)
    for d in copies:
        d.wait()


def per_device(inputs, cotangent, segment_ids, attn_gain, query_weight, gate_weight, key_weight, value_weight, output_weight, mlp_gain, mlp_gate, mlp_up, mlp_down):
    v = pltpu.VMEM
    y_rows = (4, 2, ROWS, 2048)
    scratch = [
        v((4, 4, 128, 256), BF16),
        v((4, 4, 128, 256), BF16),
        v((4, 4, 144, 256), BF16),
        v((4, 4, 256, 128), BF16),
        v((4, 4, 128, 1536), BF16),
        v((4, 4, 768, 128), BF16),
        v((4, 4, 256, 256), BF16),
        v((4, 4, 256, 256), BF16),
        v((256, 2048), BF16),
        v((256, 2048), BF16),
        v((2048, 256), BF16),
        v((256, 2048), BF16),
        v(y_rows, BF16),
        v((2048, 256), BF16),
        v(y_rows, BF16),
        v(y_rows, BF16),
        v(y_rows, BF16),
        v(y_rows, BF16),
        v(y_rows, BF16),
    ]
    for _ in range(4):
        scratch += [v((4, ROWS, 2048), BF16), v((3, ROWS, 2048), BF16)]
    scratch += [
        v((256, 128), F32),
        v((256, 256), F32),
        v((256, 256), F32),
        v((128, 512), F32),
        v((128, 512), BF16),
        v((128, 512), BF16),
        v((128, 512), F32),
        v((256, 768), F32),
        v((256, 768), F32),
        v((256, 1536), BF16),
        v((768, 256), BF16),
        v((ROWS, 2048), F32),
        v((ROWS, 2048), F32),
        v((ROWS, 128), F32),
        v((ROWS, 2048), F32),
        v((4, 4, 8, 128), F32),
        v((3, 4, 8, 128), F32),
        v((4, 8, 128), F32),
        v((3, 8, 128), F32),
        v((4, 8, 128), F32),
        v((2, 8, 128), F32),
    ]
    grad_shapes = ((128, 768), (128, 768), (768, 128), (256, 128), (128, 256), (128, 256), (128, 128), (128, 128), (8, 128))
    scratch += [v(dims, F32) for dims in grad_shapes]
    for rows, cols in ((768, 128), (128, 768), (128, 768), (256, 256), (256, 128), (128, 256), (128, 256), (128, 256)):
        scratch += scatter_bufs(rows, cols)
    scratch += [pltpu.SemaphoreType.DMA((324,)), pltpu.SemaphoreType.DMA((24,))]
    whole = pl.BlockSpec(memory_space=pltpu.VMEM)
    there = pl.BlockSpec(memory_space=pl.ANY)
    shape = jax.ShapeDtypeStruct
    out_shape = (
        shape((256, 2048), BF16),
        shape((256, 2048), F32),
        shape((1, 128), F32),
        shape((128, 256), F32),
        shape((128, 256), F32),
        shape((128, 128), F32),
        shape((128, 128), F32),
        shape((256, 128), F32),
        shape((1, 128), F32),
        shape((128, 768), F32),
        shape((128, 768), F32),
        shape((768, 128), F32),
    )
    outs = pl.pallas_call(
        kernel,
        out_shape=(shape(y_rows, BF16), shape(y_rows, BF16)) + out_shape[2:],
        in_specs=[there, there, whole, whole, whole] + [there] * 8,
        out_specs=[there] * 12,
        scratch_shapes=scratch,
        compiler_params=pltpu.CompilerParams(collective_id=0, has_side_effects=True, vmem_limit_bytes=63 << 20),
    )(
        inputs,
        cotangent,
        segment_ids.reshape(32, 128),
        attn_gain.reshape(1, 128),
        mlp_gain.reshape(1, 128),
        query_weight,
        gate_weight,
        key_weight,
        value_weight,
        output_weight,
        mlp_gate,
        mlp_up,
        mlp_down,
    )
    outs = pl.pallas_call(
        place_outputs,
        out_shape=out_shape,
        in_specs=[there] * 12,
        out_specs=[there] * 12,
        scratch_shapes=[v(o.shape, BF16 if i == 1 else o.dtype) for i, o in enumerate(out_shape)] + [v((256, 2048), F32), pltpu.SemaphoreType.DMA((32,))],
        compiler_params=pltpu.CompilerParams(vmem_limit_bytes=60 << 20),
    )(outs[0].reshape(256, 2048), outs[1].reshape(256, 2048), *outs[2:])
    outs = list(outs)
    outs[2] = outs[2].reshape(128)
    outs[8] = outs[8].reshape(128)
    return tuple(outs)


def solution(mesh):
    weights = (P("seq"), P("seq", "kv"), P("seq", "kv"), P("seq", "kv"), P("seq", "kv"), P("kv", "seq"))
    weights += (P("seq"), P("seq", "kv"), P("seq", "kv"), P("kv", "seq"))
    return jax.shard_map(
        per_device,
        mesh=mesh,
        in_specs=(P("seq", None), P("seq", None), P()) + weights,
        out_specs=(P("seq", None), P("seq", None)) + weights,
        check_vma=False,
    )
```

```python
import functools

import jax
import jax.numpy as jnp
from jax import lax
from jax.experimental import pallas as pl
from jax.experimental.pallas import tpu as pltpu
from jax.sharding import PartitionSpec as P

F32 = jnp.float32
BF16 = jnp.bfloat16
MESH = pl.DeviceIdType.MESH
EPS = 1e-06
HEAD = 128
SCALE = HEAD**-0.5
LOG2E = 1.4426950408889634
MASKED = -1e30
FLOOR = -1e29
ROWS = 32


def nn(left, right):
    return jnp.dot(left, right, preferred_element_type=F32)


def nt(left, right):
    return lax.dot_general(left, right, (((1,), (1,)), ((), ())), preferred_element_type=F32)


def half_rows(n):
    return pl.ds(16 * n, 16)


class Net:
    def __init__(self, sems):
        s, k = lax.axis_index("seq"), lax.axis_index("kv")
        self.s, self.k = s, k
        self.x, self.z, self.y, self.c = s // 4, s % 4, k // 2, k % 2
        self.sems, self.used = sems, 0

    def at(self, dx=0, dz=0, dy=0, dc=0):
        return {
            "kv": ((self.y + dy) % 4) * 2 + (self.c + dc) % 2,
            "seq": ((self.x + dx) % 4) * 4 + (self.z + dz) % 4,
        }

    def along(self, axis, d):
        return self.at(dx=d) if axis == 0 else self.at(dz=d)

    def sem(self):
        self.used += 1
        return self.sems.at[self.used - 1]

    def copy(self, src, dst, to, sent, came):
        return pltpu.make_async_remote_copy(
            src_ref=src,
            dst_ref=dst,
            send_sem=sent,
            recv_sem=came,
            device_id=to,
            device_id_type=MESH,
        )

    def send(self, src, dst, to, sent, came):
        self.copy(src, dst, to, sent, came).start()

    def wait_sent(self, ref, sem):
        self.copy(ref, ref, self.at(dc=1), sem, sem).wait_send()

    def wait_came(self, ref, sem):
        self.copy(ref, ref, self.at(dc=1), sem, sem).wait_recv()

    def barrier(self):
        sem = pltpu.get_barrier_semaphore()
        near = [self.at(dx=d) for d in (1, 2, 3)] + [self.at(dz=d) for d in (1, 2, 3)]
        near += [self.at(dy=d) for d in (1, 2, 3)] + [self.at(dc=1)]
        for to in near:
            pl.semaphore_signal(sem, inc=1, device_id=to, device_id_type=MESH)
        pl.semaphore_wait(sem, len(near))


class Gather:
    def __init__(self, net, w, cuts, cols=slice(None)):
        self.net, self.w, self.cols = net, w, cols
        q, h, q2, r = cuts
        self.spans = ((0, q, h), (h, q2, r))
        self.sent = [net.sem() for _ in range(2)]
        self.came = [net.sem() for _ in range(4)]
        rows = pl.ds(0, r)
        self.sizes = [w.at[0, 0:2, rows, cols], w.at[0, 0, rows, cols], w.at[0:2, :, rows, cols], w.at[0, :, rows, cols]]
        self.totals = [w.at[0, 0:3, rows, cols], w.at[0:3, :, rows, cols]]

    def part(self, o, n):
        r0, r1, r2 = self.spans[o]
        return (pl.ds(r0, r2 - r0), pl.ds(r0, r1 - r0), pl.ds(r1, r2 - r1))[n]

    def single(self, o, a, n):
        x, z = (a, self.net.z) if o == 0 else (self.net.x, a)
        return self.w.at[x, z, self.part(o, n), self.cols]

    def bundle(self, o, b, n):
        rows = self.part(o, n)
        return self.w.at[:, b, rows, self.cols] if o == 0 else self.w.at[b, :, rows, self.cols]

    def push(self, n, ref, axis, d):
        self.net.send(ref, ref, self.net.along(axis, d), self.sent[n // 2], self.came[n])

    def start(self):
        for o in (0, 1):
            own = self.single(o, (self.net.x, self.net.z)[o], 0)
            self.push(0, own, o, 1)
            self.push(0, own, o, -1)

    def step(self, n):
        net = self.net
        net.wait_came(self.sizes[n - 1], self.came[n - 1])
        for o in (0, 1):
            me, other = (net.x, net.z) if o == 0 else (net.z, net.x)
            if n == 1:
                self.push(1, self.single(o, (me + 3) % 4, 1), o, 1)
                self.push(1, self.single(o, (me + 1) % 4, 2), o, -1)
            elif n == 2:
                own = self.bundle(o, other, 0)
                self.push(2, own, 1 - o, 1)
                self.push(2, own, 1 - o, -1)
            else:
                self.push(3, self.bundle(o, (other + 3) % 4, 1), 1 - o, 1)
                self.push(3, self.bundle(o, (other + 1) % 4, 2), 1 - o, -1)

    def finish(self):
        self.net.wait_came(self.sizes[3], self.came[3])

    def drain(self):
        for ref, sem in zip(self.totals, self.sent):
            self.net.wait_sent(ref, sem)


class Scatter:
    def __init__(self, net, p, rows, bufs, cols=slice(None)):
        self.net, self.p, self.bufs, self.cols = net, p, bufs, cols
        self.h, self.q = rows // 2, rows // 4
        self.sent = [net.sem(), net.sem()]
        self.came = [net.sem() for _ in range(4)]
        whole = pl.ds(0, rows)
        self.totals = [p.at[0:3, :, whole, cols], p.at[0, 0:3, whole, cols]]

    def rows(self, o, part):
        base = o * self.h
        if part == 1:
            return pl.ds(base, self.q)
        if part == 2:
            return pl.ds(base + self.q, self.q)
        return pl.ds(base, self.h)

    def place(self, o):
        return (self.net.x, self.net.z) if o == 0 else (self.net.z, self.net.x)

    def bundle(self, o, a, part):
        r = self.rows(o, part)
        return self.p.at[a, :, r, self.cols] if o == 0 else self.p.at[:, a, r, self.cols]

    def block(self, o, a, i, part):
        r = self.rows(o, part)
        return self.p.at[a, i, r, self.cols] if o == 0 else self.p.at[i, a, r, self.cols]

    def half(self, side):
        return pl.ds(side * self.q, self.q)

    def push(self, n, src, dst, axis, d):
        self.net.send(src, dst, self.net.along(axis, d), self.sent[n // 2], self.came[n])

    def start(self):
        r1, r2 = self.bufs[0], self.bufs[1]
        for o in (0, 1):
            me, _ = self.place(o)
            for side, d in ((0, 1), (1, -1)):
                self.push(0, self.bundle(o, (me + 2) % 4, 1 + side), r1.at[o, side], o, d)
        for o in (0, 1):
            me, _ = self.place(o)
            for side, d in ((0, 1), (1, -1)):
                self.push(1, self.bundle(o, (me + d) % 4, 2 - side), r2.at[o, side, :, self.half(1 - side)], o, d)

    def step2(self):
        r1, r2 = self.bufs[0], self.bufs[1]
        self.net.wait_came(r1, self.came[0])
        for o in (0, 1):
            me, _ = self.place(o)
            for side, d in ((0, 1), (1, -1)):
                a, part = (me + d) % 4, 1 + side

                def add(i, _, o=o, a=a, part=part, side=side):
                    b = self.block(o, a, i, part)
                    b[...] = (b[...].astype(F32) + r1[o, side, i].astype(F32)).astype(BF16)
                    return 0

                lax.fori_loop(0, 4, add, 0)
                self.push(1, self.bundle(o, a, part), r2.at[o, side, :, self.half(side)], o, d)

    def step3(self):
        r2, r3, r4 = self.bufs[1], self.bufs[2], self.bufs[3]
        self.net.wait_came(r2, self.came[1])
        for o in (0, 1):
            me, other = self.place(o)

            def add(i, o=o, me=me):
                b = self.block(o, me, i, 0)
                total = b[...].astype(F32) + r2[o, 0, i].astype(F32) + r2[o, 1, i].astype(F32)
                b[...] = total.astype(BF16)

            def far(n, _, add=add, other=other):
                add((other + 2 + n) % 4)
                return 0

            add((other + 2) % 4)
            for side, d in ((0, 1), (1, -1)):
                self.push(2, self.block(o, me, (other + 2) % 4, 1 + side), r3.at[o, side], 1 - o, d)
            lax.fori_loop(1, 4, far, 0)
            for side, d in ((0, 1), (1, -1)):
                self.push(3, self.block(o, me, (other + d) % 4, 2 - side), r4.at[o, side, self.half(1 - side)], 1 - o, d)

    def step4(self):
        r3, r4 = self.bufs[2], self.bufs[3]
        self.net.wait_came(r3, self.came[2])
        for o in (0, 1):
            me, other = self.place(o)
            for side, d in ((0, 1), (1, -1)):
                b = self.block(o, me, (other + d) % 4, 1 + side)
                b[...] = (b[...].astype(F32) + r3[o, side].astype(F32)).astype(BF16)
                self.push(3, b, r4.at[o, side, self.half(side)], 1 - o, d)

    def finish(self, store):
        r4 = self.bufs[3]
        self.net.wait_came(r4, self.came[3])
        for o in (0, 1):
            me, other = self.place(o)
            total = self.block(o, me, other, 0)[...].astype(F32) + r4[o, 0].astype(F32) + r4[o, 1].astype(F32)
            store(self.rows(o, 0), total)

    def drain(self):
        for ref, sem in zip(self.totals, self.sent):
            self.net.wait_sent(ref, sem)


def scatter_bufs(rows, cols):
    h, q = rows // 2, rows // 4
    return [
        pltpu.VMEM((2, 2, 4, q, cols), BF16),
        pltpu.VMEM((2, 2, 4, h, cols), BF16),
        pltpu.VMEM((2, 2, q, cols), BF16),
        pltpu.VMEM((2, 2, h, cols), BF16),
    ]


class ReduceY:
    def __init__(self, net, part, cr, yr):
        self.net, self.part, self.cr, self.yr = net, part, cr, yr
        self.sent, self.core, self.far = [net.sem(), net.sem()], [net.sem(), net.sem()], [net.sem(), net.sem()]

    def start(self, n):
        net, rows = self.net, half_rows(n)
        net.send(self.part.at[:, 1 - net.c, rows], self.cr.at[:, rows], net.at(dc=1), self.sent[0], self.core[n])

    def step(self, n):
        net, rows = self.net, half_rows(n)
        net.wait_came(self.cr.at[:, rows], self.core[n])
        for d in (2, 1, 3):
            to = (net.y + d) % 4
            own = self.part.at[to, net.c, rows]
            own[...] = (own[...].astype(F32) + self.cr[to, rows].astype(F32)).astype(BF16)
            net.send(own, self.yr.at[d - 1, rows], net.at(dy=d), self.sent[1], self.far[n])

    def finish(self, n):
        net, rows, yr = self.net, half_rows(n), self.yr
        total = self.part[net.y, net.c, rows].astype(F32) + self.cr[net.y, rows].astype(F32)
        net.wait_came(yr.at[:, rows], self.far[n])
        return total + yr[0, rows].astype(F32) + yr[1, rows].astype(F32) + yr[2, rows].astype(F32)

    def drain(self):
        self.net.wait_sent(self.cr, self.sent[0])
        self.net.wait_sent(self.yr, self.sent[1])


class GatherY:
    def __init__(self, net, g):
        self.net, self.g = net, g
        self.sent, self.near, self.far = [net.sem(), net.sem()], net.sem(), [[net.sem() for _ in range(3)] for _ in range(2)]

    def put(self, n, rows):
        net = self.net
        own = self.g.at[net.y, net.c, half_rows(n)]
        own[...] = rows.astype(BF16)
        for d in (2, 1, 3):
            net.send(own, own, net.at(dy=d), self.sent[0], self.far[n][d - 1])
        net.send(own, own, net.at(dc=1), self.sent[1], self.near)

    def step(self, n):
        net = self.net
        for d in (1, 3, 2):
            came = self.g.at[(net.y + 4 - d) % 4, net.c, half_rows(n)]
            net.wait_came(came, self.far[n][d - 1])
            net.send(came, came, net.at(dc=1), self.sent[1], self.near)

    def finish(self):
        self.net.wait_came(self.g.at[:, 1 - self.net.c], self.near)

    def drain(self):
        self.net.wait_sent(self.g.at[0:3, 0], self.sent[0])
        self.net.wait_sent(self.g.at[:, 0], self.sent[1])


def kernel(*refs):
    it = iter(refs)

    def take(n):
        return [next(it) for _ in range(n)]

    x_in, cot_in, seg, gain_a, gain_b, wq_in, wg_in, wk_in, wv_in, wo_in, mg_in, mu_in, md_in = take(13)
    bo_out, ig_out, gain1_out, qg_out, gg_out, kg_out, vg_out, og_out, gain2_out, mg_out, mu_out, md_out = take(12)
    wq, wg, wkv, wo, wm, wd, kv, kvg, pd0, pd1 = take(10)
    xb, xn, xnt, g, hnb, hnt, dcb, igb, bo = take(9)
    part_a, part_b = take(2)
    yb = [take(2) for _ in range(4)]
    r1c, gp, ob, ot, qt, dot_, dqt, dmb, ab, dadu, mt = take(11)
    h32, z32, r32, dh32 = take(4)
    gx0, gxr, gx1, gzr, gy, gc = take(6)
    mg_f, mu_f, md_f, og_f, qg_f, gg_f, kg_f, vg_f, gn_f = take(9)
    sb = [take(4) for _ in range(10)]
    sems, local = take(2)

    net = Net(sems)
    s, x, z, y, c = net.s, net.x, net.z, net.y, net.c
    moved = []

    def move(src, dst):
        d = pltpu.make_async_copy(src, dst, local.at[len(moved)])
        d.start()
        moved.append(d)
        return d

    load_kv = [move(wk_in, wkv.at[x, z, pl.ds(0, 128), pl.ds(0, 128)]), move(wv_in, wkv.at[x, z, pl.ds(0, 128), pl.ds(128, 128)])]
    load_q = move(wq_in, wq.at[x, z])
    load_g = move(wg_in, wg.at[x, z])
    load_o = move(wo_in, wo.at[x, z])
    load_x = move(x_in, xb)
    load_d = move(md_in, wd.at[x, z])
    load_m = [move(mg_in, wm.at[x, z, :, pl.ds(0, 768)]), move(mu_in, wm.at[x, z, :, pl.ds(768, 768)])]
    load_c = move(cot_in, g)
    line = lax.broadcasted_iota(jnp.int32, (16, 128), 0)
    tile = jnp.where(line == 0, gain_a[...].astype(F32), jnp.where(line == 1, gain_b[...].astype(F32), 0.0))
    wkv[x, z, 128:144, :] = jnp.concatenate([tile, tile], axis=1).astype(BF16)
    net.barrier()

    ag_kvw = Gather(net, wkv, (32, 64, 112, 144))
    ag_q = Gather(net, wq, (32, 64, 96, 128))
    ag_g = Gather(net, wg, (32, 64, 96, 128))
    ag_o = Gather(net, wo, (64, 128, 192, 256))
    ag_kv = Gather(net, kv, (64, 128, 192, 256))
    ag_d = Gather(net, wd, (192, 384, 576, 768))
    ag_mg = Gather(net, wm, (32, 64, 96, 128), pl.ds(0, 768))
    ag_mu = [Gather(net, wm, (32, 64, 96, 128), pl.ds(768 + 384 * n, 384)) for n in (0, 1)]
    for d in load_kv:
        d.wait()
    ag_kvw.start()
    load_q.wait()
    ag_q.start()
    load_g.wait()
    ag_g.start()
    load_o.wait()
    ag_o.start()
    load_d.wait()
    ag_d.start()

    load_x.wait()

    def scales(i, _):
        rows = pl.ds(pl.multiple_of(i * 32, 32), 32)
        v = xb[rows, :].astype(F32)
        scale = lax.rsqrt(jnp.mean(v * v, axis=-1, keepdims=True) + EPS)
        r1c[rows, :] = jnp.broadcast_to(scale, (32, 128))
        return 0

    lax.fori_loop(0, 8, scales, 0)
    ids = seg[...].astype(F32)

    def below(v):
        return jnp.sum(jnp.where(ids < v, 1.0, 0.0), axis=(0, 1), keepdims=True)

    own_ids = jnp.concatenate([seg[pl.ds(2 * s, 1), :], seg[pl.ds(2 * s + 1, 1), :]], axis=1).astype(F32)
    first_key = jnp.where(own_ids > 2.5, below(2.5), jnp.where(own_ids > 1.5, below(1.5), jnp.where(own_ids > 0.5, below(0.5), 0.0)))
    first_key = jnp.concatenate([first_key, first_key], axis=1).astype(jnp.int32)
    query_place = s * 256 + lax.broadcasted_iota(jnp.int32, (1, 256), 1)
    query_place = jnp.concatenate([query_place, query_place], axis=1)
    top = jnp.max(ids, axis=(0, 1), keepdims=True)
    kept = below(top)

    ag_kvw.step(1)
    ag_q.step(1)
    load_c.wait()

    def mask_cot(i, _):
        rows = pl.ds(pl.multiple_of(i * 32, 32), 32)
        place = (s * 256 + i * 32 + lax.broadcasted_iota(jnp.int32, (32, 1), 0)).astype(F32)
        g[rows, :] = jnp.where(place < kept, g[rows, :].astype(F32), 0.0).astype(BF16)
        return 0

    lax.fori_loop(0, 8, mask_cot, 0)
    pairs = (s + 2) // 2

    def clear(j, _):
        kvg[j // 4, j % 4] = jnp.zeros((256, 256), BF16)
        return 0

    lax.fori_loop(2 * pairs, 16, clear, 0)
    ag_kvw.step(2)
    ag_q.step(2)
    ag_g.step(1)
    ag_o.step(1)
    ag_d.step(1)
    ag_kvw.step(3)
    ag_q.step(3)
    ag_g.step(2)
    ag_kvw.finish()

    def gain_row(n):
        return jnp.concatenate([wkv[j // 4, j % 4, 128:144, 0:128].astype(F32)[n : n + 1, :] for j in range(16)], axis=1)

    gain1 = gain_row(0)
    gain2 = gain_row(1)

    def norm_in(i, _):
        rows = pl.ds(pl.multiple_of(i * 32, 32), 32)
        v = xb[rows, :].astype(F32) * r1c[rows, 0:1]
        xn[rows, :] = (v * gain1).astype(BF16)
        return 0

    lax.fori_loop(0, 8, norm_in, 0)
    kv[x, z] = nn(xn[...], wkv[:, :, 0:128, :].reshape(2048, 256)).astype(BF16)
    ag_kv.start()
    for d in load_m:
        d.wait()
    ag_mg.start()
    ag_q.finish()
    q = nn(xn[...], wq[...].reshape(2048, 256)).astype(BF16)
    qt[...] = jnp.concatenate([q[:, :128].T, q[:, 128:].T], axis=1)
    ag_kv.step(1)
    ag_o.step(2)
    ag_kv.step(2)
    ag_mg.step(1)
    for a in ag_mu:
        a.start()
    for j in range(8):
        xnt[256 * j : 256 * j + 256, :] = xn[:, 256 * j : 256 * j + 256].T
    ag_kv.step(3)
    ag_g.step(3)
    ag_o.step(3)
    for a in ag_mu:
        a.step(1)
    ag_d.step(2)
    ag_mg.step(2)
    ag_kv.finish()

    ot[...] = jnp.zeros_like(ot)
    key_line = lax.broadcasted_iota(jnp.int32, (512, 512), 0)

    def scores(i):
        both = kv[i // 2, pl.ds(2 * (i % 2), 2)].reshape(512, 256)
        keys, values = both[:, 0:128], both[:, 128:256]
        place = i * 512 + key_line
        allowed = (place >= first_key) & (place <= query_place)
        return keys, values, jnp.where(allowed, nn(keys, qt[...]) * (SCALE * LOG2E), MASKED)

    def attend(i, state):
        top, total = state
        _, values, st = scores(i)
        new_top = jnp.maximum(top, jnp.max(st, axis=0, keepdims=True))
        probs = jnp.exp2(st - new_top)
        shrink = jnp.exp2(top - new_top)
        ot[...] = ot[...] * shrink + nn(values.T, probs.astype(BF16))
        return new_top, total * shrink + jnp.sum(probs, axis=0, keepdims=True)

    state = (jnp.full((1, 512), FLOOR, F32), jnp.zeros((1, 512), F32))
    top, total = lax.fori_loop(0, pairs, attend, state)
    lse = top + jnp.log(total) * LOG2E
    ot[...] = ot[...] / total
    o = jnp.concatenate([ot[:, 0:256].T, ot[:, 256:512].T], axis=1)
    ob[...] = o
    ag_g.finish()
    gp[...] = nn(xn[...], wg[...].reshape(2048, 256))
    yv = (o * jax.nn.sigmoid(gp[...])).astype(BF16)
    ag_o.finish()
    red = ReduceY(net, part_a, *yb[0])
    for j in range(8):
        w2 = jnp.concatenate([wo[j // 2, 2 * (j % 2) + i] for i in (0, 1)], axis=1)
        part_a[:, :, :, 256 * j : 256 * j + 256] = nn(yv, w2).astype(BF16).reshape(4, 2, 32, 256)
    for n in (0, 1):
        red.start(n)
    ag_d.step(3)
    for n in (0, 1):
        red.step(n)
    ag_mg.step(3)
    for a in ag_mu:
        a.step(2)
    yt = yv.T
    own_rows = [pl.ds(pl.multiple_of(net.k * ROWS + 16 * n, 16), 16) for n in (0, 1)]
    gat = GatherY(net, hnb)
    for n in (0, 1):
        h = xb[own_rows[n], :].astype(F32) + red.finish(n)
        h32[half_rows(n), :] = h
        scale2 = lax.rsqrt(jnp.mean(h * h, axis=-1, keepdims=True) + EPS)
        z2 = h * scale2
        z32[half_rows(n), :] = z2
        r32[half_rows(n), :] = jnp.broadcast_to(scale2, (16, 128))
        gat.put(n, z2 * gain2)
    ag_d.finish()

    for n in range(3):
        w2 = jnp.concatenate([wd[j // 4, j % 4, 256 * n : 256 * n + 256, :] for j in range(16)], axis=1)
        dmb[:, 256 * n : 256 * n + 256] = nt(g[...], w2)
    for n in (0, 1):
        gat.step(n)
    gat.finish()
    hn = hnb[...].reshape(256, 2048)
    for j in range(8):
        hnt[256 * j : 256 * j + 256, :] = hnb[:, :, :, 256 * j : 256 * j + 256].reshape(256, 256).T
    ag_mu[0].step(3)
    ag_mg.finish()
    for n in range(3):
        ab[:, 256 * n : 256 * n + 256] = nn(hn, wm[:, :, :, 256 * n : 256 * n + 256].reshape(2048, 256))
    ag_mu[1].step(3)
    for a in (ag_kvw, ag_q, ag_g, ag_o, red):
        a.drain()
    pds = (pd0, pd1)
    rs_d = [Scatter(net, pds[n], 384, sb[n]) for n in (0, 1)]

    def down_grad(n):
        for j in range(8):
            pd = nn(mt[384 * n : 384 * n + 384, :], g[:, 256 * j : 256 * j + 256])
            for i in (0, 1):
                pds[n][j // 2, 2 * (j % 2) + i] = pd[:, 128 * i : 128 * i + 128].astype(BF16)
        rs_d[n].start()

    for n in (0, 1):
        cols = slice(384 * n, 384 * n + 384)
        up_cols = slice(768 + 384 * n, 1152 + 384 * n)
        ag_mu[n].finish()
        a = ab[:, cols]
        u = nn(hn, wm[:, :, :, up_cols].reshape(2048, 384))
        sig = jax.nn.sigmoid(a)
        silu = a * sig
        mt[cols, :] = (silu * u).astype(BF16).T
        dm = dmb[:, cols]
        dadu[:, cols] = (dm * u * sig * (1.0 + a * (1.0 - sig))).astype(BF16)
        dadu[:, up_cols] = (dm * silu).astype(BF16)
        if n == 0:
            down_grad(0)
    red3 = ReduceY(net, part_a, *yb[1])
    for j in range(8):
        w2 = wm[j // 2, 2 * (j % 2) : 2 * (j % 2) + 2].reshape(256, 1536)
        part_a[:, :, :, 256 * j : 256 * j + 256] = nt(dadu[...], w2).astype(BF16).reshape(4, 2, 32, 256)
    for n in (0, 1):
        red3.start(n)
    down_grad(1)
    for a in (ag_d, ag_mg, *ag_mu):
        a.drain()
    rs_m = [Scatter(net, wm, 128, sb[2 + n], pl.ds(768 * n, 768)) for n in (0, 1)]
    for n in (0, 1):
        for j in range(8):
            pm = nn(hnt[256 * j : 256 * j + 256, :], dadu[:, 768 * n : 768 * n + 768])
            wm[j // 2, 2 * (j % 2) : 2 * (j % 2) + 2, :, 768 * n : 768 * n + 768] = pm.astype(BF16).reshape(2, 128, 768)
        rs_m[n].start()
        if n == 0:
            red3.step(0)
            red3.step(1)
    mm = mt[...].T
    for j in range(8):
        w2 = jnp.concatenate([wd[j // 2, 2 * (j % 2) + i] for i in (0, 1)], axis=1)
        part_b[:, :, :, 256 * j : 256 * j + 256] = nn(mm, w2).astype(BF16).reshape(4, 2, 32, 256)
    grads_gain2 = jnp.zeros((1, 2048), F32)
    gat3 = GatherY(net, dcb)
    for n in (0, 1):
        dhn = red3.finish(n)
        z2 = z32[half_rows(n), :]
        e2 = dhn * gain2
        grads_gain2 += jnp.sum(dhn * z2, axis=0, keepdims=True)
        dh = g[own_rows[n], :].astype(F32) + r32[half_rows(n), 0:1] * (e2 - z2 * jnp.mean(e2 * z2, axis=-1, keepdims=True))
        dh32[half_rows(n), :] = dh
        gat3.put(n, dh)
    red2 = ReduceY(net, part_b, *yb[2])
    for n in (0, 1):
        red2.start(n)
    rs_d[0].step2()
    for n in (0, 1):
        gat3.step(n)
    for n in (0, 1):
        red2.step(n)
    gat3.finish()
    dc = dcb[...].reshape(256, 2048)
    w2 = jnp.concatenate([wo[j // 4, j % 4] for j in range(16)], axis=1)
    dy = nt(dc, w2)
    sig = jax.nn.sigmoid(gp[...])
    do = (dy * sig).astype(BF16)
    dg = (dy * ob[...] * sig * (1.0 - sig)).astype(BF16)
    dot_[...] = jnp.concatenate([do[:, :128].T, do[:, 128:].T], axis=1)
    q_rows = jnp.concatenate([qt[:, 0:256].T, qt[:, 256:512].T], axis=0)
    do_rows = jnp.concatenate([do[:, :128], do[:, 128:]], axis=0)
    w = jnp.sum(dot_[...].astype(F32) * ot[...], axis=0, keepdims=True)
    dqt[...] = jnp.zeros_like(dqt)
    rs_d[1].step2()

    def attend_back(i, _):
        keys, values, st = scores(i)
        probs = jnp.exp2(st - lse)
        dp = nn(values, dot_[...])
        ds = (probs * (dp - w) * SCALE).astype(BF16)
        dk = nn(ds, q_rows).astype(BF16)
        dv = nn(probs.astype(BF16), do_rows).astype(BF16)
        kvg[i // 2, pl.ds(2 * (i % 2), 2)] = jnp.concatenate([dk, dv], axis=1).reshape(2, 256, 256)
        dqt[...] += nn(keys.T, ds)
        return 0

    lax.fori_loop(0, pairs, attend_back, 0)
    rs_kv = [Scatter(net, kvg, 256, sb[4 + 5 * n], pl.ds(128 * n, 128)) for n in (0, 1)]
    for a in rs_kv:
        a.start()
    for j in range(8):
        po = nn(yt, dcb[:, :, :, 256 * j : 256 * j + 256].reshape(256, 256))
        for i in (0, 1):
            wo[j // 2, 2 * (j % 2) + i] = po[:, 128 * i : 128 * i + 128].astype(BF16)
    for a in rs_kv:
        a.step2()
    rs_m[0].step2()
    dq = jnp.concatenate([dqt[:, 0:256].T, dqt[:, 256:512].T], axis=1).astype(BF16)
    for j in range(8):
        pair = (j // 2, slice(2 * (j % 2), 2 * (j % 2) + 2))
        xnt_j = xnt[256 * j : 256 * j + 256, :]
        xn[:, 256 * j : 256 * j + 256] = (nt(dq, wq[pair].reshape(256, 256)) + nt(dg, wg[pair].reshape(256, 256))).astype(BF16)
        wq[pair] = nn(xnt_j, dq).astype(BF16).reshape(2, 128, 256)
        wg[pair] = nn(xnt_j, dg).astype(BF16).reshape(2, 128, 256)
    rs_g = Scatter(net, wg, 128, sb[6])
    rs_g.start()
    for a in rs_kv:
        a.step3()
    rs_o = Scatter(net, wo, 256, sb[5])
    rs_o.start()
    rs_d[0].step3()
    for a in rs_kv:
        a.step4()
    rs_q = Scatter(net, wq, 128, sb[7])
    rs_q.start()
    rs_m[1].step2()
    rs_d[1].step3()
    gat2 = GatherY(net, bo)
    for n in (0, 1):
        gat2.put(n, h32[half_rows(n), :] + red2.finish(n))
    for a in (ag_kv, red3):
        a.drain()

    for n in (0, 1):

        def store_kv(rows, v, n=n):
            kv[0, 0, rows, 128 * n : 128 * n + 128] = v.astype(BF16)

        rs_kv[n].finish(store_kv)
    dkdv = kv[0, 0]
    red4 = ReduceY(net, part_a, *yb[3])
    for j in range(8):
        w2 = wkv[j // 2, 2 * (j % 2) : 2 * (j % 2) + 2, 0:128, :].reshape(256, 256)
        px = nt(dkdv, w2) + xn[:, 256 * j : 256 * j + 256].astype(F32)
        part_a[:, :, :, 256 * j : 256 * j + 256] = px.astype(BF16).reshape(4, 2, 32, 256)
    for n in (0, 1):
        red4.start(n)
    line8 = lax.broadcasted_iota(jnp.int32, (8, 128), 0)
    for j in range(8):
        cols = slice(256 * j, 256 * j + 256)
        pk = nn(xnt[cols, :], dkdv)
        wkv[j // 2, 2 * (j % 2) : 2 * (j % 2) + 2, 0:128, :] = pk.astype(BF16).reshape(2, 128, 256)
        z1 = xb[:, cols].astype(F32) * r1c[:, 0:1]
        gain1_part = jnp.sum(part_a[:, :, :, cols].reshape(256, 256).astype(F32) * z1, axis=0, keepdims=True)
        for i in (0, 1):
            own = slice(128 * i, 128 * i + 128)
            both = jnp.where(line8 == 1, grads_gain2[:, 256 * j + 128 * i : 256 * j + 128 * i + 128], 0.0)
            gx0[j // 2, 2 * (j % 2) + i] = jnp.where(line8 == 0, gain1_part[:, own], both)
    rs_kvw = Scatter(net, wkv, 128, sb[8])
    rs_kvw.start()
    for n in (0, 1):
        red4.step(n)
    sx, sz, sy, sc = ([net.sem(), net.sem()] for _ in range(4))
    for d in (1, 2, 3):
        net.send(gx0.at[(x + d) % 4], gxr.at[d - 1], net.at(dx=d), *sx)
    rs_m[0].step3()
    rs_o.step2()
    rs_g.step2()
    rs_q.step2()
    rs_kvw.step2()
    rs_m[1].step3()
    for a in rs_d:
        a.step4()
    net.wait_came(gxr, sx[1])
    gx1[...] = gx0[x] + gxr[0] + gxr[1] + gxr[2]
    for d in (1, 2, 3):
        net.send(gx1.at[(z + d) % 4], gzr.at[d - 1], net.at(dz=d), *sz)
    gat4 = GatherY(net, igb)
    for n in (0, 1):
        dxn = red4.finish(n)
        scale1 = r1c[own_rows[n], 0:1]
        z1 = xb[own_rows[n], :].astype(F32) * scale1
        e1 = dxn * gain1
        gat4.put(n, dh32[half_rows(n), :] + scale1 * (e1 - z1 * jnp.mean(e1 * z1, axis=-1, keepdims=True)))
    rs_o.step3()
    rs_g.step3()
    rs_q.step3()
    rs_kvw.step3()
    for a in rs_m:
        a.step4()

    def keep(ref, base=0):
        def store(rows, v):
            ref[pl.ds(rows.start + base, rows.size), :] = v

        return store

    for n in (0, 1):
        gat2.step(n)
    for n in (0, 1):
        rs_d[n].finish(keep(md_f, 384 * n))
    move(md_f, md_out)
    rs_o.step4()
    rs_g.step4()
    rs_q.step4()
    rs_kvw.step4()
    net.wait_came(gzr, sz[1])
    gy[y] = gx1[z] + gzr[0] + gzr[1] + gzr[2]
    for d in (1, 2, 3):
        net.send(gy.at[y], gy.at[y], net.at(dy=d), *sy)
    for n in (0, 1):
        gat4.step(n)
    rs_m[0].finish(keep(mg_f))
    move(mg_f, mg_out)
    rs_m[1].finish(keep(mu_f))
    move(mu_f, mu_out)
    gat2.finish()
    move(bo, bo_out)
    net.wait_came(gy.at[0:3], sy[1])
    gc[c] = gy[0] + gy[1] + gy[2] + gy[3]
    net.send(gc.at[c], gc.at[c], net.at(dc=1), *sc)
    rs_o.finish(keep(og_f))
    move(og_f, og_out)
    rs_g.finish(keep(gg_f))
    move(gg_f, gg_out)
    rs_q.finish(keep(qg_f))
    move(qg_f, qg_out)
    gat4.finish()
    move(igb, ig_out)

    def store_kvw(rows, v):
        kg_f[rows, :] = v[:, :128]
        vg_f[rows, :] = v[:, 128:]

    rs_kvw.finish(store_kvw)
    move(kg_f, kg_out)
    move(vg_f, vg_out)
    net.wait_came(gc.at[0], sc[1])
    gn_f[...] = gc[0] + gc[1]
    move(gn_f.at[pl.ds(0, 1)], gain1_out)
    move(gn_f.at[pl.ds(1, 1)], gain2_out)
    for a in (*rs_m, *rs_d, *rs_kv, rs_g, rs_q, rs_o, rs_kvw, red2, red4, gat, gat2, gat3, gat4):
        a.drain()
    net.wait_sent(gxr, sx[0])
    net.wait_sent(gzr, sz[0])
    net.wait_sent(gy.at[0:3], sy[0])
    net.wait_sent(gc.at[0], sc[0])
    for d in moved[10:]:
        d.wait()


def place_outputs(*refs):
    ins, outs, bufs, (wide, sems) = refs[:12], refs[12:24], refs[24:36], refs[36:]
    spans = [pl.ds(64 * i, 64) for i in range(4)]
    loads = [pltpu.make_async_copy(ins[1].at[r], bufs[1].at[r], sems.at[i]) for i, r in enumerate(spans)]
    order = [0, 9, 10, 11, 3, 4, 5, 6, 7, 2, 8]
    rest = [pltpu.make_async_copy(ins[i], bufs[i], sems.at[4 + i]) for i in order]
    for d in loads + rest:
        d.start()
    copies = []

    def out(src, dst, n):
        d = pltpu.make_async_copy(src, dst, sems.at[n])
        d.start()
        copies.append(d)

    for i, r in enumerate(spans):
        loads[i].wait()
        wide[r, :] = bufs[1][r, :].astype(F32)
        out(wide.at[r], outs[1].at[r], 16 + i)
    for i, d in zip(order, rest):
        d.wait()
        out(bufs[i], outs[i], 20 + i)
    for d in copies:
        d.wait()


def per_device(inputs, cotangent, segment_ids, attn_gain, query_weight, gate_weight, key_weight, value_weight, output_weight, mlp_gain, mlp_gate, mlp_up, mlp_down):
    v = pltpu.VMEM
    y_rows = (4, 2, ROWS, 2048)
    scratch = [
        v((4, 4, 128, 256), BF16),
        v((4, 4, 128, 256), BF16),
        v((4, 4, 144, 256), BF16),
        v((4, 4, 256, 128), BF16),
        v((4, 4, 128, 1536), BF16),
        v((4, 4, 768, 128), BF16),
        v((4, 4, 256, 256), BF16),
        v((4, 4, 256, 256), BF16),
        v((4, 4, 384, 128), BF16),
        v((4, 4, 384, 128), BF16),
        v((256, 2048), BF16),
        v((256, 2048), BF16),
        v((2048, 256), BF16),
        v((256, 2048), BF16),
        v(y_rows, BF16),
        v((2048, 256), BF16),
        v(y_rows, BF16),
        v(y_rows, BF16),
        v(y_rows, BF16),
        v(y_rows, BF16),
        v(y_rows, BF16),
    ]
    for _ in range(4):
        scratch += [v((4, ROWS, 2048), BF16), v((3, ROWS, 2048), BF16)]
    scratch += [
        v((256, 128), F32),
        v((256, 256), F32),
        v((256, 256), F32),
        v((128, 512), F32),
        v((128, 512), BF16),
        v((128, 512), BF16),
        v((128, 512), F32),
        v((256, 768), F32),
        v((256, 768), F32),
        v((256, 1536), BF16),
        v((768, 256), BF16),
        v((ROWS, 2048), F32),
        v((ROWS, 2048), F32),
        v((ROWS, 128), F32),
        v((ROWS, 2048), F32),
        v((4, 4, 8, 128), F32),
        v((3, 4, 8, 128), F32),
        v((4, 8, 128), F32),
        v((3, 8, 128), F32),
        v((4, 8, 128), F32),
        v((2, 8, 128), F32),
    ]
    grad_shapes = ((128, 768), (128, 768), (768, 128), (256, 128), (128, 256), (128, 256), (128, 128), (128, 128), (8, 128))
    scratch += [v(dims, F32) for dims in grad_shapes]
    for rows, cols in ((384, 128), (384, 128), (128, 768), (128, 768), (256, 128), (256, 128), (128, 256), (128, 256), (128, 256), (256, 128)):
        scratch += scatter_bufs(rows, cols)
    scratch += [pltpu.SemaphoreType.DMA((188,)), pltpu.SemaphoreType.DMA((24,))]
    whole = pl.BlockSpec(memory_space=pltpu.VMEM)
    there = pl.BlockSpec(memory_space=pl.ANY)
    shape = jax.ShapeDtypeStruct
    out_shape = (
        shape((256, 2048), BF16),
        shape((256, 2048), F32),
        shape((1, 128), F32),
        shape((128, 256), F32),
        shape((128, 256), F32),
        shape((128, 128), F32),
        shape((128, 128), F32),
        shape((256, 128), F32),
        shape((1, 128), F32),
        shape((128, 768), F32),
        shape((128, 768), F32),
        shape((768, 128), F32),
    )
    outs = pl.pallas_call(
        kernel,
        out_shape=(shape(y_rows, BF16), shape(y_rows, BF16)) + out_shape[2:],
        in_specs=[there, there, whole, whole, whole] + [there] * 8,
        out_specs=[there] * 12,
        scratch_shapes=scratch,
        compiler_params=pltpu.CompilerParams(collective_id=0, has_side_effects=True, vmem_limit_bytes=63 << 20),
    )(
        inputs,
        cotangent,
        segment_ids.reshape(32, 128),
        attn_gain.reshape(1, 128),
        mlp_gain.reshape(1, 128),
        query_weight,
        gate_weight,
        key_weight,
        value_weight,
        output_weight,
        mlp_gate,
        mlp_up,
        mlp_down,
    )
    outs = pl.pallas_call(
        place_outputs,
        out_shape=out_shape,
        in_specs=[there] * 12,
        out_specs=[there] * 12,
        scratch_shapes=[v(o.shape, BF16 if i == 1 else o.dtype) for i, o in enumerate(out_shape)] + [v((256, 2048), F32), pltpu.SemaphoreType.DMA((32,))],
        compiler_params=pltpu.CompilerParams(vmem_limit_bytes=60 << 20),
    )(outs[0].reshape(256, 2048), outs[1].reshape(256, 2048), *outs[2:])
    outs = list(outs)
    outs[2] = outs[2].reshape(128)
    outs[8] = outs[8].reshape(128)
    return tuple(outs)


def solution(mesh):
    weights = (P("seq"), P("seq", "kv"), P("seq", "kv"), P("seq", "kv"), P("seq", "kv"), P("kv", "seq"))
    weights += (P("seq"), P("seq", "kv"), P("seq", "kv"), P("kv", "seq"))
    return jax.shard_map(
        per_device,
        mesh=mesh,
        in_specs=(P("seq", None), P("seq", None), P()) + weights,
        out_specs=(P("seq", None), P("seq", None)) + weights,
        check_vma=False,
    )
```

```python
import functools

import jax
import jax.numpy as jnp
from jax import lax
from jax.experimental import pallas as pl
from jax.experimental.pallas import tpu as pltpu
from jax.sharding import PartitionSpec as P

F32 = jnp.float32
BF16 = jnp.bfloat16
MESH = pl.DeviceIdType.MESH
EPS = 1e-06
HEAD = 128
SCALE = HEAD**-0.5
LOG2E = 1.4426950408889634
MASKED = -1e30
FLOOR = -1e29
ROWS = 32


def nn(left, right):
    return jnp.dot(left, right, preferred_element_type=F32)


def nt(left, right):
    return lax.dot_general(left, right, (((1,), (1,)), ((), ())), preferred_element_type=F32)


def half_rows(n):
    return pl.ds(16 * n, 16)


class Net:
    def __init__(self, sems):
        s, k = lax.axis_index("seq"), lax.axis_index("kv")
        self.s, self.k = s, k
        self.x, self.z, self.y, self.c = s // 4, s % 4, k // 2, k % 2
        self.sems, self.used = sems, 0

    def at(self, dx=0, dz=0, dy=0, dc=0):
        return {
            "kv": ((self.y + dy) % 4) * 2 + (self.c + dc) % 2,
            "seq": ((self.x + dx) % 4) * 4 + (self.z + dz) % 4,
        }

    def along(self, axis, d):
        return self.at(dx=d) if axis == 0 else self.at(dz=d)

    def sem(self):
        self.used += 1
        return self.sems.at[self.used - 1]

    def copy(self, src, dst, to, sent, came):
        return pltpu.make_async_remote_copy(
            src_ref=src,
            dst_ref=dst,
            send_sem=sent,
            recv_sem=came,
            device_id=to,
            device_id_type=MESH,
        )

    def send(self, src, dst, to, sent, came):
        self.copy(src, dst, to, sent, came).start()

    def wait_sent(self, ref, sem):
        self.copy(ref, ref, self.at(dc=1), sem, sem).wait_send()

    def wait_came(self, ref, sem):
        self.copy(ref, ref, self.at(dc=1), sem, sem).wait_recv()

    def barrier(self):
        sem = pltpu.get_barrier_semaphore()
        near = [self.at(dx=d) for d in (1, 2, 3)] + [self.at(dz=d) for d in (1, 2, 3)]
        near += [self.at(dy=d) for d in (1, 2, 3)] + [self.at(dc=1)]
        for to in near:
            pl.semaphore_signal(sem, inc=1, device_id=to, device_id_type=MESH)
        pl.semaphore_wait(sem, len(near))


class Gather:
    def __init__(self, net, w, cuts, cols=slice(None)):
        self.net, self.w, self.cols = net, w, cols
        q, h, q2, r = cuts
        self.spans = ((0, q, h), (h, q2, r))
        self.sent = [net.sem() for _ in range(2)]
        self.came = [net.sem() for _ in range(4)]
        rows = pl.ds(0, r)
        self.sizes = [w.at[0, 0:2, rows, cols], w.at[0, 0, rows, cols], w.at[0:2, :, rows, cols], w.at[0, :, rows, cols]]
        self.totals = [w.at[0, 0:3, rows, cols], w.at[0:3, :, rows, cols]]

    def part(self, o, n):
        r0, r1, r2 = self.spans[o]
        return (pl.ds(r0, r2 - r0), pl.ds(r0, r1 - r0), pl.ds(r1, r2 - r1))[n]

    def single(self, o, a, n):
        x, z = (a, self.net.z) if o == 0 else (self.net.x, a)
        return self.w.at[x, z, self.part(o, n), self.cols]

    def bundle(self, o, b, n):
        rows = self.part(o, n)
        return self.w.at[:, b, rows, self.cols] if o == 0 else self.w.at[b, :, rows, self.cols]

    def push(self, n, ref, axis, d):
        self.net.send(ref, ref, self.net.along(axis, d), self.sent[n // 2], self.came[n])

    def start(self):
        for o in (0, 1):
            own = self.single(o, (self.net.x, self.net.z)[o], 0)
            self.push(0, own, o, 1)
            self.push(0, own, o, -1)

    def step(self, n):
        net = self.net
        net.wait_came(self.sizes[n - 1], self.came[n - 1])
        for o in (0, 1):
            me, other = (net.x, net.z) if o == 0 else (net.z, net.x)
            if n == 1:
                self.push(1, self.single(o, (me + 3) % 4, 1), o, 1)
                self.push(1, self.single(o, (me + 1) % 4, 2), o, -1)
            elif n == 2:
                own = self.bundle(o, other, 0)
                self.push(2, own, 1 - o, 1)
                self.push(2, own, 1 - o, -1)
            else:
                self.push(3, self.bundle(o, (other + 3) % 4, 1), 1 - o, 1)
                self.push(3, self.bundle(o, (other + 1) % 4, 2), 1 - o, -1)

    def finish(self):
        self.net.wait_came(self.sizes[3], self.came[3])

    def drain(self):
        for ref, sem in zip(self.totals, self.sent):
            self.net.wait_sent(ref, sem)


class Scatter:
    def __init__(self, net, p, rows, bufs, cols=slice(None)):
        self.net, self.p, self.bufs, self.cols = net, p, bufs, cols
        self.h, self.q = rows // 2, rows // 4
        self.sent = [net.sem(), net.sem()]
        self.came = [net.sem() for _ in range(4)]
        whole = pl.ds(0, rows)
        self.totals = [p.at[0:3, :, whole, cols], p.at[0, 0:3, whole, cols]]

    def rows(self, o, part):
        base = o * self.h
        if part == 1:
            return pl.ds(base, self.q)
        if part == 2:
            return pl.ds(base + self.q, self.q)
        return pl.ds(base, self.h)

    def place(self, o):
        return (self.net.x, self.net.z) if o == 0 else (self.net.z, self.net.x)

    def bundle(self, o, a, part):
        r = self.rows(o, part)
        return self.p.at[a, :, r, self.cols] if o == 0 else self.p.at[:, a, r, self.cols]

    def block(self, o, a, i, part):
        r = self.rows(o, part)
        return self.p.at[a, i, r, self.cols] if o == 0 else self.p.at[i, a, r, self.cols]

    def half(self, side):
        return pl.ds(side * self.q, self.q)

    def push(self, n, src, dst, axis, d):
        self.net.send(src, dst, self.net.along(axis, d), self.sent[n // 2], self.came[n])

    def start(self):
        r1, r2 = self.bufs[0], self.bufs[1]
        for o in (0, 1):
            me, _ = self.place(o)
            for side, d in ((0, 1), (1, -1)):
                self.push(0, self.bundle(o, (me + 2) % 4, 1 + side), r1.at[o, side], o, d)
        for o in (0, 1):
            me, _ = self.place(o)
            for side, d in ((0, 1), (1, -1)):
                self.push(1, self.bundle(o, (me + d) % 4, 2 - side), r2.at[o, side, :, self.half(1 - side)], o, d)

    def step2(self):
        r1, r2 = self.bufs[0], self.bufs[1]
        self.net.wait_came(r1, self.came[0])
        for o in (0, 1):
            me, _ = self.place(o)
            for side, d in ((0, 1), (1, -1)):
                a, part = (me + d) % 4, 1 + side

                def add(i, _, o=o, a=a, part=part, side=side):
                    b = self.block(o, a, i, part)
                    b[...] = (b[...].astype(F32) + r1[o, side, i].astype(F32)).astype(BF16)
                    return 0

                lax.fori_loop(0, 4, add, 0)
                self.push(1, self.bundle(o, a, part), r2.at[o, side, :, self.half(side)], o, d)

    def step3(self):
        r2, r3, r4 = self.bufs[1], self.bufs[2], self.bufs[3]
        self.net.wait_came(r2, self.came[1])
        for o in (0, 1):
            me, other = self.place(o)

            def add(i, o=o, me=me):
                b = self.block(o, me, i, 0)
                total = b[...].astype(F32) + r2[o, 0, i].astype(F32) + r2[o, 1, i].astype(F32)
                b[...] = total.astype(BF16)

            def far(n, _, add=add, other=other):
                add((other + 2 + n) % 4)
                return 0

            add((other + 2) % 4)
            for side, d in ((0, 1), (1, -1)):
                self.push(2, self.block(o, me, (other + 2) % 4, 1 + side), r3.at[o, side], 1 - o, d)
            lax.fori_loop(1, 4, far, 0)
            for side, d in ((0, 1), (1, -1)):
                self.push(3, self.block(o, me, (other + d) % 4, 2 - side), r4.at[o, side, self.half(1 - side)], 1 - o, d)

    def step4(self):
        r3, r4 = self.bufs[2], self.bufs[3]
        self.net.wait_came(r3, self.came[2])
        for o in (0, 1):
            me, other = self.place(o)
            for side, d in ((0, 1), (1, -1)):
                b = self.block(o, me, (other + d) % 4, 1 + side)
                b[...] = (b[...].astype(F32) + r3[o, side].astype(F32)).astype(BF16)
                self.push(3, b, r4.at[o, side, self.half(side)], 1 - o, d)

    def finish(self, store):
        r4 = self.bufs[3]
        self.net.wait_came(r4, self.came[3])
        for o in (0, 1):
            me, other = self.place(o)
            total = self.block(o, me, other, 0)[...].astype(F32) + r4[o, 0].astype(F32) + r4[o, 1].astype(F32)
            store(self.rows(o, 0), total)

    def drain(self):
        for ref, sem in zip(self.totals, self.sent):
            self.net.wait_sent(ref, sem)


def scatter_bufs(rows, cols):
    h, q = rows // 2, rows // 4
    return [
        pltpu.VMEM((2, 2, 4, q, cols), BF16),
        pltpu.VMEM((2, 2, 4, h, cols), BF16),
        pltpu.VMEM((2, 2, q, cols), BF16),
        pltpu.VMEM((2, 2, h, cols), BF16),
    ]


class ReduceY:
    def __init__(self, net, part, cr, yr):
        self.net, self.part, self.cr, self.yr = net, part, cr, yr
        self.sent, self.core, self.far = [net.sem(), net.sem()], [net.sem(), net.sem()], [net.sem(), net.sem()]

    def start(self, n):
        net, rows = self.net, half_rows(n)
        net.send(self.part.at[:, 1 - net.c, rows], self.cr.at[:, rows], net.at(dc=1), self.sent[0], self.core[n])

    def step(self, n):
        net, rows = self.net, half_rows(n)
        net.wait_came(self.cr.at[:, rows], self.core[n])
        for d in (2, 1, 3):
            to = (net.y + d) % 4
            own = self.part.at[to, net.c, rows]
            own[...] = (own[...].astype(F32) + self.cr[to, rows].astype(F32)).astype(BF16)
            net.send(own, self.yr.at[d - 1, rows], net.at(dy=d), self.sent[1], self.far[n])

    def finish(self, n):
        net, rows, yr = self.net, half_rows(n), self.yr
        total = self.part[net.y, net.c, rows].astype(F32) + self.cr[net.y, rows].astype(F32)
        net.wait_came(yr.at[:, rows], self.far[n])
        return total + yr[0, rows].astype(F32) + yr[1, rows].astype(F32) + yr[2, rows].astype(F32)

    def drain(self):
        self.net.wait_sent(self.cr, self.sent[0])
        self.net.wait_sent(self.yr, self.sent[1])


class GatherY:
    def __init__(self, net, g):
        self.net, self.g = net, g
        self.sent, self.near, self.far = [net.sem(), net.sem()], net.sem(), [[net.sem() for _ in range(3)] for _ in range(2)]

    def put(self, n, rows):
        net = self.net
        own = self.g.at[net.y, net.c, half_rows(n)]
        own[...] = rows.astype(BF16)
        for d in (2, 1, 3):
            net.send(own, own, net.at(dy=d), self.sent[0], self.far[n][d - 1])
        net.send(own, own, net.at(dc=1), self.sent[1], self.near)

    def step(self, n):
        net = self.net
        for d in (1, 3, 2):
            came = self.g.at[(net.y + 4 - d) % 4, net.c, half_rows(n)]
            net.wait_came(came, self.far[n][d - 1])
            net.send(came, came, net.at(dc=1), self.sent[1], self.near)

    def finish(self):
        self.net.wait_came(self.g.at[:, 1 - self.net.c], self.near)

    def drain(self):
        self.net.wait_sent(self.g.at[0:3, 0], self.sent[0])
        self.net.wait_sent(self.g.at[:, 0], self.sent[1])


def kernel(*refs):
    it = iter(refs)

    def take(n):
        return [next(it) for _ in range(n)]

    x_in, cot_in, seg, gain_a, gain_b, wq_in, wg_in, wk_in, wv_in, wo_in, mg_in, mu_in, md_in = take(13)
    bo_out, ig_out, gain1_out, qg_out, gg_out, kg_out, vg_out, og_out, gain2_out, mg_out, mu_out, md_out = take(12)
    wq, wg, wkv, wo, wm, wd, kv, kvg, pd0, pd1 = take(10)
    xb, xn, xnt, g, hnb, hnt, dcb, igb, bo = take(9)
    part_a, part_b = take(2)
    yb = [take(2) for _ in range(4)]
    r1c, gp, ob, ot, qt, dot_, dqt, dmb, ab, dadu, mt = take(11)
    h32, z32, r32, dh32 = take(4)
    gx0, gxr, gx1, gzr, gy, gc = take(6)
    md_f, og_f, qg_f, gg_f, kg_f, vg_f, gn_f = take(7)
    mg_f, mu_f = ab.at[0:128], ab.at[128:256]
    sb = [take(4) for _ in range(10)]
    sems, local = take(2)

    net = Net(sems)
    s, x, z, y, c = net.s, net.x, net.z, net.y, net.c
    moved = []

    def move(src, dst):
        d = pltpu.make_async_copy(src, dst, local.at[len(moved)])
        d.start()
        moved.append(d)
        return d

    load_kv = [move(wk_in, wkv.at[x, z, pl.ds(0, 128), pl.ds(0, 128)]), move(wv_in, wkv.at[x, z, pl.ds(0, 128), pl.ds(128, 128)])]
    load_q = move(wq_in, wq.at[x, z])
    load_g = move(wg_in, wg.at[x, z])
    load_o = move(wo_in, wo.at[x, z])
    load_x = move(x_in, xb)
    load_d = move(md_in, wd.at[x, z])
    load_m = [move(mg_in, wm.at[x, z, :, pl.ds(0, 768)]), move(mu_in, wm.at[x, z, :, pl.ds(768, 768)])]
    load_c = move(cot_in, g)
    line = lax.broadcasted_iota(jnp.int32, (16, 128), 0)
    tile = jnp.where(line == 0, gain_a[...].astype(F32), jnp.where(line == 1, gain_b[...].astype(F32), 0.0))
    wkv[x, z, 128:144, :] = jnp.concatenate([tile, tile], axis=1).astype(BF16)
    net.barrier()

    ag_kvw = Gather(net, wkv, (32, 64, 112, 144))
    ag_q = Gather(net, wq, (32, 64, 96, 128))
    ag_g = Gather(net, wg, (32, 64, 96, 128))
    ag_o = Gather(net, wo, (64, 128, 192, 256))
    ag_kv = Gather(net, kv, (64, 128, 192, 256))
    ag_d = Gather(net, wd, (192, 384, 576, 768))
    ag_mg = Gather(net, wm, (32, 64, 96, 128), pl.ds(0, 768))
    ag_mu = [Gather(net, wm, (32, 64, 96, 128), pl.ds(768 + 384 * n, 384)) for n in (0, 1)]
    for d in load_kv:
        d.wait()
    ag_kvw.start()
    load_q.wait()
    ag_q.start()
    load_g.wait()
    ag_g.start()
    load_o.wait()
    ag_o.start()
    load_d.wait()
    ag_d.start()

    load_x.wait()

    def scales(i, _):
        rows = pl.ds(pl.multiple_of(i * 32, 32), 32)
        v = xb[rows, :].astype(F32)
        scale = lax.rsqrt(jnp.mean(v * v, axis=-1, keepdims=True) + EPS)
        r1c[rows, :] = jnp.broadcast_to(scale, (32, 128))
        return 0

    lax.fori_loop(0, 8, scales, 0)
    ids = seg[...].astype(F32)

    def below(v):
        return jnp.sum(jnp.where(ids < v, 1.0, 0.0), axis=(0, 1), keepdims=True)

    own_ids = jnp.concatenate([seg[pl.ds(2 * s, 1), :], seg[pl.ds(2 * s + 1, 1), :]], axis=1).astype(F32)
    first_key = jnp.where(own_ids > 2.5, below(2.5), jnp.where(own_ids > 1.5, below(1.5), jnp.where(own_ids > 0.5, below(0.5), 0.0)))
    first_key = jnp.concatenate([first_key, first_key], axis=1).astype(jnp.int32)
    query_place = s * 256 + lax.broadcasted_iota(jnp.int32, (1, 256), 1)
    query_place = jnp.concatenate([query_place, query_place], axis=1)
    top = jnp.max(ids, axis=(0, 1), keepdims=True)
    kept = below(top)

    ag_kvw.step(1)
    ag_q.step(1)
    load_c.wait()

    def mask_cot(i, _):
        rows = pl.ds(pl.multiple_of(i * 32, 32), 32)
        place = (s * 256 + i * 32 + lax.broadcasted_iota(jnp.int32, (32, 1), 0)).astype(F32)
        g[rows, :] = jnp.where(place < kept, g[rows, :].astype(F32), 0.0).astype(BF16)
        return 0

    lax.fori_loop(0, 8, mask_cot, 0)
    pairs = (s + 2) // 2

    def clear(j, _):
        kvg[j // 4, j % 4] = jnp.zeros((256, 256), BF16)
        return 0

    lax.fori_loop(2 * pairs, 16, clear, 0)
    ag_kvw.step(2)
    ag_q.step(2)
    ag_g.step(1)
    ag_o.step(1)
    ag_d.step(1)
    ag_kvw.step(3)
    ag_q.step(3)
    ag_g.step(2)
    ag_kvw.finish()

    def gain_row(n):
        return jnp.concatenate([wkv[j // 4, j % 4, 128:144, 0:128].astype(F32)[n : n + 1, :] for j in range(16)], axis=1)

    gain1 = gain_row(0)
    gain2 = gain_row(1)

    def norm_in(i, _):
        rows = pl.ds(pl.multiple_of(i * 32, 32), 32)
        v = xb[rows, :].astype(F32) * r1c[rows, 0:1]
        xn[rows, :] = (v * gain1).astype(BF16)
        return 0

    lax.fori_loop(0, 8, norm_in, 0)
    kv[x, z] = nn(xn[...], wkv[:, :, 0:128, :].reshape(2048, 256)).astype(BF16)
    ag_kv.start()
    for d in load_m:
        d.wait()
    ag_mg.start()
    ag_q.finish()
    q = nn(xn[...], wq[...].reshape(2048, 256)).astype(BF16)
    qt[...] = jnp.concatenate([q[:, :128].T, q[:, 128:].T], axis=1)
    ag_kv.step(1)
    ag_o.step(2)
    ag_kv.step(2)
    ag_mg.step(1)
    for a in ag_mu:
        a.start()
    for j in range(8):
        xnt[256 * j : 256 * j + 256, :] = xn[:, 256 * j : 256 * j + 256].T
    ag_kv.step(3)
    ag_g.step(3)
    ag_o.step(3)
    for a in ag_mu:
        a.step(1)
    ag_d.step(2)
    ag_mg.step(2)
    ag_kv.finish()

    ot[...] = jnp.zeros_like(ot)
    key_line = lax.broadcasted_iota(jnp.int32, (512, 512), 0)

    def scores(i):
        both = kv[i // 2, pl.ds(2 * (i % 2), 2)].reshape(512, 256)
        keys, values = both[:, 0:128], both[:, 128:256]
        place = i * 512 + key_line
        allowed = (place >= first_key) & (place <= query_place)
        return keys, values, jnp.where(allowed, nn(keys, qt[...]) * (SCALE * LOG2E), MASKED)

    def attend(i, state):
        top, total = state
        _, values, st = scores(i)
        new_top = jnp.maximum(top, jnp.max(st, axis=0, keepdims=True))
        probs = jnp.exp2(st - new_top)
        shrink = jnp.exp2(top - new_top)
        ot[...] = ot[...] * shrink + nn(values.T, probs.astype(BF16))
        return new_top, total * shrink + jnp.sum(probs, axis=0, keepdims=True)

    state = (jnp.full((1, 512), FLOOR, F32), jnp.zeros((1, 512), F32))
    top, total = lax.fori_loop(0, pairs, attend, state)
    lse = top + jnp.log(total) * LOG2E
    ot[...] = ot[...] / total
    o = jnp.concatenate([ot[:, 0:256].T, ot[:, 256:512].T], axis=1)
    ob[...] = o
    ag_g.finish()
    gp[...] = nn(xn[...], wg[...].reshape(2048, 256))
    yv = (o * jax.nn.sigmoid(gp[...])).astype(BF16)
    ag_o.finish()
    red = ReduceY(net, part_a, *yb[0])
    for j in range(8):
        w2 = jnp.concatenate([wo[j // 2, 2 * (j % 2) + i] for i in (0, 1)], axis=1)
        part_a[:, :, :, 256 * j : 256 * j + 256] = nn(yv, w2).astype(BF16).reshape(4, 2, 32, 256)
    for n in (0, 1):
        red.start(n)
    ag_d.step(3)
    for n in (0, 1):
        red.step(n)
    ag_mg.step(3)
    for a in ag_mu:
        a.step(2)
    yt = yv.T
    own_rows = [pl.ds(pl.multiple_of(net.k * ROWS + 16 * n, 16), 16) for n in (0, 1)]
    gat = GatherY(net, hnb)
    for n in (0, 1):
        h = xb[own_rows[n], :].astype(F32) + red.finish(n)
        h32[half_rows(n), :] = h
        scale2 = lax.rsqrt(jnp.mean(h * h, axis=-1, keepdims=True) + EPS)
        z2 = h * scale2
        z32[half_rows(n), :] = z2
        r32[half_rows(n), :] = jnp.broadcast_to(scale2, (16, 128))
        gat.put(n, z2 * gain2)
    ag_d.finish()

    for n in range(3):
        w2 = jnp.concatenate([wd[j // 4, j % 4, 256 * n : 256 * n + 256, :] for j in range(16)], axis=1)
        dmb[:, 256 * n : 256 * n + 256] = nt(g[...], w2)
    for n in (0, 1):
        gat.step(n)
    gat.finish()
    hn = hnb[...].reshape(256, 2048)
    for j in range(8):
        hnt[256 * j : 256 * j + 256, :] = hnb[:, :, :, 256 * j : 256 * j + 256].reshape(256, 256).T
    ag_mu[0].step(3)
    ag_mg.finish()
    for n in range(3):
        ab[:, 256 * n : 256 * n + 256] = nn(hn, wm[:, :, :, 256 * n : 256 * n + 256].reshape(2048, 256))
    ag_mu[1].step(3)
    for a in (ag_kvw, ag_q, ag_g, ag_o, red):
        a.drain()
    pds = (pd0, pd1)
    rs_d = [Scatter(net, pds[n], 384, sb[n]) for n in (0, 1)]

    def down_grad(n):
        for j in range(8):
            pd = nn(mt[384 * n : 384 * n + 384, :], g[:, 256 * j : 256 * j + 256])
            for i in (0, 1):
                pds[n][j // 2, 2 * (j % 2) + i] = pd[:, 128 * i : 128 * i + 128].astype(BF16)
        rs_d[n].start()

    for n in (0, 1):
        cols = slice(384 * n, 384 * n + 384)
        up_cols = slice(768 + 384 * n, 1152 + 384 * n)
        ag_mu[n].finish()
        a = ab[:, cols]
        u = nn(hn, wm[:, :, :, up_cols].reshape(2048, 384))
        sig = jax.nn.sigmoid(a)
        silu = a * sig
        mt[cols, :] = (silu * u).astype(BF16).T
        dm = dmb[:, cols]
        dadu[:, cols] = (dm * u * sig * (1.0 + a * (1.0 - sig))).astype(BF16)
        dadu[:, up_cols] = (dm * silu).astype(BF16)
        if n == 0:
            down_grad(0)
    red3 = ReduceY(net, part_a, *yb[1])
    for j in range(8):
        w2 = wm[j // 2, 2 * (j % 2) : 2 * (j % 2) + 2].reshape(256, 1536)
        part_a[:, :, :, 256 * j : 256 * j + 256] = nt(dadu[...], w2).astype(BF16).reshape(4, 2, 32, 256)
    for n in (0, 1):
        red3.start(n)
    down_grad(1)
    for a in (ag_d, ag_mg, *ag_mu):
        a.drain()
    rs_m = [Scatter(net, wm, 128, sb[2 + n], pl.ds(768 * n, 768)) for n in (0, 1)]
    for n in (0, 1):
        for j in range(8):
            pm = nn(hnt[256 * j : 256 * j + 256, :], dadu[:, 768 * n : 768 * n + 768])
            wm[j // 2, 2 * (j % 2) : 2 * (j % 2) + 2, :, 768 * n : 768 * n + 768] = pm.astype(BF16).reshape(2, 128, 768)
        rs_m[n].start()
        if n == 0:
            red3.step(0)
            red3.step(1)
    mm = mt[...].T
    for j in range(8):
        w2 = jnp.concatenate([wd[j // 2, 2 * (j % 2) + i] for i in (0, 1)], axis=1)
        part_b[:, :, :, 256 * j : 256 * j + 256] = nn(mm, w2).astype(BF16).reshape(4, 2, 32, 256)
    grads_gain2 = jnp.zeros((1, 2048), F32)
    gat3 = GatherY(net, dcb)
    for n in (0, 1):
        dhn = red3.finish(n)
        z2 = z32[half_rows(n), :]
        e2 = dhn * gain2
        grads_gain2 += jnp.sum(dhn * z2, axis=0, keepdims=True)
        dh = g[own_rows[n], :].astype(F32) + r32[half_rows(n), 0:1] * (e2 - z2 * jnp.mean(e2 * z2, axis=-1, keepdims=True))
        dh32[half_rows(n), :] = dh
        gat3.put(n, dh)
    red2 = ReduceY(net, part_b, *yb[2])
    for n in (0, 1):
        red2.start(n)
    rs_d[0].step2()
    for n in (0, 1):
        gat3.step(n)
    for n in (0, 1):
        red2.step(n)
    gat3.finish()
    dc = dcb[...].reshape(256, 2048)
    w2 = jnp.concatenate([wo[j // 4, j % 4] for j in range(16)], axis=1)
    dy = nt(dc, w2)
    sig = jax.nn.sigmoid(gp[...])
    do = (dy * sig).astype(BF16)
    dg = (dy * ob[...] * sig * (1.0 - sig)).astype(BF16)
    dot_[...] = jnp.concatenate([do[:, :128].T, do[:, 128:].T], axis=1)
    q_rows = jnp.concatenate([qt[:, 0:256].T, qt[:, 256:512].T], axis=0)
    do_rows = jnp.concatenate([do[:, :128], do[:, 128:]], axis=0)
    w = jnp.sum(dot_[...].astype(F32) * ot[...], axis=0, keepdims=True)
    dqt[...] = jnp.zeros_like(dqt)
    rs_d[1].step2()

    def attend_back(i, _):
        keys, values, st = scores(i)
        probs = jnp.exp2(st - lse)
        dp = nn(values, dot_[...])
        ds = (probs * (dp - w) * SCALE).astype(BF16)
        dk = nn(ds, q_rows).astype(BF16)
        dv = nn(probs.astype(BF16), do_rows).astype(BF16)
        kvg[i // 2, pl.ds(2 * (i % 2), 2)] = jnp.concatenate([dk, dv], axis=1).reshape(2, 256, 256)
        dqt[...] += nn(keys.T, ds)
        return 0

    lax.fori_loop(0, pairs, attend_back, 0)
    rs_kv = [Scatter(net, kvg, 256, sb[4 + 5 * n], pl.ds(128 * n, 128)) for n in (0, 1)]
    for a in rs_kv:
        a.start()
    for j in range(8):
        po = nn(yt, dcb[:, :, :, 256 * j : 256 * j + 256].reshape(256, 256))
        for i in (0, 1):
            wo[j // 2, 2 * (j % 2) + i] = po[:, 128 * i : 128 * i + 128].astype(BF16)
    for a in rs_kv:
        a.step2()
    rs_m[0].step2()
    dq = jnp.concatenate([dqt[:, 0:256].T, dqt[:, 256:512].T], axis=1).astype(BF16)
    for j in range(8):
        pair = (j // 2, slice(2 * (j % 2), 2 * (j % 2) + 2))
        xnt_j = xnt[256 * j : 256 * j + 256, :]
        xn[:, 256 * j : 256 * j + 256] = (nt(dq, wq[pair].reshape(256, 256)) + nt(dg, wg[pair].reshape(256, 256))).astype(BF16)
        wq[pair] = nn(xnt_j, dq).astype(BF16).reshape(2, 128, 256)
        wg[pair] = nn(xnt_j, dg).astype(BF16).reshape(2, 128, 256)
    rs_g = Scatter(net, wg, 128, sb[6])
    rs_g.start()
    for a in rs_kv:
        a.step3()
    rs_o = Scatter(net, wo, 256, sb[5])
    rs_o.start()
    rs_d[0].step3()
    for a in rs_kv:
        a.step4()
    rs_q = Scatter(net, wq, 128, sb[7])
    rs_q.start()
    rs_m[1].step2()
    rs_d[1].step3()
    gat2 = GatherY(net, bo)
    for n in (0, 1):
        gat2.put(n, h32[half_rows(n), :] + red2.finish(n))
    for a in (ag_kv, red3):
        a.drain()

    for n in (0, 1):

        def store_kv(rows, v, n=n):
            kv[0, 0, rows, 128 * n : 128 * n + 128] = v.astype(BF16)

        rs_kv[n].finish(store_kv)
    dkdv = kv[0, 0]
    red4 = ReduceY(net, part_a, *yb[3])
    for j in range(8):
        w2 = wkv[j // 2, 2 * (j % 2) : 2 * (j % 2) + 2, 0:128, :].reshape(256, 256)
        px = nt(dkdv, w2) + xn[:, 256 * j : 256 * j + 256].astype(F32)
        part_a[:, :, :, 256 * j : 256 * j + 256] = px.astype(BF16).reshape(4, 2, 32, 256)
    for n in (0, 1):
        red4.start(n)
    line8 = lax.broadcasted_iota(jnp.int32, (8, 128), 0)
    for j in range(8):
        cols = slice(256 * j, 256 * j + 256)
        pk = nn(xnt[cols, :], dkdv)
        wkv[j // 2, 2 * (j % 2) : 2 * (j % 2) + 2, 0:128, :] = pk.astype(BF16).reshape(2, 128, 256)
        z1 = xb[:, cols].astype(F32) * r1c[:, 0:1]
        gain1_part = jnp.sum(part_a[:, :, :, cols].reshape(256, 256).astype(F32) * z1, axis=0, keepdims=True)
        for i in (0, 1):
            own = slice(128 * i, 128 * i + 128)
            both = jnp.where(line8 == 1, grads_gain2[:, 256 * j + 128 * i : 256 * j + 128 * i + 128], 0.0)
            gx0[j // 2, 2 * (j % 2) + i] = jnp.where(line8 == 0, gain1_part[:, own], both)
    rs_kvw = Scatter(net, wkv, 128, sb[8])
    rs_kvw.start()
    for n in (0, 1):
        red4.step(n)
    sx, sz, sy, sc = ([net.sem(), net.sem()] for _ in range(4))
    for d in (1, 2, 3):
        net.send(gx0.at[(x + d) % 4], gxr.at[d - 1], net.at(dx=d), *sx)
    rs_m[0].step3()
    rs_o.step2()
    rs_g.step2()
    rs_q.step2()
    rs_kvw.step2()
    rs_m[1].step3()
    for a in rs_d:
        a.step4()
    net.wait_came(gxr, sx[1])
    gx1[...] = gx0[x] + gxr[0] + gxr[1] + gxr[2]
    for d in (1, 2, 3):
        net.send(gx1.at[(z + d) % 4], gzr.at[d - 1], net.at(dz=d), *sz)
    gat4 = GatherY(net, igb)
    for n in (0, 1):
        dxn = red4.finish(n)
        scale1 = r1c[own_rows[n], 0:1]
        z1 = xb[own_rows[n], :].astype(F32) * scale1
        e1 = dxn * gain1
        gat4.put(n, dh32[half_rows(n), :] + scale1 * (e1 - z1 * jnp.mean(e1 * z1, axis=-1, keepdims=True)))
    rs_o.step3()
    rs_g.step3()
    rs_q.step3()
    rs_kvw.step3()
    for a in rs_m:
        a.step4()

    def keep(ref, base=0):
        def store(rows, v):
            ref[pl.ds(rows.start + base, rows.size), :] = v

        return store

    for n in (0, 1):
        gat2.step(n)
    for n in (0, 1):
        rs_d[n].finish(keep(md_f, 384 * n))
    move(md_f, md_out)
    rs_o.step4()
    rs_g.step4()
    rs_q.step4()
    rs_kvw.step4()
    net.wait_came(gzr, sz[1])
    gy[y] = gx1[z] + gzr[0] + gzr[1] + gzr[2]
    for d in (1, 2, 3):
        net.send(gy.at[y], gy.at[y], net.at(dy=d), *sy)
    for n in (0, 1):
        gat4.step(n)
    rs_m[0].finish(keep(mg_f))
    move(mg_f, mg_out)
    rs_m[1].finish(keep(mu_f))
    move(mu_f, mu_out)
    gat2.finish()
    move(bo, bo_out)
    net.wait_came(gy.at[0:3], sy[1])
    gc[c] = gy[0] + gy[1] + gy[2] + gy[3]
    net.send(gc.at[c], gc.at[c], net.at(dc=1), *sc)
    rs_o.finish(keep(og_f))
    move(og_f, og_out)
    rs_g.finish(keep(gg_f))
    move(gg_f, gg_out)
    rs_q.finish(keep(qg_f))
    move(qg_f, qg_out)
    gat4.finish()
    move(igb, ig_out)

    def store_kvw(rows, v):
        kg_f[rows, :] = v[:, :128]
        vg_f[rows, :] = v[:, 128:]

    rs_kvw.finish(store_kvw)
    move(kg_f, kg_out)
    move(vg_f, vg_out)
    net.wait_came(gc.at[0], sc[1])
    gn_f[...] = gc[0] + gc[1]
    move(gn_f.at[pl.ds(0, 1)], gain1_out)
    move(gn_f.at[pl.ds(1, 1)], gain2_out)
    for a in (*rs_m, *rs_d, *rs_kv, rs_g, rs_q, rs_o, rs_kvw, red2, red4, gat, gat2, gat3, gat4):
        a.drain()
    net.wait_sent(gxr, sx[0])
    net.wait_sent(gzr, sz[0])
    net.wait_sent(gy.at[0:3], sy[0])
    net.wait_sent(gc.at[0], sc[0])
    for d in moved[10:]:
        d.wait()


def place_outputs(*refs):
    ins, outs, (narrow, wide, sems) = refs[:12], refs[12:24], refs[24:]
    spans = [pl.ds(64 * i, 64) for i in range(4)]
    loads = [pltpu.make_async_copy(ins[1].at[r], narrow.at[r], sems.at[i]) for i, r in enumerate(spans)]
    copies = [pltpu.make_async_copy(ins[i], outs[i], sems.at[4 + i]) for i in (0, 9, 10, 11, 3, 4, 5, 6, 7, 2, 8)]
    for d in loads + copies:
        d.start()
    for i, r in enumerate(spans):
        loads[i].wait()
        wide[r, :] = narrow[r, :].astype(F32)
        d = pltpu.make_async_copy(wide.at[r], outs[1].at[r], sems.at[16 + i])
        d.start()
        copies.append(d)
    for d in copies:
        d.wait()


def per_device(inputs, cotangent, segment_ids, attn_gain, query_weight, gate_weight, key_weight, value_weight, output_weight, mlp_gain, mlp_gate, mlp_up, mlp_down):
    v = pltpu.VMEM
    y_rows = (4, 2, ROWS, 2048)
    scratch = [
        v((4, 4, 128, 256), BF16),
        v((4, 4, 128, 256), BF16),
        v((4, 4, 144, 256), BF16),
        v((4, 4, 256, 128), BF16),
        v((4, 4, 128, 1536), BF16),
        v((4, 4, 768, 128), BF16),
        v((4, 4, 256, 256), BF16),
        v((4, 4, 256, 256), BF16),
        v((4, 4, 384, 128), BF16),
        v((4, 4, 384, 128), BF16),
        v((256, 2048), BF16),
        v((256, 2048), BF16),
        v((2048, 256), BF16),
        v((256, 2048), BF16),
        v(y_rows, BF16),
        v((2048, 256), BF16),
        v(y_rows, BF16),
        v(y_rows, BF16),
        v(y_rows, BF16),
        v(y_rows, BF16),
        v(y_rows, BF16),
    ]
    for _ in range(4):
        scratch += [v((4, ROWS, 2048), BF16), v((3, ROWS, 2048), BF16)]
    scratch += [
        v((256, 128), F32),
        v((256, 256), F32),
        v((256, 256), F32),
        v((128, 512), F32),
        v((128, 512), BF16),
        v((128, 512), BF16),
        v((128, 512), F32),
        v((256, 768), F32),
        v((256, 768), F32),
        v((256, 1536), BF16),
        v((768, 256), BF16),
        v((ROWS, 2048), F32),
        v((ROWS, 2048), F32),
        v((ROWS, 128), F32),
        v((ROWS, 2048), F32),
        v((4, 4, 8, 128), F32),
        v((3, 4, 8, 128), F32),
        v((4, 8, 128), F32),
        v((3, 8, 128), F32),
        v((4, 8, 128), F32),
        v((2, 8, 128), F32),
    ]
    grad_shapes = ((768, 128), (256, 128), (128, 256), (128, 256), (128, 128), (128, 128), (8, 128))
    scratch += [v(dims, F32) for dims in grad_shapes]
    for rows, cols in ((384, 128), (384, 128), (128, 768), (128, 768), (256, 128), (256, 128), (128, 256), (128, 256), (128, 256), (256, 128)):
        scratch += scatter_bufs(rows, cols)
    scratch += [pltpu.SemaphoreType.DMA((188,)), pltpu.SemaphoreType.DMA((24,))]
    whole = pl.BlockSpec(memory_space=pltpu.VMEM)
    there = pl.BlockSpec(memory_space=pl.ANY)
    shape = jax.ShapeDtypeStruct
    out_shape = (
        shape((256, 2048), BF16),
        shape((256, 2048), F32),
        shape((1, 128), F32),
        shape((128, 256), F32),
        shape((128, 256), F32),
        shape((128, 128), F32),
        shape((128, 128), F32),
        shape((256, 128), F32),
        shape((1, 128), F32),
        shape((128, 768), F32),
        shape((128, 768), F32),
        shape((768, 128), F32),
    )
    outs = pl.pallas_call(
        kernel,
        out_shape=tuple(v(o.shape, o.dtype) for o in (shape(y_rows, BF16), shape(y_rows, BF16)) + out_shape[2:]),
        in_specs=[there, there, whole, whole, whole] + [there] * 8,
        out_specs=[there] * 12,
        scratch_shapes=scratch,
        compiler_params=pltpu.CompilerParams(collective_id=0, has_side_effects=True, vmem_limit_bytes=58 << 20),
    )(
        inputs,
        cotangent,
        segment_ids.reshape(32, 128),
        attn_gain.reshape(1, 128),
        mlp_gain.reshape(1, 128),
        query_weight,
        gate_weight,
        key_weight,
        value_weight,
        output_weight,
        mlp_gate,
        mlp_up,
        mlp_down,
    )
    outs = pl.pallas_call(
        place_outputs,
        out_shape=out_shape,
        in_specs=[there] * 12,
        out_specs=[there] * 12,
        scratch_shapes=[v((256, 2048), BF16), v((256, 2048), F32), pltpu.SemaphoreType.DMA((20,))],
        compiler_params=pltpu.CompilerParams(vmem_limit_bytes=8 << 20),
    )(outs[0].reshape(256, 2048), outs[1].reshape(256, 2048), *outs[2:])
    outs = list(outs)
    outs[2] = outs[2].reshape(128)
    outs[8] = outs[8].reshape(128)
    return tuple(outs)


def solution(mesh):
    weights = (P("seq"), P("seq", "kv"), P("seq", "kv"), P("seq", "kv"), P("seq", "kv"), P("kv", "seq"))
    weights += (P("seq"), P("seq", "kv"), P("seq", "kv"), P("kv", "seq"))
    return jax.shard_map(
        per_device,
        mesh=mesh,
        in_specs=(P("seq", None), P("seq", None), P()) + weights,
        out_specs=(P("seq", None), P("seq", None)) + weights,
        check_vma=False,
    )
```

```python
import functools

import jax
import jax.numpy as jnp
from jax import lax
from jax.experimental import pallas as pl
from jax.experimental.pallas import tpu as pltpu
from jax.sharding import PartitionSpec as P

F32 = jnp.float32
BF16 = jnp.bfloat16
MESH = pl.DeviceIdType.MESH
EPS = 1e-06
HEAD = 128
SCALE = HEAD**-0.5
LOG2E = 1.4426950408889634
MASKED = -1e30
FLOOR = -1e29
ROWS = 32


def nn(left, right):
    return jnp.dot(left, right, preferred_element_type=F32)


def nt(left, right):
    return lax.dot_general(left, right, (((1,), (1,)), ((), ())), preferred_element_type=F32)


def half_rows(n):
    return pl.ds(16 * n, 16)


class Net:
    def __init__(self, sems):
        s, k = lax.axis_index("seq"), lax.axis_index("kv")
        self.s, self.k = s, k
        self.x, self.z, self.y, self.c = s // 4, s % 4, k // 2, k % 2
        self.sems, self.used = sems, 0

    def at(self, dx=0, dz=0, dy=0, dc=0):
        return {
            "kv": ((self.y + dy) % 4) * 2 + (self.c + dc) % 2,
            "seq": ((self.x + dx) % 4) * 4 + (self.z + dz) % 4,
        }

    def along(self, axis, d):
        return self.at(dx=d) if axis == 0 else self.at(dz=d)

    def sem(self):
        self.used += 1
        return self.sems.at[self.used - 1]

    def copy(self, src, dst, to, sent, came):
        return pltpu.make_async_remote_copy(
            src_ref=src,
            dst_ref=dst,
            send_sem=sent,
            recv_sem=came,
            device_id=to,
            device_id_type=MESH,
        )

    def send(self, src, dst, to, sent, came):
        self.copy(src, dst, to, sent, came).start()

    def wait_sent(self, ref, sem):
        self.copy(ref, ref, self.at(dc=1), sem, sem).wait_send()

    def wait_came(self, ref, sem):
        self.copy(ref, ref, self.at(dc=1), sem, sem).wait_recv()

    def barrier(self):
        sem = pltpu.get_barrier_semaphore()
        near = [self.at(dx=d) for d in (1, 2, 3)] + [self.at(dz=d) for d in (1, 2, 3)]
        near += [self.at(dy=d) for d in (1, 2, 3)] + [self.at(dc=1)]
        for to in near:
            pl.semaphore_signal(sem, inc=1, device_id=to, device_id_type=MESH)
        pl.semaphore_wait(sem, len(near))


class Gather:
    def __init__(self, net, w, cuts, cols=slice(None)):
        self.net, self.w, self.cols = net, w, cols
        q, h, q2, r = cuts
        self.spans = ((0, q, h), (h, q2, r))
        self.sent = [net.sem() for _ in range(2)]
        self.came = [net.sem() for _ in range(4)]
        rows = pl.ds(0, r)
        self.sizes = [w.at[0, 0:2, rows, cols], w.at[0, 0, rows, cols], w.at[0:2, :, rows, cols], w.at[0, :, rows, cols]]
        self.totals = [w.at[0, 0:3, rows, cols], w.at[0:3, :, rows, cols]]

    def part(self, o, n):
        r0, r1, r2 = self.spans[o]
        return (pl.ds(r0, r2 - r0), pl.ds(r0, r1 - r0), pl.ds(r1, r2 - r1))[n]

    def single(self, o, a, n):
        x, z = (a, self.net.z) if o == 0 else (self.net.x, a)
        return self.w.at[x, z, self.part(o, n), self.cols]

    def bundle(self, o, b, n):
        rows = self.part(o, n)
        return self.w.at[:, b, rows, self.cols] if o == 0 else self.w.at[b, :, rows, self.cols]

    def push(self, n, ref, axis, d):
        self.net.send(ref, ref, self.net.along(axis, d), self.sent[n // 2], self.came[n])

    def start(self):
        for o in (0, 1):
            own = self.single(o, (self.net.x, self.net.z)[o], 0)
            self.push(0, own, o, 1)
            self.push(0, own, o, -1)

    def step(self, n):
        net = self.net
        net.wait_came(self.sizes[n - 1], self.came[n - 1])
        for o in (0, 1):
            me, other = (net.x, net.z) if o == 0 else (net.z, net.x)
            if n == 1:
                self.push(1, self.single(o, (me + 3) % 4, 1), o, 1)
                self.push(1, self.single(o, (me + 1) % 4, 2), o, -1)
            elif n == 2:
                own = self.bundle(o, other, 0)
                self.push(2, own, 1 - o, 1)
                self.push(2, own, 1 - o, -1)
            else:
                self.push(3, self.bundle(o, (other + 3) % 4, 1), 1 - o, 1)
                self.push(3, self.bundle(o, (other + 1) % 4, 2), 1 - o, -1)

    def finish(self):
        self.net.wait_came(self.sizes[3], self.came[3])

    def drain(self):
        for ref, sem in zip(self.totals, self.sent):
            self.net.wait_sent(ref, sem)


class Scatter:
    def __init__(self, net, p, rows, bufs, cols=slice(None)):
        self.net, self.p, self.bufs, self.cols = net, p, bufs, cols
        self.h, self.q = rows // 2, rows // 4
        self.sent = [net.sem(), net.sem()]
        self.came = [net.sem() for _ in range(4)]
        whole = pl.ds(0, rows)
        self.totals = [p.at[0:3, :, whole, cols], p.at[0, 0:3, whole, cols]]

    def rows(self, o, part):
        base = o * self.h
        if part == 1:
            return pl.ds(base, self.q)
        if part == 2:
            return pl.ds(base + self.q, self.q)
        return pl.ds(base, self.h)

    def place(self, o):
        return (self.net.x, self.net.z) if o == 0 else (self.net.z, self.net.x)

    def bundle(self, o, a, part):
        r = self.rows(o, part)
        return self.p.at[a, :, r, self.cols] if o == 0 else self.p.at[:, a, r, self.cols]

    def block(self, o, a, i, part):
        r = self.rows(o, part)
        return self.p.at[a, i, r, self.cols] if o == 0 else self.p.at[i, a, r, self.cols]

    def half(self, side):
        return pl.ds(side * self.q, self.q)

    def push(self, n, src, dst, axis, d):
        self.net.send(src, dst, self.net.along(axis, d), self.sent[n // 2], self.came[n])

    def start(self):
        r1, r2 = self.bufs[0], self.bufs[1]
        for o in (0, 1):
            me, _ = self.place(o)
            for side, d in ((0, 1), (1, -1)):
                self.push(0, self.bundle(o, (me + 2) % 4, 1 + side), r1.at[o, side], o, d)
        for o in (0, 1):
            me, _ = self.place(o)
            for side, d in ((0, 1), (1, -1)):
                self.push(1, self.bundle(o, (me + d) % 4, 2 - side), r2.at[o, side, :, self.half(1 - side)], o, d)

    def step2(self):
        r1, r2 = self.bufs[0], self.bufs[1]
        self.net.wait_came(r1, self.came[0])
        for o in (0, 1):
            me, _ = self.place(o)
            for side, d in ((0, 1), (1, -1)):
                a, part = (me + d) % 4, 1 + side

                def add(i, _, o=o, a=a, part=part, side=side):
                    b = self.block(o, a, i, part)
                    b[...] = (b[...].astype(F32) + r1[o, side, i].astype(F32)).astype(BF16)
                    return 0

                lax.fori_loop(0, 4, add, 0)
                self.push(1, self.bundle(o, a, part), r2.at[o, side, :, self.half(side)], o, d)

    def step3(self):
        r2, r3, r4 = self.bufs[1], self.bufs[2], self.bufs[3]
        self.net.wait_came(r2, self.came[1])
        for o in (0, 1):
            me, other = self.place(o)

            def add(i, o=o, me=me):
                b = self.block(o, me, i, 0)
                total = b[...].astype(F32) + r2[o, 0, i].astype(F32) + r2[o, 1, i].astype(F32)
                b[...] = total.astype(BF16)

            def far(n, _, add=add, other=other):
                add((other + 2 + n) % 4)
                return 0

            add((other + 2) % 4)
            for side, d in ((0, 1), (1, -1)):
                self.push(2, self.block(o, me, (other + 2) % 4, 1 + side), r3.at[o, side], 1 - o, d)
            lax.fori_loop(1, 4, far, 0)
            for side, d in ((0, 1), (1, -1)):
                self.push(3, self.block(o, me, (other + d) % 4, 2 - side), r4.at[o, side, self.half(1 - side)], 1 - o, d)

    def step4(self):
        r3, r4 = self.bufs[2], self.bufs[3]
        self.net.wait_came(r3, self.came[2])
        for o in (0, 1):
            me, other = self.place(o)
            for side, d in ((0, 1), (1, -1)):
                b = self.block(o, me, (other + d) % 4, 1 + side)
                b[...] = (b[...].astype(F32) + r3[o, side].astype(F32)).astype(BF16)
                self.push(3, b, r4.at[o, side, self.half(side)], 1 - o, d)

    def finish(self, store):
        r4 = self.bufs[3]
        self.net.wait_came(r4, self.came[3])
        for o in (0, 1):
            me, other = self.place(o)
            total = self.block(o, me, other, 0)[...].astype(F32) + r4[o, 0].astype(F32) + r4[o, 1].astype(F32)
            store(self.rows(o, 0), total)

    def drain(self):
        for ref, sem in zip(self.totals, self.sent):
            self.net.wait_sent(ref, sem)


def scatter_bufs(rows, cols):
    h, q = rows // 2, rows // 4
    return [
        pltpu.VMEM((2, 2, 4, q, cols), BF16),
        pltpu.VMEM((2, 2, 4, h, cols), BF16),
        pltpu.VMEM((2, 2, q, cols), BF16),
        pltpu.VMEM((2, 2, h, cols), BF16),
    ]


class ReduceY:
    def __init__(self, net, part, cr, yr):
        self.net, self.part, self.cr, self.yr = net, part, cr, yr
        self.sent, self.core, self.far = [net.sem(), net.sem()], [net.sem(), net.sem()], [net.sem(), net.sem()]

    def start(self, n):
        net, rows = self.net, half_rows(n)
        net.send(self.part.at[:, 1 - net.c, rows], self.cr.at[:, rows], net.at(dc=1), self.sent[0], self.core[n])

    def step(self, n):
        net, rows = self.net, half_rows(n)
        net.wait_came(self.cr.at[:, rows], self.core[n])
        for d in (2, 1, 3):
            to = (net.y + d) % 4
            own = self.part.at[to, net.c, rows]
            own[...] = (own[...].astype(F32) + self.cr[to, rows].astype(F32)).astype(BF16)
            net.send(own, self.yr.at[d - 1, rows], net.at(dy=d), self.sent[1], self.far[n])

    def finish(self, n):
        net, rows, yr = self.net, half_rows(n), self.yr
        total = self.part[net.y, net.c, rows].astype(F32) + self.cr[net.y, rows].astype(F32)
        net.wait_came(yr.at[:, rows], self.far[n])
        return total + yr[0, rows].astype(F32) + yr[1, rows].astype(F32) + yr[2, rows].astype(F32)

    def drain(self):
        self.net.wait_sent(self.cr, self.sent[0])
        self.net.wait_sent(self.yr, self.sent[1])


class GatherY:
    def __init__(self, net, g):
        self.net, self.g = net, g
        self.sent, self.near, self.far = [net.sem(), net.sem()], net.sem(), [[net.sem() for _ in range(3)] for _ in range(2)]

    def put(self, n, rows):
        net = self.net
        own = self.g.at[net.y, net.c, half_rows(n)]
        own[...] = rows.astype(BF16)
        for d in (2, 1, 3):
            net.send(own, own, net.at(dy=d), self.sent[0], self.far[n][d - 1])
        net.send(own, own, net.at(dc=1), self.sent[1], self.near)

    def step(self, n):
        net = self.net
        for d in (1, 3, 2):
            came = self.g.at[(net.y + 4 - d) % 4, net.c, half_rows(n)]
            net.wait_came(came, self.far[n][d - 1])
            net.send(came, came, net.at(dc=1), self.sent[1], self.near)

    def finish(self):
        self.net.wait_came(self.g.at[:, 1 - self.net.c], self.near)

    def drain(self):
        self.net.wait_sent(self.g.at[0:3, 0], self.sent[0])
        self.net.wait_sent(self.g.at[:, 0], self.sent[1])


def kernel(*refs):
    it = iter(refs)

    def take(n):
        return [next(it) for _ in range(n)]

    x_in, cot_in, seg, gain_a, gain_b, wq_in, wg_in, wk_in, wv_in, wo_in, mg_in, mu_in, md_in = take(13)
    bo_out, ig_out, gain1_out, qg_out, gg_out, kg_out, vg_out, og_out, gain2_out, mg_out, mu_out, md_out = take(12)
    wq, wg, wkv, wo, wm, wd, kv, kvg, pd0, pd1 = take(10)
    xb, xn, xnt, g, hnb, hnt, dcb, igb, bo = take(9)
    part_a, part_b = take(2)
    yb = [take(2) for _ in range(4)]
    r1c, gp, ob, ot, qt, dot_, dqt, dmb, ab, dadu, mt = take(11)
    h32, z32, r32, dh32 = take(4)
    gx0, gxr, gx1, gzr, gy, gc = take(6)
    md_f, og_f, qg_f, gg_f, kg_f, vg_f, gn_f = take(7)
    mg_f, mu_f = ab.at[0:128], ab.at[128:256]
    sb = [take(4) for _ in range(10)]
    sems, local = take(2)

    net = Net(sems)
    s, x, z, y, c = net.s, net.x, net.z, net.y, net.c
    moved = []

    def move(src, dst):
        d = pltpu.make_async_copy(src, dst, local.at[len(moved)])
        d.start()
        moved.append(d)
        return d

    load_kv = [move(wk_in, wkv.at[x, z, pl.ds(0, 128), pl.ds(0, 128)]), move(wv_in, wkv.at[x, z, pl.ds(0, 128), pl.ds(128, 128)])]
    load_q = move(wq_in, wq.at[x, z])
    load_g = move(wg_in, wg.at[x, z])
    load_o = move(wo_in, wo.at[x, z])
    load_x = move(x_in, xb)
    load_d = move(md_in, wd.at[x, z])
    load_m = [move(mg_in, wm.at[x, z, :, pl.ds(0, 768)]), move(mu_in, wm.at[x, z, :, pl.ds(768, 768)])]
    load_c = move(cot_in, g)
    line = lax.broadcasted_iota(jnp.int32, (16, 128), 0)
    tile = jnp.where(line == 0, gain_a[...].astype(F32), jnp.where(line == 1, gain_b[...].astype(F32), 0.0))
    wkv[x, z, 128:144, :] = jnp.concatenate([tile, tile], axis=1).astype(BF16)
    net.barrier()

    ag_kvw = Gather(net, wkv, (32, 64, 112, 144))
    ag_q = Gather(net, wq, (32, 64, 96, 128))
    ag_g = Gather(net, wg, (32, 64, 96, 128))
    ag_o = Gather(net, wo, (64, 128, 192, 256))
    ag_kv = Gather(net, kv, (64, 128, 192, 256))
    ag_d = Gather(net, wd, (192, 384, 576, 768))
    ag_mg = Gather(net, wm, (32, 64, 96, 128), pl.ds(0, 768))
    ag_mu = [Gather(net, wm, (32, 64, 96, 128), pl.ds(768 + 384 * n, 384)) for n in (0, 1)]
    for d in load_kv:
        d.wait()
    ag_kvw.start()
    load_q.wait()
    ag_q.start()
    load_g.wait()
    ag_g.start()
    load_o.wait()
    ag_o.start()
    load_d.wait()
    ag_d.start()

    load_x.wait()

    def scales(i, _):
        rows = pl.ds(pl.multiple_of(i * 32, 32), 32)
        v = xb[rows, :].astype(F32)
        scale = lax.rsqrt(jnp.mean(v * v, axis=-1, keepdims=True) + EPS)
        r1c[rows, :] = jnp.broadcast_to(scale, (32, 128))
        return 0

    lax.fori_loop(0, 8, scales, 0)
    ids = seg[...].astype(F32)

    def below(v):
        return jnp.sum(jnp.where(ids < v, 1.0, 0.0), axis=(0, 1), keepdims=True)

    own_ids = jnp.concatenate([seg[pl.ds(2 * s, 1), :], seg[pl.ds(2 * s + 1, 1), :]], axis=1).astype(F32)
    first_key = jnp.where(own_ids > 2.5, below(2.5), jnp.where(own_ids > 1.5, below(1.5), jnp.where(own_ids > 0.5, below(0.5), 0.0)))
    first_key = jnp.concatenate([first_key, first_key], axis=1).astype(jnp.int32)
    query_place = s * 256 + lax.broadcasted_iota(jnp.int32, (1, 256), 1)
    query_place = jnp.concatenate([query_place, query_place], axis=1)
    top = jnp.max(ids, axis=(0, 1), keepdims=True)
    kept = below(top)

    ag_kvw.step(1)
    ag_q.step(1)
    load_c.wait()

    def mask_cot(i, _):
        rows = pl.ds(pl.multiple_of(i * 32, 32), 32)
        place = (s * 256 + i * 32 + lax.broadcasted_iota(jnp.int32, (32, 1), 0)).astype(F32)
        g[rows, :] = jnp.where(place < kept, g[rows, :].astype(F32), 0.0).astype(BF16)
        return 0

    lax.fori_loop(0, 8, mask_cot, 0)
    pairs = (s + 2) // 2

    def clear(j, _):
        kvg[j // 4, j % 4] = jnp.zeros((256, 256), BF16)
        return 0

    lax.fori_loop(2 * pairs, 16, clear, 0)
    ag_kvw.step(2)
    ag_q.step(2)
    ag_g.step(1)
    ag_o.step(1)
    ag_d.step(1)
    ag_kvw.step(3)
    ag_q.step(3)
    ag_g.step(2)
    ag_kvw.finish()

    def gain_row(n):
        return jnp.concatenate([wkv[j // 4, j % 4, 128:144, 0:128].astype(F32)[n : n + 1, :] for j in range(16)], axis=1)

    gain1 = gain_row(0)
    gain2 = gain_row(1)

    def norm_in(i, _):
        rows = pl.ds(pl.multiple_of(i * 32, 32), 32)
        v = xb[rows, :].astype(F32) * r1c[rows, 0:1]
        xn[rows, :] = (v * gain1).astype(BF16)
        return 0

    lax.fori_loop(0, 8, norm_in, 0)
    kv[x, z] = nn(xn[...], wkv[:, :, 0:128, :].reshape(2048, 256)).astype(BF16)
    ag_kv.start()
    for d in load_m:
        d.wait()
    ag_mg.start()
    ag_q.finish()
    q = nn(xn[...], wq[...].reshape(2048, 256)).astype(BF16)
    qt[...] = jnp.concatenate([q[:, :128].T, q[:, 128:].T], axis=1)
    ag_kv.step(1)
    ag_o.step(2)
    ag_kv.step(2)
    ag_mg.step(1)
    for a in ag_mu:
        a.start()
    for j in range(8):
        xnt[256 * j : 256 * j + 256, :] = xn[:, 256 * j : 256 * j + 256].T
    ag_kv.step(3)
    ag_g.step(3)
    ag_o.step(3)
    for a in ag_mu:
        a.step(1)
    ag_d.step(2)
    ag_mg.step(2)
    ag_kv.finish()

    ot[...] = jnp.zeros_like(ot)
    key_line = lax.broadcasted_iota(jnp.int32, (512, 512), 0)

    def scores(i):
        both = kv[i // 2, pl.ds(2 * (i % 2), 2)].reshape(512, 256)
        keys, values = both[:, 0:128], both[:, 128:256]
        place = i * 512 + key_line
        allowed = (place >= first_key) & (place <= query_place)
        return keys, values, jnp.where(allowed, nn(keys, qt[...]) * (SCALE * LOG2E), MASKED)

    def attend(i, state):
        top, total = state
        _, values, st = scores(i)
        new_top = jnp.maximum(top, jnp.max(st, axis=0, keepdims=True))
        probs = jnp.exp2(st - new_top)
        shrink = jnp.exp2(top - new_top)
        ot[...] = ot[...] * shrink + nn(values.T, probs.astype(BF16))
        return new_top, total * shrink + jnp.sum(probs, axis=0, keepdims=True)

    state = (jnp.full((1, 512), FLOOR, F32), jnp.zeros((1, 512), F32))
    top, total = lax.fori_loop(0, pairs, attend, state)
    lse = top + jnp.log(total) * LOG2E
    ot[...] = ot[...] / total
    o = jnp.concatenate([ot[:, 0:256].T, ot[:, 256:512].T], axis=1)
    ob[...] = o
    ag_g.finish()
    gp[...] = nn(xn[...], wg[...].reshape(2048, 256))
    yv = (o * jax.nn.sigmoid(gp[...])).astype(BF16)
    ag_o.finish()
    red = ReduceY(net, part_a, *yb[0])
    for j in range(8):
        w2 = jnp.concatenate([wo[j // 2, 2 * (j % 2) + i] for i in (0, 1)], axis=1)
        part_a[:, :, :, 256 * j : 256 * j + 256] = nn(yv, w2).astype(BF16).reshape(4, 2, 32, 256)
    for n in (0, 1):
        red.start(n)
    ag_d.step(3)
    for n in (0, 1):
        red.step(n)
    ag_mg.step(3)
    for a in ag_mu:
        a.step(2)
    yt = yv.T
    own_rows = [pl.ds(pl.multiple_of(net.k * ROWS + 16 * n, 16), 16) for n in (0, 1)]
    gat = GatherY(net, hnb)
    for n in (0, 1):
        h = xb[own_rows[n], :].astype(F32) + red.finish(n)
        h32[half_rows(n), :] = h
        scale2 = lax.rsqrt(jnp.mean(h * h, axis=-1, keepdims=True) + EPS)
        z2 = h * scale2
        z32[half_rows(n), :] = z2
        r32[half_rows(n), :] = jnp.broadcast_to(scale2, (16, 128))
        gat.put(n, z2 * gain2)
    ag_d.finish()

    for n in range(3):
        w2 = jnp.concatenate([wd[j // 4, j % 4, 256 * n : 256 * n + 256, :] for j in range(16)], axis=1)
        dmb[:, 256 * n : 256 * n + 256] = nt(g[...], w2)
    for n in (0, 1):
        gat.step(n)
    gat.finish()
    hn = hnb[...].reshape(256, 2048)
    for j in range(8):
        hnt[256 * j : 256 * j + 256, :] = hnb[:, :, :, 256 * j : 256 * j + 256].reshape(256, 256).T
    ag_mu[0].step(3)
    ag_mg.finish()
    for n in range(3):
        ab[:, 256 * n : 256 * n + 256] = nn(hn, wm[:, :, :, 256 * n : 256 * n + 256].reshape(2048, 256))
    ag_mu[1].step(3)
    for a in (ag_kvw, ag_q, ag_g, ag_o, red):
        a.drain()
    pds = (pd0, pd1)
    rs_d = [Scatter(net, pds[n], 384, sb[n]) for n in (0, 1)]

    def down_grad(n):
        for j in range(8):
            pd = nn(mt[384 * n : 384 * n + 384, :], g[:, 256 * j : 256 * j + 256])
            for i in (0, 1):
                pds[n][j // 2, 2 * (j % 2) + i] = pd[:, 128 * i : 128 * i + 128].astype(BF16)
        rs_d[n].start()

    for n in (0, 1):
        cols = slice(384 * n, 384 * n + 384)
        up_cols = slice(768 + 384 * n, 1152 + 384 * n)
        ag_mu[n].finish()
        a = ab[:, cols]
        u = nn(hn, wm[:, :, :, up_cols].reshape(2048, 384))
        sig = jax.nn.sigmoid(a)
        silu = a * sig
        mt[cols, :] = (silu * u).astype(BF16).T
        dm = dmb[:, cols]
        dadu[:, cols] = (dm * u * sig * (1.0 + a * (1.0 - sig))).astype(BF16)
        dadu[:, up_cols] = (dm * silu).astype(BF16)
        if n == 0:
            down_grad(0)
    red3 = ReduceY(net, part_a, *yb[1])
    for j in range(8):
        w2 = wm[j // 2, 2 * (j % 2) : 2 * (j % 2) + 2].reshape(256, 1536)
        part_a[:, :, :, 256 * j : 256 * j + 256] = nt(dadu[...], w2).astype(BF16).reshape(4, 2, 32, 256)
    for n in (0, 1):
        red3.start(n)
    down_grad(1)
    for a in (ag_d, ag_mg, *ag_mu):
        a.drain()
    rs_m = [Scatter(net, wm, 128, sb[2 + n], pl.ds(768 * n, 768)) for n in (0, 1)]
    for n in (0, 1):
        for j in range(8):
            pm = nn(hnt[256 * j : 256 * j + 256, :], dadu[:, 768 * n : 768 * n + 768])
            wm[j // 2, 2 * (j % 2) : 2 * (j % 2) + 2, :, 768 * n : 768 * n + 768] = pm.astype(BF16).reshape(2, 128, 768)
        rs_m[n].start()
        if n == 0:
            red3.step(0)
            red3.step(1)
    mm = mt[...].T
    for j in range(8):
        w2 = jnp.concatenate([wd[j // 2, 2 * (j % 2) + i] for i in (0, 1)], axis=1)
        part_b[:, :, :, 256 * j : 256 * j + 256] = nn(mm, w2).astype(BF16).reshape(4, 2, 32, 256)
    grads_gain2 = jnp.zeros((1, 2048), F32)
    gat3 = GatherY(net, dcb)
    for n in (0, 1):
        dhn = red3.finish(n)
        z2 = z32[half_rows(n), :]
        e2 = dhn * gain2
        grads_gain2 += jnp.sum(dhn * z2, axis=0, keepdims=True)
        dh = g[own_rows[n], :].astype(F32) + r32[half_rows(n), 0:1] * (e2 - z2 * jnp.mean(e2 * z2, axis=-1, keepdims=True))
        dh32[half_rows(n), :] = dh
        gat3.put(n, dh)
    red2 = ReduceY(net, part_b, *yb[2])
    for n in (0, 1):
        red2.start(n)
    rs_d[0].step2()
    for n in (0, 1):
        gat3.step(n)
    for n in (0, 1):
        red2.step(n)
    gat3.finish()
    dc = dcb[...].reshape(256, 2048)
    w2 = jnp.concatenate([wo[j // 4, j % 4] for j in range(16)], axis=1)
    dy = nt(dc, w2)
    sig = jax.nn.sigmoid(gp[...])
    do = (dy * sig).astype(BF16)
    dg = (dy * ob[...] * sig * (1.0 - sig)).astype(BF16)
    dot_[...] = jnp.concatenate([do[:, :128].T, do[:, 128:].T], axis=1)
    q_rows = jnp.concatenate([qt[:, 0:256].T, qt[:, 256:512].T], axis=0)
    do_rows = jnp.concatenate([do[:, :128], do[:, 128:]], axis=0)
    w = jnp.sum(dot_[...].astype(F32) * ot[...], axis=0, keepdims=True)
    dqt[...] = jnp.zeros_like(dqt)
    rs_d[1].step2()

    def attend_back(i, _):
        keys, values, st = scores(i)
        probs = jnp.exp2(st - lse)
        dp = nn(values, dot_[...])
        ds = (probs * (dp - w) * SCALE).astype(BF16)
        dk = nn(ds, q_rows).astype(BF16)
        dv = nn(probs.astype(BF16), do_rows).astype(BF16)
        kvg[i // 2, pl.ds(2 * (i % 2), 2)] = jnp.concatenate([dk, dv], axis=1).reshape(2, 256, 256)
        dqt[...] += nn(keys.T, ds)
        return 0

    lax.fori_loop(0, pairs, attend_back, 0)
    rs_kv = [Scatter(net, kvg, 256, sb[4 + 5 * n], pl.ds(128 * n, 128)) for n in (0, 1)]
    for a in rs_kv:
        a.start()
    for j in range(8):
        po = nn(yt, dcb[:, :, :, 256 * j : 256 * j + 256].reshape(256, 256))
        for i in (0, 1):
            wo[j // 2, 2 * (j % 2) + i] = po[:, 128 * i : 128 * i + 128].astype(BF16)
    for a in rs_kv:
        a.step2()
    rs_m[0].step2()
    dq = jnp.concatenate([dqt[:, 0:256].T, dqt[:, 256:512].T], axis=1).astype(BF16)
    for j in range(8):
        pair = (j // 2, slice(2 * (j % 2), 2 * (j % 2) + 2))
        xnt_j = xnt[256 * j : 256 * j + 256, :]
        xn[:, 256 * j : 256 * j + 256] = (nt(dq, wq[pair].reshape(256, 256)) + nt(dg, wg[pair].reshape(256, 256))).astype(BF16)
        wq[pair] = nn(xnt_j, dq).astype(BF16).reshape(2, 128, 256)
        wg[pair] = nn(xnt_j, dg).astype(BF16).reshape(2, 128, 256)
    rs_g = Scatter(net, wg, 128, sb[6])
    rs_g.start()
    for a in rs_kv:
        a.step3()
    rs_o = Scatter(net, wo, 256, sb[5])
    rs_o.start()
    rs_d[0].step3()
    for a in rs_kv:
        a.step4()
    rs_q = Scatter(net, wq, 128, sb[7])
    rs_q.start()
    rs_m[1].step2()
    rs_d[1].step3()
    gat2 = GatherY(net, bo)
    for n in (0, 1):
        gat2.put(n, h32[half_rows(n), :] + red2.finish(n))
    for a in (ag_kv, red3):
        a.drain()

    for n in (0, 1):

        def store_kv(rows, v, n=n):
            kv[0, 0, rows, 128 * n : 128 * n + 128] = v.astype(BF16)

        rs_kv[n].finish(store_kv)
    dkdv = kv[0, 0]
    red4 = ReduceY(net, part_a, *yb[3])
    for j in range(8):
        w2 = wkv[j // 2, 2 * (j % 2) : 2 * (j % 2) + 2, 0:128, :].reshape(256, 256)
        px = nt(dkdv, w2) + xn[:, 256 * j : 256 * j + 256].astype(F32)
        part_a[:, :, :, 256 * j : 256 * j + 256] = px.astype(BF16).reshape(4, 2, 32, 256)
    for n in (0, 1):
        red4.start(n)
    line8 = lax.broadcasted_iota(jnp.int32, (8, 128), 0)
    for j in range(8):
        cols = slice(256 * j, 256 * j + 256)
        pk = nn(xnt[cols, :], dkdv)
        wkv[j // 2, 2 * (j % 2) : 2 * (j % 2) + 2, 0:128, :] = pk.astype(BF16).reshape(2, 128, 256)
        z1 = xb[:, cols].astype(F32) * r1c[:, 0:1]
        gain1_part = jnp.sum(part_a[:, :, :, cols].reshape(256, 256).astype(F32) * z1, axis=0, keepdims=True)
        for i in (0, 1):
            own = slice(128 * i, 128 * i + 128)
            both = jnp.where(line8 == 1, grads_gain2[:, 256 * j + 128 * i : 256 * j + 128 * i + 128], 0.0)
            gx0[j // 2, 2 * (j % 2) + i] = jnp.where(line8 == 0, gain1_part[:, own], both)
    rs_kvw = Scatter(net, wkv, 128, sb[8])
    rs_kvw.start()
    for n in (0, 1):
        red4.step(n)
    sx, sz, sy, sc = ([net.sem(), net.sem()] for _ in range(4))
    for d in (1, 2, 3):
        net.send(gx0.at[(x + d) % 4], gxr.at[d - 1], net.at(dx=d), *sx)
    rs_m[0].step3()
    rs_o.step2()
    rs_g.step2()
    rs_q.step2()
    rs_kvw.step2()
    rs_m[1].step3()
    for a in rs_d:
        a.step4()
    net.wait_came(gxr, sx[1])
    gx1[...] = gx0[x] + gxr[0] + gxr[1] + gxr[2]
    for d in (1, 2, 3):
        net.send(gx1.at[(z + d) % 4], gzr.at[d - 1], net.at(dz=d), *sz)
    gat4 = GatherY(net, igb)
    for n in (0, 1):
        dxn = red4.finish(n)
        scale1 = r1c[own_rows[n], 0:1]
        z1 = xb[own_rows[n], :].astype(F32) * scale1
        e1 = dxn * gain1
        gat4.put(n, dh32[half_rows(n), :] + scale1 * (e1 - z1 * jnp.mean(e1 * z1, axis=-1, keepdims=True)))
    rs_o.step3()
    rs_g.step3()
    rs_q.step3()
    rs_kvw.step3()
    for a in rs_m:
        a.step4()

    def keep(ref, base=0):
        def store(rows, v):
            ref[pl.ds(rows.start + base, rows.size), :] = v

        return store

    for n in (0, 1):
        gat2.step(n)
    for n in (0, 1):
        rs_d[n].finish(keep(md_f, 384 * n))
    move(md_f, md_out)
    rs_o.step4()
    rs_g.step4()
    rs_q.step4()
    rs_kvw.step4()
    net.wait_came(gzr, sz[1])
    gy[y] = gx1[z] + gzr[0] + gzr[1] + gzr[2]
    for d in (1, 2, 3):
        net.send(gy.at[y], gy.at[y], net.at(dy=d), *sy)
    for n in (0, 1):
        gat4.step(n)
    rs_m[0].finish(keep(mg_f))
    move(mg_f, mg_out)
    rs_m[1].finish(keep(mu_f))
    move(mu_f, mu_out)
    gat2.finish()
    move(bo, bo_out)
    net.wait_came(gy.at[0:3], sy[1])
    gc[c] = gy[0] + gy[1] + gy[2] + gy[3]
    net.send(gc.at[c], gc.at[c], net.at(dc=1), *sc)
    rs_o.finish(keep(og_f))
    move(og_f, og_out)
    rs_g.finish(keep(gg_f))
    move(gg_f, gg_out)
    rs_q.finish(keep(qg_f))
    move(qg_f, qg_out)
    gat4.finish()
    move(igb, ig_out)

    def store_kvw(rows, v):
        kg_f[rows, :] = v[:, :128]
        vg_f[rows, :] = v[:, 128:]

    rs_kvw.finish(store_kvw)
    move(kg_f, kg_out)
    move(vg_f, vg_out)
    net.wait_came(gc.at[0], sc[1])
    gn_f[...] = gc[0] + gc[1]
    move(gn_f.at[pl.ds(0, 1)], gain1_out)
    move(gn_f.at[pl.ds(1, 1)], gain2_out)
    for a in (*rs_m, *rs_d, *rs_kv, rs_g, rs_q, rs_o, rs_kvw, red2, red4, gat, gat2, gat3, gat4):
        a.drain()
    net.wait_sent(gxr, sx[0])
    net.wait_sent(gzr, sz[0])
    net.wait_sent(gy.at[0:3], sy[0])
    net.wait_sent(gc.at[0], sc[0])
    for d in moved[10:]:
        d.wait()


def place_outputs(*refs):
    ins, outs, (wide, sems) = refs[:12], refs[12:24], refs[24:]
    copies = [pltpu.make_async_copy(ins[i], outs[i], sems.at[i]) for i in (0, 9, 10, 11, 3, 4, 5, 6, 7, 2, 8)]
    for d in copies:
        d.start()
    for i in range(4):
        r = pl.ds(64 * i, 64)
        wide[r, :] = ins[1][r, :].astype(F32)
        d = pltpu.make_async_copy(wide.at[r], outs[1].at[r], sems.at[12 + i])
        d.start()
        copies.append(d)
    for d in copies:
        d.wait()


def per_device(inputs, cotangent, segment_ids, attn_gain, query_weight, gate_weight, key_weight, value_weight, output_weight, mlp_gain, mlp_gate, mlp_up, mlp_down):
    v = pltpu.VMEM
    y_rows = (4, 2, ROWS, 2048)
    scratch = [
        v((4, 4, 128, 256), BF16),
        v((4, 4, 128, 256), BF16),
        v((4, 4, 144, 256), BF16),
        v((4, 4, 256, 128), BF16),
        v((4, 4, 128, 1536), BF16),
        v((4, 4, 768, 128), BF16),
        v((4, 4, 256, 256), BF16),
        v((4, 4, 256, 256), BF16),
        v((4, 4, 384, 128), BF16),
        v((4, 4, 384, 128), BF16),
        v((256, 2048), BF16),
        v((256, 2048), BF16),
        v((2048, 256), BF16),
        v((256, 2048), BF16),
        v(y_rows, BF16),
        v((2048, 256), BF16),
        v(y_rows, BF16),
        v(y_rows, BF16),
        v(y_rows, BF16),
        v(y_rows, BF16),
        v(y_rows, BF16),
    ]
    for _ in range(4):
        scratch += [v((4, ROWS, 2048), BF16), v((3, ROWS, 2048), BF16)]
    scratch += [
        v((256, 128), F32),
        v((256, 256), F32),
        v((256, 256), F32),
        v((128, 512), F32),
        v((128, 512), BF16),
        v((128, 512), BF16),
        v((128, 512), F32),
        v((256, 768), F32),
        v((256, 768), F32),
        v((256, 1536), BF16),
        v((768, 256), BF16),
        v((ROWS, 2048), F32),
        v((ROWS, 2048), F32),
        v((ROWS, 128), F32),
        v((ROWS, 2048), F32),
        v((4, 4, 8, 128), F32),
        v((3, 4, 8, 128), F32),
        v((4, 8, 128), F32),
        v((3, 8, 128), F32),
        v((4, 8, 128), F32),
        v((2, 8, 128), F32),
    ]
    grad_shapes = ((768, 128), (256, 128), (128, 256), (128, 256), (128, 128), (128, 128), (8, 128))
    scratch += [v(dims, F32) for dims in grad_shapes]
    for rows, cols in ((384, 128), (384, 128), (128, 768), (128, 768), (256, 128), (256, 128), (128, 256), (128, 256), (128, 256), (256, 128)):
        scratch += scatter_bufs(rows, cols)
    scratch += [pltpu.SemaphoreType.DMA((188,)), pltpu.SemaphoreType.DMA((24,))]
    whole = pl.BlockSpec(memory_space=pltpu.VMEM)
    there = pl.BlockSpec(memory_space=pl.ANY)
    shape = jax.ShapeDtypeStruct
    out_shape = (
        shape((256, 2048), BF16),
        shape((256, 2048), F32),
        shape((1, 128), F32),
        shape((128, 256), F32),
        shape((128, 256), F32),
        shape((128, 128), F32),
        shape((128, 128), F32),
        shape((256, 128), F32),
        shape((1, 128), F32),
        shape((128, 768), F32),
        shape((128, 768), F32),
        shape((768, 128), F32),
    )
    outs = pl.pallas_call(
        kernel,
        out_shape=tuple(v(o.shape, o.dtype) for o in (shape(y_rows, BF16), shape(y_rows, BF16)) + out_shape[2:]),
        in_specs=[there, there, whole, whole, whole] + [there] * 8,
        out_specs=[there] * 12,
        scratch_shapes=scratch,
        compiler_params=pltpu.CompilerParams(collective_id=0, has_side_effects=True, vmem_limit_bytes=58 << 20),
    )(
        inputs,
        cotangent,
        segment_ids.reshape(32, 128),
        attn_gain.reshape(1, 128),
        mlp_gain.reshape(1, 128),
        query_weight,
        gate_weight,
        key_weight,
        value_weight,
        output_weight,
        mlp_gate,
        mlp_up,
        mlp_down,
    )
    outs = pl.pallas_call(
        place_outputs,
        out_shape=out_shape,
        in_specs=[there, whole] + [there] * 10,
        out_specs=[there] * 12,
        scratch_shapes=[v((256, 2048), F32), pltpu.SemaphoreType.DMA((16,))],
        compiler_params=pltpu.CompilerParams(vmem_limit_bytes=8 << 20),
    )(outs[0].reshape(256, 2048), outs[1].reshape(256, 2048), *outs[2:])
    outs = list(outs)
    outs[2] = outs[2].reshape(128)
    outs[8] = outs[8].reshape(128)
    return tuple(outs)


def solution(mesh):
    weights = (P("seq"), P("seq", "kv"), P("seq", "kv"), P("seq", "kv"), P("seq", "kv"), P("kv", "seq"))
    weights += (P("seq"), P("seq", "kv"), P("seq", "kv"), P("kv", "seq"))
    return jax.shard_map(
        per_device,
        mesh=mesh,
        in_specs=(P("seq", None), P("seq", None), P()) + weights,
        out_specs=(P("seq", None), P("seq", None)) + weights,
        check_vma=False,
    )
```
